128 devices in a mesh: dp: 32 (over x, y, z_lo), tensor: 4 (over z_hi, core).
Axes of the slice: x: 4, y: 4, z: 4 (z_hi: 2, z_lo: 2; z = z_hi * 2 + z_lo), core: 2. Of those that a mesh axis runs over, the one named last changes fastest.
Arguments:
- hidden: bfloat16 [32768, 1536], P(('dp', 'tensor')), may hold values from -6 to 6
- in_gain: float32 [1536], replicated, may hold values from 0.5 to 1.5
- proj_main: bfloat16 [1536, 2, 3072], P('dp', None, 'tensor'), may hold values from -0.15625 to 0.15625
- proj_step: bfloat16 [1536, 48], P('dp', 'tensor'), may hold values from -0.15625 to 0.15625
- proj_state: bfloat16 [1536, 256], P('dp'), may hold values from -0.15625 to 0.15625
- conv_inner: float32 [4, 3072], P(None, 'tensor'), may hold values from -3 to 3
- conv_inner_bias: float32 [3072], P('tensor'), may hold values from -0.5 to 0.5
- conv_state: float32 [4, 256], replicated, may hold values from -3 to 3
- conv_state_bias: float32 [256], replicated, may hold values from -0.5 to 0.5
- step_bias: float32 [48], P('tensor'), may hold values from -3 to -1
- decay_log: float32 [48], P('tensor'), may hold values from -4 to 1
- skip_gain: float32 [48], P('tensor'), may hold values from 0.5 to 1.5
- out_gain: float32 [3072], P('tensor'), may hold values from 0.5 to 1.5
- proj_out: bfloat16 [1536, 3072], P('dp', 'tensor'), may hold values from -0.109375 to 0.109375
- grad_out: bfloat16 [32768, 1536], P(('dp', 'tensor')), may hold values from -6 to 6
Outputs:
- new_hidden: bfloat16 [32768, 1536], P(('dp', 'tensor'))
- grad_hidden: bfloat16 [32768, 1536], P(('dp', 'tensor'))
- grad_in_gain: float32 [1536], replicated
- grad_proj_main: float32 [1536, 2, 3072], P('dp', None, 'tensor')
- grad_proj_step: float32 [1536, 48], P('dp', 'tensor')
- grad_proj_state: float32 [1536, 256], P('dp')
- grad_conv_inner: float32 [4, 3072], P(None, 'tensor')
- grad_conv_inner_bias: float32 [3072], P('tensor')
- grad_conv_state: float32 [4, 256], replicated
- grad_conv_state_bias: float32 [256], replicated
- grad_step_bias: float32 [48], P('tensor')
- grad_decay_log: float32 [48], P('tensor')
- grad_skip_gain: float32 [48], P('tensor')
- grad_out_gain: float32 [3072], P('tensor')
- grad_proj_out: float32 [1536, 3072], P('dp', 'tensor')
The draws below stay inside these ranges and needn't reach their ends.
All inputs are finite; a program needn't handle non-finite values.
Results may differ from the reference program's by a relative error of at most 0.03.
Values may be sent and summed in bfloat16 or wider, within the bound.
A program may use at most 192 MiB of HBM per device.

```python
import math
import jax
import jax.numpy as jnp
from jax import lax

D = 1536
HEADS = 48
STATE = 128
CONV = 4
SPAN = 256
LEN = 512
INNER = 3072
TOKENS = 32768


def block_levels(rng, shape, split, low, largest):
    factor_of, own = 1.0, jax.random.fold_in(rng, 6)
    for position, blocks in split:
        steps = jnp.exp(jax.random.uniform(jax.random.fold_in(own, position), (blocks,), jnp.float32, low / len(split), largest / len(split)))
        factor_of = factor_of * jnp.repeat(steps, shape[position] // blocks).reshape([-1 if axis == position else 1 for axis in range(len(shape))])
    return factor_of


def noise(key, dims, scale, reach, cuts=(), held_as=jnp.bfloat16):
    array = jax.random.normal(key, dims, jnp.float32) * scale
    if len(cuts) > 0:
        array = block_levels(key, dims, cuts, -0.22, 0.18) * array
    return jnp.clip(array, min=-reach, max=reach).astype(held_as)


def setup_inputs(seed: int = 0) -> dict:
    key_list = jax.random.split(jax.random.key(seed), 16)
    hidden = noise(key_list[0], (TOKENS, D), 1.0, 6.0, ((0, 128),))
    in_gain = jnp.clip(1.0 + 0.1 * jax.random.normal(key_list[1], (D,), jnp.float32), 0.5, 1.5)
    proj_main = noise(key_list[2], (D, 2, INNER), D ** -0.5, 0.15625, ((0, 32), (2, 4)))
    proj_step = noise(key_list[3], (D, HEADS), D ** -0.5, 0.15625, ((0, 32), (1, 4)))
    proj_state = noise(key_list[4], (D, 2 * STATE), D ** -0.5, 0.15625, ((0, 32),))
    conv_inner = noise(key_list[5], (CONV, INNER), CONV ** -0.5, 3.0, ((1, 4),), jnp.float32)
    conv_inner_bias = jnp.clip(jax.random.uniform(key_list[6], (INNER,), jnp.float32, -0.5, 0.5) * block_levels(key_list[6], (INNER,), ((0, 4),), -0.4, 0.0), -0.5, 0.5)
    conv_state = noise(key_list[7], (CONV, 2 * STATE), CONV ** -0.5, 3.0, (), jnp.float32)
    conv_state_bias = jnp.clip(jax.random.uniform(key_list[8], (2 * STATE,), jnp.float32, -0.5, 0.5), -0.5, 0.5)
    step_bias = jnp.clip(-3.0 + 2.0 * jax.random.uniform(key_list[9], (HEADS,), jnp.float32) ** block_levels(key_list[9], (HEADS,), ((0, 4),), -0.2, 0.2), -3.0, -1.0)
    decay_log = jnp.clip(-4.0 + 5.0 * jax.random.uniform(key_list[10], (HEADS,), jnp.float32) ** block_levels(key_list[10], (HEADS,), ((0, 4),), -0.2, 0.2), -4.0, 1.0)
    skip_gain = jnp.clip(0.5 + 1.0 * jax.random.uniform(key_list[11], (HEADS,), jnp.float32) ** block_levels(key_list[11], (HEADS,), ((0, 4),), -0.2, 0.2), 0.5, 1.5)
    out_gain = jnp.clip(1.0 + 0.1 * jax.random.normal(key_list[12], (INNER,), jnp.float32), 0.5, 1.5)
    proj_out = noise(key_list[13], (D, INNER), INNER ** -0.5, 0.109375, ((0, 32), (1, 4)))
    grad_out = noise(key_list[14], (TOKENS, D), 1.0, 6.0, ((0, 128),))
    return dict(hidden=hidden, in_gain=in_gain, proj_main=proj_main, proj_step=proj_step, proj_state=proj_state, conv_inner=conv_inner, conv_inner_bias=conv_inner_bias, conv_state=conv_state, conv_state_bias=conv_state_bias, step_bias=step_bias, decay_log=decay_log, skip_gain=skip_gain, out_gain=out_gain, proj_out=proj_out, grad_out=grad_out)


EPS = 1e-05
HIGH = lax.Precision.HIGHEST

@jax.custom_vjp
def low(v):
    return lax.optimization_barrier(v.astype(jnp.bfloat16)).astype(jnp.float32)

@jax.custom_vjp
def low_back(v):
    return v

def low_keep(v):
    return (low(v), None)

def low_pass(kept, grad):
    return (grad,)

def back_keep(v):
    return (v, None)

def back_low(kept, grad):
    return (low(grad),)
low.defvjp(low_keep, low_pass)
low_back.defvjp(back_keep, back_low)

def conv_silu(source, weight, offset):
    tap_count = weight.shape[0]
    length = source.shape[1]
    padded = jnp.pad(source, ((0, 0), (tap_count - 1, 0), (0, 0)))
    summed = offset + jnp.zeros_like(source)
    for lag_index in range(tap_count):
        begin = tap_count - 1 - lag_index
        summed = summed + weight[lag_index] * padded[:, begin:begin + length]
    return jax.nn.silu(summed)

def span_scan(inputs, step_sizes, decay_rate, write_vec, read_vec):
    seq_count, length, head_count, head_size = inputs.shape
    state_size = write_vec.shape[-1]
    blocks = length // SPAN

    def to_blocks(values):
        shaped = values.reshape((seq_count, blocks, SPAN) + values.shape[2:])
        return jnp.moveaxis(shaped, 1, 0)
    log_decay = step_sizes * decay_rate
    causal = jnp.arange(SPAN)[:, None] >= jnp.arange(SPAN)[None, :]
    causal = causal[None, :, :, None]

    def advance(carry_state, pieces):
        in_block, step_block, log_block, write_block, read_block = pieces
        cum_log = jnp.cumsum(log_block, axis=1)
        spread = cum_log[:, :, None, :] - cum_log[:, None, :, :]
        within = jnp.where(causal, jnp.exp(jnp.where(causal, spread, 0.0)), 0.0)
        scores = jnp.einsum('stn,srn->str', read_block, write_block, precision=HIGH)
        mixing = scores[:, :, :, None] * within * step_block[:, None, :, :]
        local_out = jnp.einsum('strh,srhp->sthp', mixing, in_block, precision=HIGH)
        carried = jnp.einsum('stn,shpn->sthp', read_block, carry_state, precision=HIGH)
        carried = carried * jnp.exp(cum_log)[:, :, :, None]
        last_cum = cum_log[:, -1, :]
        tail_weight = jnp.exp(last_cum[:, None, :] - cum_log) * step_block
        added_state = jnp.einsum('srh,srhp,srn->shpn', tail_weight, in_block, write_block, precision=HIGH)
        carry_state = jnp.exp(last_cum)[:, :, None, None] * carry_state + added_state
        return (carry_state, local_out + carried)
    zero_state = jnp.zeros((seq_count, head_count, head_size, state_size), jnp.float32)
    blocked = (to_blocks(inputs), to_blocks(step_sizes), to_blocks(log_decay), to_blocks(write_vec), to_blocks(read_vec))
    ignored, outputs = lax.scan(jax.checkpoint(advance), zero_state, blocked)
    return jnp.moveaxis(outputs, 0, 1).reshape(inputs.shape)

def mixer(inner_raw, step_raw, write_vec, read_vec, gate_raw, conv_inner, conv_inner_bias, step_bias, decay_log, skip_gain):
    inputs = conv_silu(inner_raw, conv_inner, conv_inner_bias)
    seq_count, length, inner_width = inputs.shape
    head_count = step_bias.shape[0]
    inputs = inputs.reshape(seq_count, length, head_count, inner_width // head_count)
    step_sizes = jax.nn.softplus(step_raw + step_bias)
    decay_rate = -jnp.exp(decay_log)
    mixed = span_scan(inputs, step_sizes, decay_rate, write_vec, read_vec)
    mixed = mixed + skip_gain[:, None] * inputs
    return mixed.reshape(seq_count, length, inner_width) * jax.nn.silu(gate_raw)

def forward(hidden, in_gain, proj_main, proj_step, proj_state, conv_inner, conv_inner_bias, conv_state, conv_state_bias, step_bias, decay_log, skip_gain, out_gain, proj_out):
    row_count, model_width = hidden.shape
    seq_count = row_count // LEN
    scale_in = lax.rsqrt(lax.optimization_barrier(jnp.mean(hidden * hidden, axis=-1, keepdims=True)) + EPS)
    normed = low(hidden * scale_in * in_gain)
    main = jnp.dot(normed, proj_main.reshape(model_width, -1), precision=HIGH, preferred_element_type=jnp.float32)
    main = low_back(low(main))
    inner_width = main.shape[1] // 2
    step_raw = low_back(low(jnp.dot(normed, proj_step, precision=HIGH, preferred_element_type=jnp.float32)))
    state_raw = low_back(low(jnp.dot(normed, proj_state, precision=HIGH, preferred_element_type=jnp.float32)))
    state_conv = conv_silu(state_raw.reshape(seq_count, LEN, -1), conv_state, conv_state_bias)
    half_width = state_conv.shape[-1] // 2
    gated_in = mixer(main[:, inner_width:].reshape(seq_count, LEN, inner_width), step_raw.reshape(seq_count, LEN, -1), state_conv[:, :, :half_width], state_conv[:, :, half_width:], main[:, :inner_width].reshape(seq_count, LEN, inner_width), conv_inner, conv_inner_bias, step_bias, decay_log, skip_gain)
    gated_in = gated_in.reshape(row_count, inner_width)
    scale_out = lax.rsqrt(lax.optimization_barrier(jnp.mean(gated_in * gated_in, axis=-1, keepdims=True)) + EPS)
    gated = low(gated_in * scale_out * out_gain)
    branch = jnp.dot(gated, proj_out.T, precision=HIGH, preferred_element_type=jnp.float32)
    return hidden + branch

def reference(hidden, in_gain, proj_main, proj_step, proj_state, conv_inner, conv_inner_bias, conv_state, conv_state_bias, step_bias, decay_log, skip_gain, out_gain, proj_out, grad_out):
    params = tuple((param.astype(jnp.float32) for param in (in_gain, proj_main, proj_step, proj_state, conv_inner, conv_inner_bias, conv_state, conv_state_bias, step_bias, decay_log, skip_gain, out_gain, proj_out)))
    total_seqs = TOKENS // LEN
    group_seqs = math.gcd(total_seqs, max(1, 4096 // LEN))
    group_rows = group_seqs * LEN
    group_count = TOKENS // group_rows
    hidden_groups = hidden.astype(jnp.float32).reshape(group_count, group_rows, D)
    grad_groups = grad_out.astype(jnp.float32).reshape(group_count, group_rows, D)

    def one_group(grad_sums, pieces):
        block_in, block_grad = pieces
        outputs, pull_back = jax.vjp(forward, block_in, *params)
        grad_list = pull_back(block_grad)
        grad_sums = jax.tree.map(jnp.add, grad_sums, tuple(grad_list[1:]))
        return (grad_sums, (outputs.astype(jnp.bfloat16), grad_list[0].astype(jnp.bfloat16)))
    zero_sums = tuple((jnp.zeros_like(param) for param in params))
    grad_sums, (outputs, grad_rows) = lax.scan(one_group, zero_sums, (hidden_groups, grad_groups))
    return (outputs.reshape(TOKENS, D), grad_rows.reshape(TOKENS, D), grad_sums[0], grad_sums[1], grad_sums[2], grad_sums[3], grad_sums[4], grad_sums[5], grad_sums[6], grad_sums[7], grad_sums[8], grad_sums[9], grad_sums[10], grad_sums[11], grad_sums[12])
```

```python
import functools

import jax
import jax.numpy as jnp
from jax import lax
from jax.experimental import pallas as pl
from jax.experimental.pallas import tpu as pltpu
from jax.sharding import PartitionSpec as P

MESH = pl.DeviceIdType.MESH
CHUNKS = ((0, 256), (256, 768), (1024, 768), (1792, 768))
COLS = 2560
ORDERS = ("xyz", "yzx", "zxy")

def place():
    dp, tp = lax.axis_index("dp"), lax.axis_index("tensor")
    return dict(x=dp // 8, y=(dp // 2) % 4, z=(tp // 2) * 2 + dp % 2, core=tp % 2)

def device_at(at):
    return ((at["x"] * 4 + at["y"]) * 2 + at["z"] % 2, (at["z"] // 2) * 2 + at["core"])

def moved(at, axis, by):
    return {**at, axis: (at[axis] + by) % 4}

def units(at, whole):
    return tuple([slice(None) if "z" in whole else at["z"] // 2, slice(None) if "x" in whole else at["x"],
         slice(None) if "y" in whole else at["y"], slice(None) if "z" in whole else at["z"] % 2])

def gather_kernel(shard, ends, cots, params, full, rows_out, cots_out, params_out, send, recv, local, swap_send, swap_recv):
    at = place()
    mate = {**at, "core": 1 - at["core"]}
    far = moved(at, "z", 2)
    near = [moved(at, axis, by) for axis in "xyz" for by in (1, 3)]
    barrier = pltpu.get_barrier_semaphore()
    greet = near + [mate, far]
    for other in greet:
        pl.semaphore_signal(barrier, inc=1, device_id=device_at(other), device_id_type=MESH)
    pl.semaphore_wait(barrier, len(greet))

    def copy(region, source, axis, by, chunk, piece, stage, kind):
        return pltpu.make_async_remote_copy(src_ref=source, dst_ref=region, send_sem=send.at[chunk, piece, stage, kind],
            recv_sem=recv.at[chunk, piece, stage, kind], device_id=device_at(moved(at, axis, by)), device_id_type=MESH)

    def part(where, whole, chunk, piece, half=None):
        begin, width = CHUNKS[chunk]
        if half is not None:
            width = width // 2
            begin = begin + half * width
        return full.at[units(where, whole) + (piece, slice(None), pl.ds(begin, width))]

    own_rows = pl.ds(pl.multiple_of(at["core"] * 256, 256), 256)
    locals_ = [pltpu.make_async_copy(shard, full.at[units(at, "")], local.at[0]),
               pltpu.make_async_copy(ends, rows_out.at[own_rows], local.at[1]),
               pltpu.make_async_copy(cots, cots_out.at[own_rows], local.at[2]),
               pltpu.make_async_copy(params, params_out.at[at["z"] // 2], local.at[3])]
    for c in locals_:
        c.start()
    swaps = [pltpu.make_async_remote_copy(src_ref=s, dst_ref=d, send_sem=swap_send.at[i], recv_sem=swap_recv.at[i], device_id=device_at(o), device_id_type=MESH)
        for i, (s, d, o) in enumerate([(ends, rows_out.at[own_rows], mate), (cots, cots_out.at[own_rows], mate), (params, params_out.at[at["z"] // 2], far)])]
    for c in swaps:
        c.start()
    locals_[0].wait()
    started = []
    live = {}
    def step(chunk, k):
        stage, forward = k // 2, k % 2
        for piece in range(3):
            order = ORDERS[piece]
            axis, whole = order[stage], order[:stage]
            if not forward:
                if stage > 0:
                    for c in live.pop((chunk, piece)):
                        c.wait_recv()
                src = part(at, whole, chunk, piece)
                fulls = [copy(src, src, axis, by, chunk, piece, stage, i) for i, by in enumerate((1, 3))]
                for c in fulls:
                    c.start()
                started.extend(fulls)
                live[chunk, piece] = fulls
            else:
                halves = []
                for i, c in enumerate(live[chunk, piece]):
                    c.wait_recv()
                    by = (1, 3)[i]
                    src = part(moved(at, axis, -by), whole, chunk, piece, half=i)
                    h = copy(src, src, axis, by, chunk, piece, stage, 2 + i)
                    h.start()
                    halves.append(h)
                started.extend(halves)
                live[chunk, piece] = halves
    n = len(CHUNKS)
    for t in range(n + 5):
        for chunk in range(n):
            if 0 <= t - chunk < 6:
                step(chunk, t - chunk)
    for group in live.values():
        for c in group:
            c.wait_recv()
    for c in started:
        c.wait_send()
    for c in swaps:
        c.wait()
    for c in locals_[1:]:
        c.wait()

def gather(shard, rows, cots, params):
    any_ = pl.BlockSpec(memory_space=pl.ANY)
    n = len(CHUNKS)
    return pl.pallas_call(
        gather_kernel,
        out_shape=[jax.ShapeDtypeStruct((2, 4, 4, 2, 3, 16, COLS), jnp.bfloat16),
                   jax.ShapeDtypeStruct((512, 1536), jnp.bfloat16), jax.ShapeDtypeStruct((512, 1536), jnp.bfloat16),
                   jax.ShapeDtypeStruct((2,) + params.shape, jnp.float32)],
        in_specs=[any_] * 4, out_specs=[any_] * 4,
        scratch_shapes=[pltpu.SemaphoreType.DMA((n, 3, 3, 4)), pltpu.SemaphoreType.DMA((n, 3, 3, 4)), pltpu.SemaphoreType.DMA((4,)),
                        pltpu.SemaphoreType.DMA((3,)), pltpu.SemaphoreType.DMA((3,))],
        compiler_params=pltpu.CompilerParams(collective_id=0, has_side_effects=True),
    )(shard, rows, cots, params)


F32, BF16 = jnp.float32, jnp.bfloat16
EPS = 1e-5
T, SPAN, HEAD, STATE, GROUP = 512, 256, 64, 128, 4
WIDE = GROUP * HEAD
INNER = 3072


def dot(a, b, ca=1, cb=0):
    return lax.dot_general(a, b, (((ca,), (cb,)), ((), ())), preferred_element_type=F32)


def lanes(rows, width=T):
    return lax.broadcasted_iota(jnp.int32, (rows, width), 1)


def later(u, k):
    return jnp.where(lanes(u.shape[0]) >= k, pltpu.roll(u, k, 1), 0.0) if k else u


def sooner(u, k):
    return jnp.where(lanes(u.shape[0]) < T - k, pltpu.roll(u, T - k, 1), 0.0) if k else u


def sig(v):
    return 1.0 / (1.0 + jnp.exp(-v))


def split(v):
    a = v.astype(BF16)
    r = v - a.astype(F32)
    b = r.astype(BF16)
    return a, b, (r - b.astype(F32)).astype(BF16)


def exact_dot(v, ones):
    n = v.shape[0]
    s = dot(jnp.concatenate(split(v), axis=0), ones)
    return s[:n] + s[n:2 * n] + s[2 * n:]


def tri(n, keep):
    r = lax.broadcasted_iota(jnp.int32, (n, n), 0)
    c = lax.broadcasted_iota(jnp.int32, (n, n), 1)
    return jnp.where(keep(r, c), 1.0, 0.0).astype(BF16)


def conv(u, cols):
    moved = [later(u, k) for k in range(4)]
    p = cols[:, 4:5] + cols[:, 0:1] * moved[0]
    for k in range(1, 4):
        p = p + cols[:, k:k + 1] * moved[k]
    return p, moved


def decay(cum_row, cum_col, b):
    r = cum_row[:, b * SPAN:(b + 1) * SPAN]
    return jnp.exp(jnp.minimum(r - cum_col, 0.0))


def fwd_kernel(x, g, wst, wg, wi, wo, prm, heads, spar,
               xt, gt, zt, ut, dgt, yt, sums, dtt, cumt, cumc, stept, statet, bc, bct, cbt,
               ):
    j = pl.program_id(0)

    @pl.when(j == 0)
    def _():
        xt[...] = x[...].T
        gt[...] = g[...].T
        sums[...] = jnp.zeros_like(sums)
        for zh in range(2):
            raw = dot(x[...], wst[zh]).T.astype(BF16)
            statet[zh * 128:(zh + 1) * 128, :] = raw[:128]
            stept[zh * 16:(zh + 1) * 16, :] = raw[128:144]
        for zh in range(2):
            p, _ = conv(statet[zh * 128:(zh + 1) * 128, :].astype(F32), spar[zh * 128:(zh + 1) * 128, :])
            c = p * sig(p)
            bct[zh * 128:(zh + 1) * 128, :] = c.astype(BF16)
            bc[:, zh * 128:(zh + 1) * 128] = c.T.astype(BF16)
        upper = tri(SPAN, lambda r, c: r <= c)
        for b in range(2):
            rows = pl.ds(b * SPAN, SPAN)
            scores = dot(bc[rows, 0:128], bc[rows, 128:256], 1, 1)
            cbt[b] = scores * upper.astype(F32)
        cumc[...] = jnp.zeros_like(cumc)
        for zh in range(2):
            cols = heads[zh].T
            v = stept[zh * 16:(zh + 1) * 16, :].astype(F32) + cols[:16, 6:7]
            dt = jnp.maximum(v, 0.0) + jnp.log1p(jnp.exp(-jnp.abs(v)))
            dtt[zh * 16:(zh + 1) * 16, :] = dt
            la = dt * -jnp.exp(cols[:16, 7:8])
            for b in range(2):
                cumt[zh * 16:(zh + 1) * 16, b * SPAN:(b + 1) * SPAN] = exact_dot(la[:, b * SPAN:(b + 1) * SPAN], upper)
        cumc[...] = jnp.concatenate([cumt[...], jnp.zeros((96, T), F32)], axis=0).T

    zt[...] = dot(x[...], wg[0]).T.astype(BF16)
    ut[...] = dot(x[...], wi[0]).T.astype(BF16)
    dgt[...] = dot(g[...], wo[0]).T.astype(BF16)
    base = (j % 2) * 16 + (j // 2) * GROUP
    cols = prm[0].T
    cc = pltpu.roll(cumc[...], 128 - base, 1)
    hcols = heads[j % 2].T
    skip_all = pltpu.roll(jnp.broadcast_to(hcols[:, 8:9], (128, 128)), 128 - (j // 2) * GROUP, 0)
    s1 = jnp.zeros((1, T), F32)
    s2 = jnp.zeros((1, T), F32)
    for i in range(GROUP):
        r = slice(i * HEAD, (i + 1) * HEAD)
        p, _ = conv(ut[r, :].astype(F32), cols[r])
        xs = p * sig(p)
        dt = dtt[pl.ds(base + i, 1), :]
        cum = cumt[pl.ds(base + i, 1), :]
        xdt = (xs * dt)
        xdtb = xdt.astype(BF16)
        ys = []
        for b in range(2):
            m = (decay(cum, cc[b * SPAN:(b + 1) * SPAN, i:i + 1], b) * cbt[b]).astype(BF16)
            ys.append(dot(xdtb[:, b * SPAN:(b + 1) * SPAN], m))
        tail = jnp.exp(cum[:, SPAN - 1:SPAN] - cum[:, :SPAN])
        xe = (xdt[:, :SPAN] * tail).astype(BF16)
        st = dot(xe, bc[0:SPAN, 0:128]).astype(BF16)
        ys[1] = ys[1] + jnp.exp(cum[:, SPAN:]) * dot(st, bc[SPAN:, 128:256], 1, 1)
        y = jnp.concatenate(ys, axis=1)
        yt[r, :] = y
        y = y + skip_all[i:i + 1, 0:1] * xs
        z = zt[r, :].astype(F32)
        v = y * (z * sig(z))
        s1 = s1 + jnp.sum(v * v, axis=0, keepdims=True)
        s2 = s2 + jnp.sum(dgt[r, :].astype(F32) * cols[r, 5:6] * v, axis=0, keepdims=True)
    sums[0:1, :] += s1
    sums[1:2, :] += s2


def bwd_kernel(xt, gt, wst, wg, wi, wo, prm, heads, zt, ut, dgt, yt, sums, dtt, cumt, cumc, stept, bc, bct, cbt,
               grads, prow, hrow, dn, br, dbct, dstept,
               pcols, dnt, brt, dcbt, dzt, dut, gat, dye_all, xe_all, st_all, ds_all, cross, dcum, ddt1, gskip):
    j = pl.program_id(0)

    @pl.when(j == 0)
    def _():
        for ref in (dnt, brt, dcbt, cross, dcum, ddt1, gskip):
            ref[...] = jnp.zeros_like(ref)

    base = (j % 2) * 16 + (j // 2) * GROUP
    cols = prm[0].T
    cc = pltpu.roll(cumc[...], 128 - base, 1)
    hcols = heads[j % 2].T
    skip_all = pltpu.roll(jnp.broadcast_to(hcols[:, 8:9], (128, 128)), 128 - (j // 2) * GROUP, 0)
    r_out = lax.rsqrt(sums[0:1, :] / INNER + EPS)
    k2 = r_out * r_out * r_out * sums[1:2, :] / INNER
    for i in range(GROUP):
        r = slice(i * HEAD, (i + 1) * HEAD)
        skip = skip_all[i:i + 1, 0:1]
        p, moved = conv(ut[r, :].astype(F32), cols[r])
        sp = sig(p)
        xs = p * sp
        dsil = sp + xs * (1.0 - sp)
        yssm = yt[r, :]
        y = yssm + skip * xs
        z = zt[r, :].astype(F32)
        sz = sig(z)
        zs = z * sz
        v = y * zs
        dg = dgt[r, :].astype(F32)
        og = cols[r, 5:6]
        vr = v * r_out
        gat[r, :] = (vr * og).astype(BF16)
        gog = jnp.sum(dg * vr, axis=1, keepdims=True)
        dv = dg * og * r_out - v * k2
        dy = dv * zs
        dzt[r, :] = (dv * y * (sz + zs * (1.0 - sz))).astype(BF16)
        dyb = dy.astype(BF16)
        gskip[pl.ds(base + i, 1), :] = jnp.sum(dy * xs, axis=0, keepdims=True)
        dt = dtt[pl.ds(base + i, 1), :]
        cum = cumt[pl.ds(base + i, 1), :]
        xdt = xs * dt
        xdtb = xdt.astype(BF16)
        dxs = []
        for b in range(2):
            c = slice(b * SPAN, (b + 1) * SPAN)
            w = decay(cum, cc[c, i:i + 1], b)
            m = (w * cbt[b]).astype(BF16)
            dxs.append(dot(dyb[:, c], m, 1, 1))
            dcbt[b] += dot(xdtb[:, c], dyb[:, c], 0, 0) * w
        tail = jnp.exp(cum[:, SPAN - 1:SPAN] - cum[:, :SPAN])
        xe = (xdt[:, :SPAN] * tail).astype(BF16)
        st = dot(xe, bc[0:SPAN, 0:128]).astype(BF16)
        dye = (dy[:, SPAN:] * jnp.exp(cum[:, SPAN:])).astype(BF16)
        ds = dot(dye, bc[SPAN:, 128:256]).astype(BF16)
        xe_all[r, :] = xe
        st_all[r, :] = st
        dye_all[r, :] = dye
        ds_all[r, :] = ds
        dxs[0] = dxs[0] + tail * dot(ds, bc[0:SPAN, 0:128], 1, 1)
        dx = jnp.concatenate(dxs, axis=1)
        dcum[pl.ds(base + i, 1), :] = jnp.sum(dyb.astype(F32) * yssm - xdtb.astype(F32) * dx, axis=0, keepdims=True)
        ddt1[pl.ds(base + i, 1), :] = jnp.sum(xs * dx, axis=0, keepdims=True)
        dp = (dt * dx + skip * dy) * dsil
        taps = [jnp.sum(dp * moved[k], axis=1, keepdims=True) for k in range(4)]
        pcols[r, :] = jnp.concatenate(taps + [jnp.sum(dp, axis=1, keepdims=True), gog, jnp.zeros((HEAD, 122), F32)], axis=1)
        du = cols[r, 0:1] * dp
        for k in range(1, 4):
            du = du + cols[r, k:k + 1] * sooner(dp, k)
        dut[r, :] = du.astype(BF16)
    prow[0] = pcols[...].T[:8]
    cross[1] += dot(st_all[...], dye_all[...], 0, 0)
    cross[0] += dot(ds_all[...], xe_all[...], 0, 0)
    grads[0, :, 0:256] = dot(xt[...], dzt[...], 1, 1).astype(BF16)
    grads[0, :, 256:512] = dot(xt[...], dut[...], 1, 1).astype(BF16)
    grads[0, :, 512:768] = dot(gt[...], gat[...], 1, 1).astype(BF16)
    dnt[...] += dot(wg[0], dzt[...]) + dot(wi[0], dut[...])
    brt[...] += dot(wo[0], gat[...])

    @pl.when(j == 5)
    def _():
        suffix = tri(T, lambda r, c: r >= c)
        dla = exact_dot(dcum[...], suffix)
        for zh in range(2):
            rows = slice(zh * 16, (zh + 1) * 16)
            hc = heads[zh].T
            rate = -jnp.exp(hc[:16, 7:8])
            d = dla[rows]
            ddt = ddt1[rows, :] + rate * d
            pre = stept[rows, :].astype(F32) + hc[:16, 6:7]
            dstep = ddt * sig(pre)
            dstept[zh * 16:(zh + 1) * 16, :] = dstep.astype(BF16)
            gd = jnp.sum(d * dtt[rows, :] * rate, axis=1, keepdims=True)
            hcol = jnp.concatenate(
                [jnp.sum(dstep, axis=1, keepdims=True), gd, jnp.sum(gskip[rows, :], axis=1, keepdims=True), jnp.zeros((16, 125), F32)], axis=1)
            hrow[:, zh * 128:(zh + 1) * 128] = jnp.concatenate([hcol, jnp.zeros((112, 128), F32)], axis=0).T[:8]
            keep = lax.broadcasted_iota(jnp.int32, (16, T), 0) < 12
            dsp = jnp.concatenate([jnp.where(keep, dstep, 0.0).astype(BF16), jnp.zeros((112, T), BF16)], axis=0)
            dnt[...] += dot(wst[zh, :, 128:256], dsp)
        upper = tri(SPAN, lambda r, c: r <= c).astype(F32)
        for b in range(2):
            c = slice(b * SPAN, (b + 1) * SPAN)
            d = (dcbt[b] * upper).astype(BF16)
            db = dot(bct[128:256, c], d, 1, 1)
            dc = dot(bct[0:128, c], d)
            if b == 0:
                db = db + cross[0]
            else:
                dc = dc + cross[1]
            dbct[0:128, c] = db.astype(BF16)
            dbct[128:256, c] = dc.astype(BF16)
        dn[...] = dnt[...].T.astype(BF16)
        br[...] = brt[...].T.astype(BF16)


def const(shape):
    return pl.BlockSpec(shape, lambda j: (0,) * len(shape))


def wspec(k):
    return pl.BlockSpec((1, 1536, 256), lambda j: (j % 2, 0, 1 + 3 * (j // 2) + k))


def group_spec(width=T):
    return pl.BlockSpec((WIDE, width), lambda j: ((j % 2) * 3 + j // 2, 0))


PRM = pl.BlockSpec((1, 16, 256), lambda j: (j % 2, 0, j // 2))
PARAMS = pltpu.CompilerParams(dimension_semantics=("arbitrary",), vmem_limit_bytes=60 << 20)


def sds(shape, dtype=F32):
    return jax.ShapeDtypeStruct(shape, dtype)


def forward(x, g, w, prm, spar):
    return pl.pallas_call(
        fwd_kernel, grid=(6,),
        in_specs=[const((T, 1536)), const((T, 1536)), const((2, 1536, 256)), wspec(0), wspec(1), wspec(2), PRM,
                  const((2, 16, 128)), const((256, 8))],
        out_specs=[const((1536, T)), const((1536, T)), group_spec(), group_spec(), group_spec(), group_spec(), const((8, T)),
                   const((32, T)), const((32, T)), const((T, 128)), const((32, T)), const((256, T)), const((T, 256)), const((256, T)), const((2, SPAN, SPAN))],
        out_shape=[sds((1536, T), BF16), sds((1536, T), BF16), sds((1536, T), BF16), sds((1536, T), BF16), sds((1536, T), BF16), sds((1536, T)), sds((8, T)),
                   sds((32, T)), sds((32, T)), sds((T, 128)), sds((32, T), BF16), sds((256, T), BF16), sds((T, 256), BF16), sds((256, T), BF16), sds((2, SPAN, SPAN))],
        compiler_params=PARAMS,
    )(x, g, w, w, w, w, prm, prm, spar)


def backward(w, prm, xt, gt, zt, ut, dgt, yt, sums, dtt, cumt, cumc, stept, bc, bct, cbt):
    return pl.pallas_call(
        bwd_kernel, grid=(6,),
        in_specs=[const((1536, T)), const((1536, T)), const((2, 1536, 256)), wspec(0), wspec(1), wspec(2), PRM, const((2, 16, 128)),
                  group_spec(), group_spec(), group_spec(), group_spec(), const((8, T)), const((32, T)), const((32, T)), const((T, 128)), const((32, T)),
                  const((T, 256)), const((256, T)), const((2, SPAN, SPAN))],
        out_specs=[pl.BlockSpec((1, 1536, 768), lambda j: (j % 2, 0, j // 2)), pl.BlockSpec((1, 8, WIDE), lambda j: ((j % 2) * 3 + j // 2, 0, 0)),
                   const((8, 256)), const((T, 1536)), const((T, 1536)), const((256, T)), const((32, T))],
        out_shape=[sds((2, 1536, 2304), BF16), sds((6, 8, WIDE)), sds((8, 256)), sds((T, 1536), BF16), sds((T, 1536), BF16), sds((256, T), BF16), sds((32, T), BF16)],
        scratch_shapes=[pltpu.VMEM((WIDE, 128), F32), pltpu.VMEM((1536, T), F32), pltpu.VMEM((1536, T), F32), pltpu.VMEM((2, SPAN, SPAN), F32),
                        pltpu.VMEM((WIDE, T), BF16), pltpu.VMEM((WIDE, T), BF16), pltpu.VMEM((WIDE, T), BF16),
                        pltpu.VMEM((WIDE, SPAN), BF16), pltpu.VMEM((WIDE, SPAN), BF16), pltpu.VMEM((WIDE, 128), BF16), pltpu.VMEM((WIDE, 128), BF16),
                        pltpu.VMEM((2, 128, SPAN), F32), pltpu.VMEM((32, T), F32), pltpu.VMEM((32, T), F32), pltpu.VMEM((32, T), F32)],
        compiler_params=PARAMS,
    )(xt, gt, w, w, w, w, prm, prm, zt, ut, dgt, yt, sums, dtt, cumt, cumc, stept, bc, bct, cbt)


RCHUNKS = ((0, 768), (768, 768), (1536, 768), (2304, 128))
RCOLS = 2432
SUMS = 72


def swap_kernel(mine, total, there, send, recv):
    at = place()
    mate = device_at({**at, "core": 1 - at["core"]})
    barrier = pltpu.get_barrier_semaphore()
    pl.semaphore_signal(barrier, inc=1, device_id=mate, device_id_type=MESH)
    pl.semaphore_wait(barrier, 1)
    c = pltpu.make_async_remote_copy(src_ref=mine, dst_ref=there, send_sem=send, recv_sem=recv, device_id=mate, device_id_type=MESH)
    c.start()
    c.wait()
    total[...] = mine[...] + there[...]


def swap(rows):
    whole = pl.BlockSpec(memory_space=pltpu.VMEM)
    return pl.pallas_call(
        swap_kernel, out_shape=sds(rows.shape), in_specs=[whole], out_specs=whole,
        scratch_shapes=[pltpu.VMEM(rows.shape, F32), pltpu.SemaphoreType.DMA, pltpu.SemaphoreType.DMA],
        compiler_params=pltpu.CompilerParams(collective_id=1, has_side_effects=True),
    )(rows)


def reduce_axis(stage, piece):
    order = ORDERS[piece]
    return order[2 - stage], order[:2 - stage]


def region_shape(stage, piece, width):
    whole = ORDERS[piece][:2 - stage]
    dims = ([2] if "z" in whole else []) + ([4] if "x" in whole else []) + ([4] if "y" in whole else []) + ([2] if "z" in whole else [])
    return tuple(dims) + (16, width)


def half_of(ref, stage, piece, width, half):
    if stage == 0:
        return ref.at[pl.ds(2 * half, 2)] if piece == 0 else ref.at[:, pl.ds(2 * half, 2)]
    if stage == 1:
        return ref.at[pl.ds(2 * half, 2)] if piece < 2 else ref.at[half]
    return ref.at[:, pl.ds(half * (width // 2), width // 2)] if width > 128 else ref


def half_shape(stage, piece, width):
    if stage == 0:
        return (2, 4, 16, width) if piece == 0 else (2, 2, 2, 16, width)
    if stage == 1:
        return (2, 16, width)
    return (16, width // 2) if width > 128 else (16, width)


def add_into(target, *others):
    def add(t, o):
        v = t[...].astype(F32)
        for other in o:
            v = v + other[...].astype(F32)
        t[...] = v.astype(BF16)
    if len(target.shape) == 2:
        add(target, others)
    else:
        @pl.loop(0, target.shape[0])
        def _(i):
            add(target.at[i], [o.at[i] for o in others])


def reduce_kernel(grads, xt, wst, statet, spar, dbct, dstept, dn, br, hidden, cot, gain, prow, hrow,
                  out, gstate, gsmall, new_hidden, grad_hidden, *scratch):
    n = len(RCHUNKS)
    part, lefts, rights, left_halves, right_halves = scratch[0], *[scratch[1 + 9 * n * q: 1 + 9 * n * (q + 1)] for q in range(4)]
    (dbct_in, dn_in, br_in, dstate, lhs, dst, vec, vec_in, gain_in, quarter, quarters,
     send, recv, local, swap_send, swap_recv, vec_send, vec_recv, q_send, q_recv) = scratch[1 + 36 * n:]
    at = place()
    mate = {**at, "core": 1 - at["core"]}
    far = moved(at, "z", 2)
    far_mate = {**far, "core": 1 - at["core"]}
    greet = [moved(at, axis, by) for axis in "xyz" for by in (1, 2, 3)] + [mate, far_mate]
    barrier = pltpu.get_barrier_semaphore()
    for other in greet:
        pl.semaphore_signal(barrier, inc=1, device_id=device_at(other), device_id_type=MESH)
    pl.semaphore_wait(barrier, len(greet))

    def remote(src, dst_ref, s, r, to):
        c = pltpu.make_async_remote_copy(src_ref=src, dst_ref=dst_ref, send_sem=s, recv_sem=r, device_id=device_at(to), device_id_type=MESH)
        c.start()
        return c

    loads = []
    for chunk in range(n - 1):
        begin, width = RCHUNKS[chunk]
        cols = pl.ds(begin, width)
        c = pltpu.make_async_copy(grads.at[..., cols], part.at[..., cols], local.at[chunk])
        c.start()
        loads.append(c)
    mine = pl.ds(pl.multiple_of(at["core"] * 256, 256), 256)
    theirs = pl.ds(pl.multiple_of((1 - at["core"]) * 256, 256), 256)
    swaps = [remote(s, d, swap_send.at[i], swap_recv.at[i], mate)
             for i, (s, d) in enumerate([(dbct, dbct_in), (dn.at[theirs], dn_in), (br.at[theirs], br_in)])]
    started = []

    def slot(chunk, piece, stage):
        return (chunk * 3 + piece) * 3 + stage

    def block(where, chunk, piece, stage):
        begin, width = RCHUNKS[chunk]
        axis, whole = reduce_axis(stage, piece)
        return part.at[units(where, whole) + (piece, slice(None), pl.ds(begin, width))]

    def half(ref, chunk, piece, stage, h):
        return half_of(ref, stage, piece, RCHUNKS[chunk][1], h)

    live = {}

    def begin_stage(chunk, piece, stage):
        axis, _ = reduce_axis(stage, piece)
        k = slot(chunk, piece, stage)
        split = not (stage == 2 and RCHUNKS[chunk][1] <= 128)
        right, left, opposite = moved(at, axis, 1), moved(at, axis, 3), moved(at, axis, 2)
        sems = lambda i: (send.at[chunk, piece, stage, i], recv.at[chunk, piece, stage, i])
        flights = [remote(half(block(opposite, chunk, piece, stage), chunk, piece, stage, 0), left_halves[k], *sems(0), right)]
        if split:
            flights.append(remote(half(block(opposite, chunk, piece, stage), chunk, piece, stage, 1), right_halves[k], *sems(1), left))
            flights.append(remote(half(block(right, chunk, piece, stage), chunk, piece, stage, 1),
                                  half(lefts[k], chunk, piece, stage, 1), *sems(2), right))
            flights.append(remote(half(block(left, chunk, piece, stage), chunk, piece, stage, 0),
                                  half(rights[k], chunk, piece, stage, 0), *sems(3), left))
        else:
            flights.append(remote(block(left, chunk, piece, stage), rights[k], *sems(3), left))
        live[chunk, piece] = flights
        started.extend(flights)

    def middle_stage(chunk, piece, stage):
        axis, _ = reduce_axis(stage, piece)
        k = slot(chunk, piece, stage)
        split = not (stage == 2 and RCHUNKS[chunk][1] <= 128)
        right, left = moved(at, axis, 1), moved(at, axis, 3)
        sems = lambda i: (send.at[chunk, piece, stage, i], recv.at[chunk, piece, stage, i])
        flights = live[chunk, piece]
        flights[0].wait_recv()
        mid = half(block(right, chunk, piece, stage), chunk, piece, stage, 0)
        add_into(mid, left_halves[k])
        onward = [remote(mid, half(lefts[k], chunk, piece, stage, 0), *sems(4), right)]
        if split:
            flights[1].wait_recv()
            mid = half(block(left, chunk, piece, stage), chunk, piece, stage, 1)
            add_into(mid, right_halves[k])
            onward.append(remote(mid, half(rights[k], chunk, piece, stage, 1), *sems(5), left))
        live[chunk, piece] = (flights[2:] if split else flights[1:]) + onward
        started.extend(onward)

    def end_stage(chunk, piece, stage):
        for c in live.pop((chunk, piece)):
            c.wait_recv()
        k = slot(chunk, piece, stage)
        add_into(block(at, chunk, piece, stage), lefts[k], rights[k])

    def step(chunk, k):
        for piece in range(3):
            if k % 2 == 0:
                if k > 0:
                    end_stage(chunk, piece, k // 2 - 1)
                if k < 6:
                    begin_stage(chunk, piece, k // 2)
            else:
                middle_stage(chunk, piece, k // 2)

    for chunk in range(n - 1):
        loads[chunk].wait()
        step(chunk, 0)

    swaps[0].wait_recv()
    vec[...] = jnp.zeros_like(vec)
    for q in range(4):
        r = slice(q * 64, (q + 1) * 64)
        cols = spar[r]
        p, shifted = conv(statet[r, :].astype(F32), cols)
        sp = sig(p)
        dp = (dbct[r, :].astype(F32) + dbct_in[r, :].astype(F32)) * (sp + p * sp * (1.0 - sp))
        du = cols[:, 0:1] * dp
        for k in range(1, 4):
            du = du + cols[:, k:k + 1] * sooner(dp, k)
        dstate[r, :] = du.astype(BF16)
        dst[r, :] = jnp.concatenate([jnp.sum(dp * shifted[k], axis=1, keepdims=True) for k in range(4)]
                                    + [jnp.sum(dp, axis=1, keepdims=True), jnp.zeros((64, 123), F32)], axis=1)
    vec[48:56, :] = dst[...].T[:8]
    last = n - 1
    for zh in range(2):
        lhs[zh, 0:64, :] = dstate[pl.ds(zh * 128 + pl.multiple_of(at["core"] * 64, 64), 64), :]
        lhs[zh, 64:80, :] = dstept[zh * 16:(zh + 1) * 16, :]
        lhs[zh, 80:128, :] = jnp.zeros((48, T), BF16)
        g = dot(xt[...], lhs[zh], 1, 1).astype(BF16).reshape(4, 4, 2, 3, 16, 128)
        part[zh, :, :, :, :, :, pl.ds(RCHUNKS[last][0], 128)] = g
    step(last, 0)

    for s in swaps[1:]:
        s.wait_recv()
    own_state = dstate[:, mine].astype(F32).T.astype(BF16)
    whole = dn[mine, :].astype(F32) + dn_in[...].astype(F32)
    whole = whole + dot(own_state[:, 0:128], wst[0, :, 0:128], 1, 1) + dot(own_state[:, 128:256], wst[1, :, 0:128], 1, 1)
    h = hidden[...].astype(F32)
    r_in = lax.rsqrt(jnp.mean(h * h, axis=1, keepdims=True) + EPS)
    scaled = whole * gain[...]
    back = scaled * r_in - h * (r_in * r_in * r_in * (jnp.sum(scaled * h, axis=1, keepdims=True) / 1536))
    grad_hidden[...] = (cot[...].astype(F32) + back).astype(BF16)
    new_hidden[...] = (h + br[mine, :].astype(F32) + br_in[...].astype(F32)).astype(BF16)
    ggain = jnp.sum(whole * h * r_in, axis=0, keepdims=True)
    for q in range(6):
        vec[q * 8:(q + 1) * 8, :] = prow[q]
        vec[56 + q:57 + q, :] = ggain[:, q * 256:(q + 1) * 256]
    vec[64:72, :] = hrow[...]

    def vec_stage(s):
        axis = "xyz"[s]
        return [remote(vec, vec_in.at[s, by - 1], vec_send.at[s, by - 1], vec_recv.at[s, by - 1], moved(at, axis, by)) for by in (1, 2, 3)]

    def vec_end(s, flights):
        for c in flights:
            c.wait()
        vec[...] = vec[...] + vec_in[s, 0] + vec_in[s, 1] + vec_in[s, 2]

    flights = vec_stage(0)
    for t in range(1, n + 6):
        for chunk in range(n):
            if 1 <= t - chunk < 7:
                step(chunk, t - chunk)
        if t in (1, 2, 3):
            vec_end(t - 1, flights)
            if t < 3:
                flights = vec_stage(t)
    final = remote(vec.at[pl.ds(56, 8)], gain_in, q_send.at[3], q_recv.at[3], mate)

    own = units(at, "")
    for piece in range(3):
        quarter[piece * 16:(piece + 1) * 16, :] = part[own + (piece, slice(None), pl.ds(RCHUNKS[last][0], 128))].astype(F32)
    thirds = [remote(quarter, quarters.at[i], q_send.at[i], q_recv.at[i], to) for i, to in enumerate((mate, far, far_mate))]
    for piece in range(3):
        out[piece * 16:(piece + 1) * 16, :] = part[own + (piece, slice(None), pl.ds(0, 2304))].astype(F32)
    gsmall[...] = vec[...]
    final.wait()
    gsmall[56:64, :] = vec[56:64, :] + gain_in[...]
    for c in thirds:
        c.wait()
    me_low = at["core"] == 0
    q0, q1, q2, q3 = quarter[...], quarters[0], quarters[1], quarters[2]
    here = jnp.where(me_low, jnp.concatenate([q0[:, :64], q1[:, :64]], axis=1), jnp.concatenate([q1[:, :64], q0[:, :64]], axis=1))
    there = jnp.where(me_low, jnp.concatenate([q2[:, :64], q3[:, :64]], axis=1), jnp.concatenate([q3[:, :64], q2[:, :64]], axis=1))
    first = at["z"] < 2
    gstate[:, 0:128] = jnp.where(first, here, there)
    gstate[:, 128:256] = jnp.where(first, there, here)
    gstate[:, 256:384] = q0
    for c in started:
        c.wait_send()
    for s in swaps:
        s.wait_send()


def reduce(grads, *rest):
    n = len(RCHUNKS)
    vm = pl.BlockSpec(memory_space=pltpu.VMEM)
    shapes = [(stage, piece, RCHUNKS[chunk][1]) for chunk in range(n) for piece in range(3) for stage in range(3)]
    regions = [pltpu.VMEM(region_shape(*s), BF16) for s in shapes]
    halves = [pltpu.VMEM(half_shape(*s), BF16) for s in shapes]
    dma = pltpu.SemaphoreType.DMA
    return pl.pallas_call(
        reduce_kernel,
        in_specs=[pl.BlockSpec(memory_space=pl.ANY)] + [vm] * len(rest),
        out_specs=[vm] * 5,
        out_shape=[sds((48, 2304)), sds((48, 384)), sds((SUMS, 256)), sds((256, 1536), BF16), sds((256, 1536), BF16)],
        scratch_shapes=[pltpu.VMEM((2, 4, 4, 2, 3, 16, RCOLS), BF16)] + regions + regions + halves + halves + [
            pltpu.VMEM((256, T), BF16), pltpu.VMEM((256, 1536), BF16), pltpu.VMEM((256, 1536), BF16), pltpu.VMEM((256, T), BF16),
            pltpu.VMEM((2, 128, T), BF16), pltpu.VMEM((256, 128), F32), pltpu.VMEM((SUMS, 256), F32), pltpu.VMEM((3, 3, SUMS, 256), F32),
            pltpu.VMEM((8, 256), F32), pltpu.VMEM((48, 128), F32), pltpu.VMEM((3, 48, 128), F32),
            dma((n, 3, 3, 6)), dma((n, 3, 3, 6)), dma((n,)), dma((3,)), dma((3,)), dma((3, 3)), dma((3, 3)), dma((4,)), dma((4,))],
        compiler_params=pltpu.CompilerParams(collective_id=2, has_side_effects=True, vmem_limit_bytes=60 << 20),
    )(grads.reshape(2, 4, 4, 2, 3, 16, 2304), *rest)


def per_device(hidden, in_gain, proj_main, proj_step, proj_state, conv_inner, conv_inner_bias, conv_state, conv_state_bias,
               step_bias, decay_log, skip_gain, out_gain, proj_out, grad_out):
    z_hi = lax.axis_index("tensor") // 2
    h = hidden.astype(F32)
    normed = (h * lax.rsqrt(jnp.mean(h * h, axis=1, keepdims=True) + EPS) * in_gain).astype(BF16)
    pieces = [lax.dynamic_slice(proj_state, (0, z_hi * 128), (48, 128)), proj_step, jnp.zeros((48, 116), BF16)]
    for c in range(3):
        s = slice(c * 256, (c + 1) * 256)
        pieces += [proj_main[:, 0, s], proj_main[:, 1, s], proj_out[:, s]]
    shard = jnp.concatenate(pieces, axis=1).reshape(3, 16, COLS)
    wide = lambda v: jnp.pad(v, (0, 768 - v.shape[0]))[None]
    params = jnp.concatenate([conv_inner, conv_inner_bias[None], out_gain[None], wide(step_bias), wide(decay_log), wide(skip_gain),
                              jnp.zeros((7, 768), F32)], axis=0)
    spar = jnp.concatenate([conv_state.T, conv_state_bias[:, None], jnp.zeros((256, 3), F32)], axis=1)
    full, x, g, prm = gather(shard, normed, grad_out, params)
    w = full.reshape(2, 1536, COLS)
    xt, gt, zt, ut, dgt, yt, sums, dtt, cumt, cumc, stept, statet, bc, bct, cbt = forward(x, g, w, prm, spar)
    sums = swap(sums)
    grads, prow, hrow, dn, br, dbct, dstept = backward(w, prm, xt, gt, zt, ut, dgt, yt, sums, dtt, cumt, cumc, stept, bc, bct, cbt)
    out, gstate, small, new_hidden, grad_hidden = reduce(grads, xt, w[:, :, :256], statet, spar, dbct, dstept, dn, br, hidden, grad_out,
                                                         in_gain[None], prow, hrow)
    out = out.reshape(48, 3, 3, 256)
    grad_main = jnp.moveaxis(out[:, :, :2], 2, 1).reshape(48, 2, 768)
    own = lax.dynamic_slice(small, (z_hi * 24, 0), (24, 256)).reshape(3, 8, 256)
    inner = jnp.moveaxis(own, 1, 0).reshape(8, 768)
    heads = lax.dynamic_slice(small, (64, z_hi * 128), (8, 12))
    return (new_hidden, grad_hidden, small[56:62].reshape(1536), grad_main, gstate[:, 320:332], gstate[:, :256], inner[:4], inner[4],
            small[48:52], small[52], heads[0], heads[1], heads[2], inner[5], out[:, :, 2].reshape(48, 768))


def solution(mesh):
    rows = P(("dp", "tensor"), None)
    per_head = P("tensor")
    in_specs = (rows, P(), P("dp", None, "tensor"), P("dp", "tensor"), P("dp", None), P(None, "tensor"), per_head, P(), P(),
                per_head, per_head, per_head, per_head, P("dp", "tensor"), rows)
    out_specs = (rows, rows, P(), P("dp", None, "tensor"), P("dp", "tensor"), P("dp", None), P(None, "tensor"), per_head, P(), P(),
                 per_head, per_head, per_head, per_head, P("dp", "tensor"))
    return jax.shard_map(per_device, mesh=mesh, in_specs=in_specs, out_specs=out_specs, check_vma=False)
```

```python
import functools

import jax
import jax.numpy as jnp
from jax import lax
from jax.experimental import pallas as pl
from jax.experimental.pallas import tpu as pltpu
from jax.sharding import PartitionSpec as P

MESH = pl.DeviceIdType.MESH
F32, BF16 = jnp.float32, jnp.bfloat16
EPS = 1e-5
T, SPAN, HEAD, GROUP = 512, 256, 64, 4
WIDE = GROUP * HEAD
INNER = 3072
COLS = 2560
STAGED = ((0, 256), (256, 768), (1024, 768), (1792, 768))
ORDERS = ("xyz", "yzx", "zxy")
RCHUNKS = ((0, 768), (768, 768), (1536, 256), (1792, 256), (2048, 256), (2304, 128))
RCOLS = 2432
SUMS = 72


def sds(shape, dtype=F32):
    return jax.ShapeDtypeStruct(shape, dtype)


def place():
    dp, tp = lax.axis_index("dp"), lax.axis_index("tensor")
    return dict(x=dp // 8, y=(dp // 2) % 4, z=(tp // 2) * 2 + dp % 2, core=tp % 2)


def device_at(at):
    return ((at["x"] * 4 + at["y"]) * 2 + at["z"] % 2, (at["z"] // 2) * 2 + at["core"])


def moved(at, axis, by):
    return {**at, axis: (at[axis] + by) % 4}


def units(at, whole):
    return (slice(None) if "z" in whole else at["z"] // 2, slice(None) if "x" in whole else at["x"],
            slice(None) if "y" in whole else at["y"], slice(None) if "z" in whole else at["z"] % 2)


def greet(others):
    barrier = pltpu.get_barrier_semaphore()
    for other in others:
        pl.semaphore_signal(barrier, inc=1, device_id=device_at(other), device_id_type=MESH)
    return lambda: pl.semaphore_wait(barrier, len(others))


def half_of(ref, stage, piece, width, half):
    if stage == 0:
        return ref.at[pl.ds(2 * half, 2)] if piece == 0 else ref.at[:, pl.ds(2 * half, 2)]
    if stage == 1:
        return ref.at[pl.ds(2 * half, 2)] if piece < 2 else ref.at[half]
    return ref.at[:, pl.ds(half * (width // 2), width // 2)] if width > 128 else ref


def half_shape(stage, piece, width):
    if stage == 0:
        return (2, 4, 16, width) if piece == 0 else (2, 2, 2, 16, width)
    if stage == 1:
        return (2, 16, width)
    return (16, width // 2) if width > 128 else (16, width)


def region_shape(stage, piece, width):
    whole = ORDERS[piece][:2 - stage]
    dims = ([2] if "z" in whole else []) + ([4] if "x" in whole else []) + ([4] if "y" in whole else []) + ([2] if "z" in whole else [])
    return tuple(dims) + (16, width)


def dot(a, b, ca=1, cb=0):
    return lax.dot_general(a, b, (((ca,), (cb,)), ((), ())), preferred_element_type=F32)


def lanes(rows, width=T):
    return lax.broadcasted_iota(jnp.int32, (rows, width), 1)


def later(u, k):
    return jnp.where(lanes(u.shape[0]) >= k, pltpu.roll(u, k, 1), 0.0) if k else u


def sooner(u, k):
    return jnp.where(lanes(u.shape[0]) < T - k, pltpu.roll(u, T - k, 1), 0.0) if k else u


def sig(v):
    return 1.0 / (1.0 + jnp.exp(-v))


def split(v):
    a = v.astype(BF16)
    r = v - a.astype(F32)
    b = r.astype(BF16)
    return a, b, (r - b.astype(F32)).astype(BF16)


def exact_dot(v, ones):
    n = v.shape[0]
    s = dot(jnp.concatenate(split(v), axis=0), ones)
    return s[:n] + s[n:2 * n] + s[2 * n:]


def tri(n, keep):
    r = lax.broadcasted_iota(jnp.int32, (n, n), 0)
    c = lax.broadcasted_iota(jnp.int32, (n, n), 1)
    return jnp.where(keep(r, c), 1.0, 0.0).astype(BF16)


def conv(u, cols):
    shifted = [later(u, k) for k in range(4)]
    p = cols[:, 4:5] + cols[:, 0:1] * shifted[0]
    for k in range(1, 4):
        p = p + cols[:, k:k + 1] * shifted[k]
    return p, shifted


def conv_back(dp, cols):
    du = cols[:, 0:1] * dp
    for k in range(1, 4):
        du = du + cols[:, k:k + 1] * sooner(dp, k)
    return du


def decay(cum_row, cum_col, b):
    return jnp.exp(jnp.minimum(cum_row[:, b * SPAN:(b + 1) * SPAN] - cum_col, 0.0))


def group_at(n):
    zh, c = n % 2, n // 2
    return zh, c, pl.multiple_of((zh * 3 + c) * WIDE, WIDE), zh * 16 + c * GROUP


def group_cols(prm, zh, c):
    return prm[zh, :, pl.ds(pl.multiple_of(c * WIDE, WIDE), WIDE)].T


def group_skip(prm, zh, c):
    cols = prm[zh, :, 0:128].T
    return pltpu.roll(jnp.broadcast_to(cols[:, 8:9], (128, 128)), 128 - c * GROUP, 0)


def forward_kernel(main, step_w, state_w, out_w, hidden, cot, vecs, cinner, cstate,
                   xt_o, gt_o, zt_o, ut_o, dgt_o, vt_o, xst_o, yt_o, w_o, wst_o,
                   sums_o, dtt, cumt, cumc, stept, statet, bc, bct, cbt, prm_o, spar,
                   shard, w, x, g, xt, gt, zt, ut, dgt, vt, xst, yt, prm, acc, acc_in,
                   send, recv, local, w_sem, out_sem, swap_send, swap_recv):
    at = place()
    z_hi = at["z"] // 2
    mate = {**at, "core": 1 - at["core"]}
    far = moved(at, "z", 2)
    entered = greet([moved(at, axis, by) for axis in "xyz" for by in (1, 3)] + [mate, far])
    state_cols = pl.ds(pl.multiple_of(z_hi * 128, 128), 128)
    for piece in range(3):
        rows = pl.ds(piece * 16, 16)
        shard[piece, :, 0:128] = state_w[rows, state_cols]
        shard[piece, :, 128:256] = jnp.zeros((16, 128), BF16)
        shard[piece, :, 128:140] = step_w[rows, :]
        shard[piece, :, 256:1024] = main[rows, 768:1536]
        shard[piece, :, 1024:1792] = main[rows, 0:768]
        shard[piece, :, 1792:2560] = out_w[rows, :]
    entered()

    def part(where, piece, stage, chunk):
        begin, width = STAGED[chunk] if stage == 2 else (0, COLS)
        return w.at[units(where, ORDERS[piece][:stage]) + (piece, slice(None), pl.ds(begin, width))]

    def flight(piece, stage, chunk, kind):
        axis, by = ORDERS[piece][stage], (1, 3)[kind % 2]
        width = STAGED[chunk][1] if stage == 2 else COLS
        if kind < 2:
            target = part(at, piece, stage, chunk)
            source = shard.at[piece] if stage == 0 else target
        else:
            target = source = half_of(part(moved(at, axis, -by), piece, stage, chunk), 2 - stage, piece, width, kind - 2)
        sem = (stage + chunk if stage == 2 else stage, piece, kind)
        return pltpu.make_async_remote_copy(src_ref=source, dst_ref=target, send_sem=send.at[sem], recv_sem=recv.at[sem],
                                            device_id=device_at(moved(at, axis, by)), device_id_type=MESH)

    def fulls(stage, chunk=0):
        for piece in range(3):
            if stage > 0 and chunk == 0:
                for kind in (2, 3):
                    flight(piece, stage - 1, 0, kind).wait_recv()
            for kind in (0, 1):
                flight(piece, stage, chunk, kind).start()

    def halves(stage, chunk=0):
        for piece in range(3):
            for kind in (0, 1):
                flight(piece, stage, chunk, kind).wait_recv()
                flight(piece, stage, chunk, kind + 2).start()

    def arrived(chunk):
        for piece in range(3):
            for kind in (2, 3):
                flight(piece, 2, chunk, kind).wait_recv()

    fulls(0)
    own = [pltpu.make_async_copy(shard.at[piece], part(at, piece, 0, 0), local.at[piece]) for piece in range(3)]
    for c in own:
        c.start()

    prm[z_hi] = jnp.zeros((16, 768), F32)
    prm[z_hi, 0:4, :] = cinner[...]
    prm[z_hi, 4:5, :] = vecs[:, 0:768]
    prm[z_hi, 5:6, :] = vecs[:, 768:1536]
    for i in range(3):
        prm[z_hi, 6 + i:7 + i, 0:128] = vecs[:, 3328 + i * 128:3456 + i * 128]
    h = hidden[...].astype(F32)
    scale = lax.rsqrt(jnp.mean(h * h, axis=1, keepdims=True) + EPS)
    mine = pl.ds(pl.multiple_of(at["core"] * 256, 256), 256)
    x[mine, :] = (h * scale * vecs[:, 1792:3328]).astype(BF16)
    g[mine, :] = cot[...]
    swaps = [pltpu.make_async_remote_copy(src_ref=s, dst_ref=s, send_sem=swap_send.at[i], recv_sem=swap_recv.at[i],
                                          device_id=device_at(to), device_id_type=MESH)
             for i, (s, to) in enumerate([(x.at[mine], mate), (g.at[mine], mate), (prm.at[z_hi], far)])]
    for c in swaps:
        c.start()
    spar[...] = jnp.concatenate([cstate[...], vecs[:, 1536:1792], jnp.zeros((11, 256), F32)], axis=0).T

    halves(0)
    for c in own:
        c.wait()
    fulls(1)
    out_copies = []

    def put(i, source, target):
        c = pltpu.make_async_copy(source, target, out_sem.at[i])
        c.start()
        out_copies.append(c)

    for c in swaps[:2]:
        c.wait_recv()
    xt[...] = x[...].T
    gt[...] = g[...].T
    put(0, xt, xt_o)
    put(1, gt, gt_o)
    halves(1)
    swaps[2].wait_recv()
    prm_o[...] = prm[...]
    acc[...] = jnp.zeros_like(acc)
    cumc[...] = jnp.zeros_like(cumc)
    fulls(2, 0)
    fulls(2, 1)
    halves(2, 0)
    halves(2, 1)
    fulls(2, 2)
    arrived(0)
    put(2, w.at[:, :, :, :, :, :, pl.ds(0, 256)], wst_o)

    def weight(zh, begin):
        return w[zh, :, :, :, :, :, pl.ds(begin, WIDE)].reshape(1536, WIDE)

    for zh in range(2):
        raw = dot(x[...], weight(zh, 0)).T.astype(BF16)
        statet[zh * 128:(zh + 1) * 128, :] = raw[:128]
        stept[zh * 16:(zh + 1) * 16, :] = raw[128:144]
    for q in range(4):
        r = slice(q * 64, (q + 1) * 64)
        p, _ = conv(statet[r, :].astype(F32), spar[r])
        bct[r, :] = (p * sig(p)).astype(BF16)
    bc[...] = bct[...].T
    upper = tri(SPAN, lambda r, c: r <= c)
    for b in range(2):
        rows = pl.ds(b * SPAN, SPAN)
        cbt[b] = dot(bc[rows, 0:128], bc[rows, 128:256], 1, 1) * upper.astype(F32)
    for zh in range(2):
        cols = prm[zh, :, 0:128].T
        v = stept[zh * 16:(zh + 1) * 16, :].astype(F32) + cols[:16, 6:7]
        dt = jnp.maximum(v, 0.0) + jnp.log1p(jnp.exp(-jnp.abs(v)))
        dtt[zh * 16:(zh + 1) * 16, :] = dt
        la = dt * -jnp.exp(cols[:16, 7:8])
        for b in range(2):
            cumt[zh * 16:(zh + 1) * 16, b * SPAN:(b + 1) * SPAN] = exact_dot(la[:, b * SPAN:(b + 1) * SPAN], upper)
    cumc[...] = jnp.concatenate([cumt[...], jnp.zeros((96, T), F32)], axis=0).T

    def put_weights(kind, begin):
        for n in range(6):
            zh, c = n % 2, n // 2
            pltpu.make_async_copy(w.at[zh, :, :, :, :, :, pl.ds(begin + c * WIDE, WIDE)], w_o.at[kind, zh, c], w_sem.at[kind * 6 + n]).start()

    arrived(1)
    put_weights(2, 256)

    @pl.loop(0, 6)
    def _(n):
        zh, c, off, base = group_at(n)
        cols = group_cols(prm, zh, c)
        skip = group_skip(prm, zh, c)
        cc = pltpu.roll(cumc[...], 128 - base, 1)
        ut[pl.ds(off, WIDE), :] = dot(x[...], weight(zh, pl.multiple_of(256 + c * WIDE, WIDE))).T.astype(BF16)
        for i in range(GROUP):
            r = slice(i * HEAD, (i + 1) * HEAD)
            rows = pl.ds(pl.multiple_of(off + i * HEAD, HEAD), HEAD)
            p, _ = conv(ut[rows, :].astype(F32), cols[r])
            xsb = (p * sig(p)).astype(BF16)
            xst[rows, :] = xsb
            xs = xsb.astype(F32)
            cum = cumt[pl.ds(base + i, 1), :]
            xdt = xs * dtt[pl.ds(base + i, 1), :]
            xdtb = xdt.astype(BF16)
            ys = []
            for b in range(2):
                m = (decay(cum, cc[b * SPAN:(b + 1) * SPAN, i:i + 1], b) * cbt[b]).astype(BF16)
                ys.append(dot(xdtb[:, b * SPAN:(b + 1) * SPAN], m))
            tail = jnp.exp(cum[:, SPAN - 1:SPAN] - cum[:, :SPAN])
            state = dot((xdt[:, :SPAN] * tail).astype(BF16), bc[0:SPAN, 0:128]).astype(BF16)
            ys[1] = ys[1] + jnp.exp(cum[:, SPAN:]) * dot(state, bc[SPAN:, 128:256], 1, 1)
            yt[rows, :] = jnp.concatenate(ys, axis=1) + skip[i:i + 1, 0:1] * xs

        @pl.when(n == 2)
        def _():
            halves(2, 2)
            fulls(2, 3)

    put(3, xst, xst_o)
    put(4, yt, yt_o)
    put(5, ut, ut_o)
    arrived(2)
    put_weights(1, 1024)

    @pl.loop(0, 6)
    def _(n):
        zh, c, off, _ = group_at(n)
        zt[pl.ds(off, WIDE), :] = dot(x[...], weight(zh, pl.multiple_of(1024 + c * WIDE, WIDE))).T.astype(BF16)
        for i in range(GROUP):
            rows = pl.ds(pl.multiple_of(off + i * HEAD, HEAD), HEAD)
            z = zt[rows, :].astype(F32)
            vb = (yt[rows, :] * (z * sig(z))).astype(BF16)
            vt[rows, :] = vb
            v = vb.astype(F32)
            acc[0:1, :] += jnp.sum(v * v, axis=0, keepdims=True)

        @pl.when(n == 3)
        def _():
            halves(2, 3)

    put(6, zt, zt_o)
    put(7, vt, vt_o)
    arrived(3)
    put_weights(0, 1792)

    @pl.loop(0, 6)
    def _(n):
        zh, c, off, _ = group_at(n)
        cols = group_cols(prm, zh, c)
        dgt[pl.ds(off, WIDE), :] = dot(g[...], weight(zh, pl.multiple_of(1792 + c * WIDE, WIDE))).T.astype(BF16)
        for i in range(GROUP):
            rows = pl.ds(pl.multiple_of(off + i * HEAD, HEAD), HEAD)
            s = dgt[rows, :].astype(F32) * cols[i * HEAD:(i + 1) * HEAD, 5:6] * vt[rows, :].astype(F32)
            acc[1:2, :] += jnp.sum(s, axis=0, keepdims=True)

    c = pltpu.make_async_remote_copy(src_ref=acc, dst_ref=acc_in, send_sem=swap_send.at[3], recv_sem=swap_recv.at[3],
                                     device_id=device_at(mate), device_id_type=MESH)
    c.start()
    put(8, dgt, dgt_o)
    for piece in range(3):
        for kind in range(4):
            for stage in range(2):
                flight(piece, stage, 0, kind).wait_send()
            for chunk in range(4):
                flight(piece, 2, chunk, kind).wait_send()
    for s in swaps:
        s.wait_send()
    c.wait()
    sums_o[...] = acc[...] + acc_in[...]
    for kind in range(3):
        for n in range(6):
            pltpu.make_async_copy(w.at[0, :, :, :, :, :, pl.ds(0, WIDE)], w_o.at[kind, n % 2, n // 2], w_sem.at[kind * 6 + n]).wait()
    for c in out_copies:
        c.wait()


def forward(main, step_w, state_w, out_w, hidden, cot, vecs, cinner, cstate):
    vm = pl.BlockSpec(memory_space=pltpu.VMEM)
    any_ = pl.BlockSpec(memory_space=pl.ANY)
    dma = pltpu.SemaphoreType.DMA
    tall = [sds((1536, T), BF16)] * 7 + [sds((1536, T))]
    big = tall + [sds((3, 2, 3, 4, 4, 2, 3, 16, WIDE), BF16), sds((2, 4, 4, 2, 3, 16, 256), BF16)]
    small = [sds((8, T)), sds((32, T)), sds((32, T)), sds((T, 128)), sds((32, T), BF16), sds((256, T), BF16), sds((T, 256), BF16),
             sds((256, T), BF16), sds((2, SPAN, SPAN)), sds((2, 16, 768)), sds((256, 16))]
    return pl.pallas_call(
        forward_kernel, out_shape=big + small, in_specs=[vm] * 9, out_specs=[any_] * 10 + [vm] * 11,
        scratch_shapes=[pltpu.VMEM((3, 16, COLS), BF16), pltpu.VMEM((2, 4, 4, 2, 3, 16, COLS), BF16), pltpu.VMEM((T, 1536), BF16),
                        pltpu.VMEM((T, 1536), BF16)] + [pltpu.VMEM(s.shape, s.dtype) for s in tall] + [
            pltpu.VMEM((2, 16, 768), F32), pltpu.VMEM((8, T), F32), pltpu.VMEM((8, T), F32),
            dma((6, 3, 4)), dma((6, 3, 4)), dma((3,)), dma((18,)), dma((9,)), dma((4,)), dma((4,))],
        compiler_params=pltpu.CompilerParams(collective_id=0, has_side_effects=True, vmem_limit_bytes=60 << 20),
    )(main, step_w, state_w, out_w, hidden, cot, vecs, cinner, cstate)


GATE_STEPS = {2: [(0, 1)]}
SCAN_STEPS = {0: [(0, 2)], 2: [(0, 3)], 3: [(1, 1)], 4: [(0, 4)], 6: [(1, 2)], 7: [(0, 5)], 8: [(1, 3)], 9: [(0, 6)], 10: [(1, 4)], 11: [(1, 5)]}
CONV_STEPS = {1: [(2, 0)], 2: [(1, 6), (2, 1)], 3: [(3, 0), (2, 2), (5, 1)], 4: [(5, 2), (2, 3), (3, 1)], 5: [(4, 0), (5, 3), (2, 4), (3, 2)]}
REST = [(5, 4), (2, 5), (3, 3), (4, 1), (5, 5), (2, 6), (3, 4), (4, 2), (5, 6), (3, 5), (4, 3), (3, 6), (4, 4), (4, 5), (4, 6)]


def add_into(target, *others):
    def add(t, o):
        v = t[...].astype(F32)
        for other in o:
            v = v + other[...].astype(F32)
        t[...] = v.astype(BF16)
    if len(target.shape) == 2:
        add(target, others)
    else:
        @pl.loop(0, target.shape[0])
        def _(i):
            add(target.at[i], [o.at[i] for o in others])


def backward_kernel(xt_h, gt_h, zt_h, ut_h, dgt_h, vt_h, xst_h, yt_h, w_h, wst_h,
                    sums, dtt, cumt, cumc, stept, statet, bc, bct, cbt, prm, spar, hidden, cot, gain,
                    out, gstate, gsmall, new_hidden, grad_hidden, *scratch):
    n = len(RCHUNKS)
    part, lefts, rights, left_halves, right_halves = scratch[0], *[scratch[1 + 9 * n * q: 1 + 9 * n * (q + 1)] for q in range(4)]
    (xt, gt, zt, dgt, vt, yt, wbuf, wst, total, dcbt, lt, ld, dye_all, xe_all, st_all, ds_all, cross, pcols, prow, hrow,
     dcum, ddt1, gskip, dstep_t, dbct, dbct_in, dn_out, dn_in, br_out, br_in, br_own, dstate, dst, vec, vec_in, own_state, ggain, gain_in, quarter, quarters,
     send, recv, load_sem, w_sem, swap_send, swap_recv, vec_send, vec_recv, q_send, q_recv) = scratch[1 + 36 * n:]
    xst, ut, dyt = gt, vt, zt
    at = place()
    mate = {**at, "core": 1 - at["core"]}
    far = moved(at, "z", 2)
    far_mate = {**far, "core": 1 - at["core"]}
    entered = greet([moved(at, axis, by) for axis in "xyz" for by in (1, 2, 3)] + [mate, far_mate])
    mine = pl.ds(pl.multiple_of(at["core"] * 256, 256), 256)
    theirs = pl.ds(pl.multiple_of((1 - at["core"]) * 256, 256), 256)

    loads = [pltpu.make_async_copy(s, d, load_sem.at[i]) for i, (s, d) in enumerate(
        [(vt_h, vt), (gt_h, gt), (yt_h, yt), (zt_h, zt), (dgt_h, dgt), (xt_h, xt), (xst_h, xst), (ut_h, ut), (wst_h, wst)])]

    def weights(i):
        return pltpu.make_async_copy(w_h.at[i // 6, (i % 6) % 2, (i % 6) // 2], wbuf.at[i % 2], w_sem.at[i % 2])

    def next_weights(i):
        weights(i).wait()

        @pl.when(i + 1 < 18)
        def _():
            weights(i + 1).start()
        return wbuf[i % 2].reshape(1536, WIDE)

    for c in loads[:2]:
        c.start()
    weights(0).start()
    for c in loads[2:6] + loads[8:]:
        c.start()

    def remote(src, dst_ref, s, r, to):
        return pltpu.make_async_remote_copy(src_ref=src, dst_ref=dst_ref, send_sem=s, recv_sem=r, device_id=device_at(to), device_id_type=MESH)

    def block(where, chunk, piece, stage):
        begin, width = RCHUNKS[chunk]
        return part.at[units(where, ORDERS[piece][:2 - stage]) + (piece, slice(None), pl.ds(begin, width))]

    def whole(chunk, stage):
        return stage == 2 and RCHUNKS[chunk][1] <= 128

    def flight(chunk, piece, stage, i):
        axis = ORDERS[piece][2 - stage]
        k = (chunk * 3 + piece) * 3 + stage
        right, left, opposite = moved(at, axis, 1), moved(at, axis, 3), moved(at, axis, 2)
        cut = lambda ref, h: half_of(ref, stage, piece, RCHUNKS[chunk][1], h)
        own = lambda where: block(where, chunk, piece, stage)
        if i == 0:
            src, dst_ref, to = cut(own(opposite), 0), left_halves[k], right
        elif i == 1:
            src, dst_ref, to = cut(own(opposite), 1), right_halves[k], left
        elif i == 2:
            src, dst_ref, to = cut(own(right), 1), cut(lefts[k], 1), right
        elif i == 3:
            src, dst_ref, to = cut(own(left), 0), cut(rights[k], 0), left
        elif i == 4:
            src, dst_ref, to = cut(own(right), 0), cut(lefts[k], 0), right
        else:
            src, dst_ref, to = cut(own(left), 1), cut(rights[k], 1), left
        return remote(src, dst_ref, send.at[chunk, piece, stage, i], recv.at[chunk, piece, stage, i], to)

    def kinds(chunk, stage):
        return ((0,), (3,), (4,)) if whole(chunk, stage) else ((0, 1), (2, 3), (4, 5))

    def step(chunk, k):
        for piece in range(3):
            stage = k // 2
            if k % 2:
                first, _, last = kinds(chunk, stage)
                for i, j in zip(first, last):
                    flight(chunk, piece, stage, i).wait_recv()
                    axis = ORDERS[piece][2 - stage]
                    mid = half_of(block(moved(at, axis, 1 if j == 4 else 3), chunk, piece, stage), stage, piece, RCHUNKS[chunk][1], j - 4)
                    add_into(mid, (left_halves if j == 4 else right_halves)[(chunk * 3 + piece) * 3 + stage])
                    flight(chunk, piece, stage, j).start()
            else:
                if k > 0:
                    _, second, last = kinds(chunk, stage - 1)
                    for i in second + last:
                        flight(chunk, piece, stage - 1, i).wait_recv()
                    s = (chunk * 3 + piece) * 3 + stage - 1
                    add_into(block(at, chunk, piece, stage - 1), lefts[s], rights[s])
                if k < 6:
                    first, second, _ = kinds(chunk, stage)
                    for i in first + second:
                        flight(chunk, piece, stage, i).start()

    def steps_after(table, index):
        for i, todo in table.items():
            @pl.when(index == i)
            def _(todo=todo):
                for chunk, k in todo:
                    step(chunk, k)

    def gradients(left, right, zh, col):
        for q in range(4):
            value = dot(left[q * 384:(q + 1) * 384, :], right, 1, 1).astype(BF16)
            part[zh, q, :, :, :, :, pl.ds(col, right.shape[0])] = value.reshape(4, 2, 3, 16, right.shape[0])

    def add_total(weight, values):
        for q in range(4):
            r = slice(q * 384, (q + 1) * 384)
            total[r, :] += dot(weight[r], values)

    r_out = lax.rsqrt(sums[0:1, :] / INNER + EPS)
    k2 = r_out * r_out * r_out * sums[1:2, :] / INNER
    for ref in (total, dcbt, cross, dcum, ddt1, gskip, vec, ggain):
        ref[...] = jnp.zeros_like(ref)

    for c in loads[:2]:
        c.wait()

    @pl.loop(0, 6)
    def _(m):
        zh, c, off, _ = group_at(m)
        cols = group_cols(prm, zh, c)
        for i in range(GROUP):
            r = slice(i * HEAD, (i + 1) * HEAD)
            rows = pl.ds(pl.multiple_of(off + i * HEAD, HEAD), HEAD)
            lt[r, :] = (vt[rows, :].astype(F32) * r_out * cols[r, 5:6]).astype(BF16)
        gradients(gt, lt[...], zh, pl.multiple_of(c * WIDE, WIDE))
        add_total(next_weights(m), lt[...])

    loads[6].start()
    entered()
    step(0, 0)

    def rows_of(half, q):
        return total[:, pl.ds(pl.multiple_of(half * 256 + q * 128, 128), 128)].T

    for q in range(2):
        br_out[q * 128:(q + 1) * 128, :] = rows_of(1 - at["core"], q).astype(BF16)
    swap_br = remote(br_out, br_in, swap_send.at[0], swap_recv.at[0], mate)
    swap_br.start()
    for q in range(2):
        br_own[q * 128:(q + 1) * 128, :] = rows_of(at["core"], q).astype(BF16)
    total[...] = jnp.zeros_like(total)
    for c in loads[2:6]:
        c.wait()

    @pl.loop(0, 6)
    def _(m):
        zh, c, off, _ = group_at(m)
        cols = group_cols(prm, zh, c)
        for i in range(GROUP):
            r = slice(i * HEAD, (i + 1) * HEAD)
            rows = pl.ds(pl.multiple_of(off + i * HEAD, HEAD), HEAD)
            z = zt[rows, :].astype(F32)
            dg = dgt[rows, :].astype(F32)
            v = vt[rows, :].astype(F32)
            sz = sig(z)
            zs = z * sz
            dv = dg * cols[r, 5:6] * r_out - v * k2
            pcols[r, 5:6] = jnp.sum(dg * v * r_out, axis=1, keepdims=True)
            dyt[rows, :] = (dv * zs).astype(BF16)
            lt[r, :] = (dv * yt[rows, :] * (sz + zs * (1.0 - sz))).astype(BF16)
        prow[zh * 3 + c, :, :] = pcols[...].T[:8]
        gradients(xt, lt[...], zh, pl.multiple_of(768 + c * WIDE, WIDE))
        add_total(next_weights(6 + m), lt[...])
        steps_after(GATE_STEPS, m)

    loads[7].start()
    step(1, 0)
    loads[6].wait()

    @pl.loop(0, 6)
    def _(m):
        zh, c, off, base = group_at(m)
        cc = pltpu.roll(cumc[...], 128 - base, 1)
        skips = group_skip(prm, zh, c)
        for i in range(GROUP):
            r = slice(i * HEAD, (i + 1) * HEAD)
            rows = pl.ds(pl.multiple_of(off + i * HEAD, HEAD), HEAD)
            skip = skips[i:i + 1, 0:1]
            xs = xst[rows, :].astype(F32)
            dyb = dyt[rows, :]
            dy = dyb.astype(F32)
            yssm = yt[rows, :] - skip * xs
            gskip[pl.ds(base + i, 1), :] = jnp.sum(dy * xs, axis=0, keepdims=True)
            dt = dtt[pl.ds(base + i, 1), :]
            cum = cumt[pl.ds(base + i, 1), :]
            xdt = xs * dt
            xdtb = xdt.astype(BF16)
            dxs = []
            for b in range(2):
                s = slice(b * SPAN, (b + 1) * SPAN)
                w = decay(cum, cc[s, i:i + 1], b)
                dxs.append(dot(dyb[:, s], (w * cbt[b]).astype(BF16), 1, 1))
                dcbt[b] += dot(xdtb[:, s], dyb[:, s], 0, 0) * w
            tail = jnp.exp(cum[:, SPAN - 1:SPAN] - cum[:, :SPAN])
            xe = (xdt[:, :SPAN] * tail).astype(BF16)
            dye = (dy[:, SPAN:] * jnp.exp(cum[:, SPAN:])).astype(BF16)
            ds = dot(dye, bc[SPAN:, 128:256]).astype(BF16)
            xe_all[r, :] = xe
            dye_all[r, :] = dye
            st_all[r, :] = dot(xe, bc[0:SPAN, 0:128]).astype(BF16)
            ds_all[r, :] = ds
            dxs[0] = dxs[0] + tail * dot(ds, bc[0:SPAN, 0:128], 1, 1)
            dx = jnp.concatenate(dxs, axis=1)
            dcum[pl.ds(base + i, 1), :] = jnp.sum(dy * yssm - xdtb.astype(F32) * dx, axis=0, keepdims=True)
            ddt1[pl.ds(base + i, 1), :] = jnp.sum(xs * dx, axis=0, keepdims=True)
            dyt[rows, :] = (dt * dx + skip * dy).astype(BF16)
            if i % 2:
                steps_after(SCAN_STEPS, m * 2 + i // 2)
        cross[1] += dot(st_all[...], dye_all[...], 0, 0)
        cross[0] += dot(ds_all[...], xe_all[...], 0, 0)

    upper = tri(SPAN, lambda r, c: r <= c).astype(F32)
    for b in range(2):
        s = slice(b * SPAN, (b + 1) * SPAN)
        d = (dcbt[b] * upper).astype(BF16)
        db = dot(bct[128:256, s], d, 1, 1)
        dc = dot(bct[0:128, s], d)
        dbct[0:128, s] = (db + cross[0] if b == 0 else db).astype(BF16)
        dbct[128:256, s] = (dc + cross[1] if b == 1 else dc).astype(BF16)
    swap_bc = remote(dbct, dbct_in, swap_send.at[1], swap_recv.at[1], mate)
    swap_bc.start()

    loads[8].wait()
    dla = exact_dot(dcum[...], tri(T, lambda r, c: r >= c))
    for zh in range(2):
        rows = slice(zh * 16, (zh + 1) * 16)
        hc = prm[zh, :, 0:128].T
        rate = -jnp.exp(hc[:16, 7:8])
        d = dla[rows]
        dstep = (ddt1[rows, :] + rate * d) * sig(stept[rows, :].astype(F32) + hc[:16, 6:7])
        gd = jnp.sum(d * dtt[rows, :] * rate, axis=1, keepdims=True)
        hcol = jnp.concatenate([jnp.sum(dstep, axis=1, keepdims=True), gd, jnp.sum(gskip[rows, :], axis=1, keepdims=True),
                                jnp.zeros((16, 125), F32)], axis=1)
        hrow[:, zh * 128:(zh + 1) * 128] = jnp.concatenate([hcol, jnp.zeros((112, 128), F32)], axis=0).T[:8]
        keep = lax.broadcasted_iota(jnp.int32, (16, T), 0) < 12
        dstep_t[zh, 0:16, :] = jnp.where(keep, dstep, 0.0).astype(BF16)
        dstep_t[zh, 16:128, :] = jnp.zeros((112, T), BF16)
        for q in range(4):
            total[q * 384:(q + 1) * 384, :] += dot(wst[zh, q, :, :, :, :, pl.ds(128, 128)].reshape(384, 128), dstep_t[zh])

    loads[7].wait()

    def convolution(m):
        zh, c, off, _ = group_at(m)
        cols = group_cols(prm, zh, c)
        for i in range(GROUP):
            r = slice(i * HEAD, (i + 1) * HEAD)
            rows = pl.ds(pl.multiple_of(off + i * HEAD, HEAD), HEAD)
            p, shifted = conv(ut[rows, :].astype(F32), cols[r])
            sp = sig(p)
            dp = dyt[rows, :].astype(F32) * (sp + p * sp * (1.0 - sp))
            pcols[r, 0:5] = jnp.concatenate([jnp.sum(dp * shifted[k], axis=1, keepdims=True) for k in range(4)]
                                            + [jnp.sum(dp, axis=1, keepdims=True)], axis=1)
            lt[r, :] = conv_back(dp, cols[r]).astype(BF16)
        prow[zh * 3 + c, 0:5, :] = pcols[...].T[:5]
        gradients(xt, lt[...], zh, pl.multiple_of(1536 + c * WIDE, WIDE))
        add_total(next_weights(12 + m), lt[...])

    def state_back():
        swap_bc.wait_recv()
        for q in range(4):
            r = slice(q * 64, (q + 1) * 64)
            cols = spar[r]
            p, shifted = conv(statet[r, :].astype(F32), cols)
            sp = sig(p)
            dp = (dbct[r, :].astype(F32) + dbct_in[r, :].astype(F32)) * (sp + p * sp * (1.0 - sp))
            dstate[r, :] = conv_back(dp, cols).astype(BF16)
            dst[r, :] = jnp.concatenate([jnp.sum(dp * shifted[k], axis=1, keepdims=True) for k in range(4)]
                                        + [jnp.sum(dp, axis=1, keepdims=True), jnp.zeros((64, 123), F32)], axis=1)
        vec[48:56, :] = dst[...].T[:8]
        for zh in range(2):
            ld[0:64, :] = dstate[pl.ds(zh * 128 + pl.multiple_of(at["core"] * 64, 64), 64), :]
            ld[64:128, :] = dstep_t[zh, 0:64, :]
            gradients(xt, ld[...], zh, 2304)

    @pl.loop(0, 6)
    def _(m):
        convolution(m)

        @pl.when(m == 2)
        def _():
            state_back()
            step(5, 0)
        steps_after(CONV_STEPS, m)

    for q in range(2):
        dn_out[q * 128:(q + 1) * 128, :] = rows_of(1 - at["core"], q).astype(BF16)
    swap_dn = remote(dn_out, dn_in, swap_send.at[2], swap_recv.at[2], mate)
    swap_dn.start()
    rest = list(REST)

    def go(count):
        for _ in range(count):
            step(*rest.pop(0))

    go(3)
    own_state[...] = dstate[:, mine].T
    swap_dn.wait_recv()

    @pl.loop(0, 2)
    def _(q):
        r = pl.ds(pl.multiple_of(q * 128, 128), 128)
        full = rows_of(at["core"], q) + dn_in[r, :].astype(F32)
        for zh in range(2):
            full = full + dot(own_state[r, zh * 128:(zh + 1) * 128], wst[zh, :, :, :, :, :, pl.ds(0, 128)].reshape(1536, 128), 1, 1)
        h = hidden[r, :].astype(F32)
        r_in = lax.rsqrt(jnp.mean(h * h, axis=1, keepdims=True) + EPS)
        ggain[...] += jnp.sum(full * h * r_in, axis=0, keepdims=True)
        scaled = full * gain[...]
        back = scaled * r_in - h * (r_in * r_in * r_in * (jnp.sum(scaled * h, axis=1, keepdims=True) / 1536))
        grad_hidden[r, :] = (cot[r, :].astype(F32) + back).astype(BF16)

    for q in range(6):
        vec[q * 8:(q + 1) * 8, :] = prow[q]
        vec[56 + q:57 + q, :] = ggain[:, q * 256:(q + 1) * 256]
    vec[64:72, :] = hrow[...]

    def vec_flights(s):
        return [remote(vec, vec_in.at[s, by - 1], vec_send.at[s, by - 1], vec_recv.at[s, by - 1], moved(at, "xyz"[s], by)) for by in (1, 2, 3)]

    def vec_end(s):
        for c in vec_flights(s):
            c.wait()
        vec[...] = vec[...] + vec_in[s, 0] + vec_in[s, 1] + vec_in[s, 2]

    def vec_start(s):
        for c in vec_flights(s):
            c.start()

    vec_start(0)
    swap_br.wait_recv()

    @pl.loop(0, 2)
    def _(q):
        r = pl.ds(pl.multiple_of(q * 128, 128), 128)
        new_hidden[r, :] = (hidden[r, :].astype(F32) + br_own[r, :].astype(F32) + br_in[r, :].astype(F32)).astype(BF16)

    go(3)
    vec_end(0)
    vec_start(1)
    go(3)
    vec_end(1)
    vec_start(2)
    own = units(at, "")
    last = RCHUNKS[n - 1][0]
    for piece in range(3):
        quarter[piece * 16:(piece + 1) * 16, :] = part[own + (piece, slice(None), pl.ds(last, 128))].astype(F32)
    thirds = [remote(quarter, quarters.at[i], q_send.at[i], q_recv.at[i], to) for i, to in enumerate((mate, far, far_mate))]
    for c in thirds:
        c.start()
    go(3)
    vec_end(2)
    final = remote(vec.at[pl.ds(56, 8)], gain_in, q_send.at[3], q_recv.at[3], mate)
    final.start()
    go(len(rest))
    for piece in range(3):
        out[piece * 16:(piece + 1) * 16, :] = part[own + (piece, slice(None), pl.ds(0, 2304))].astype(F32)
    gsmall[...] = vec[...]
    final.wait()
    gsmall[56:64, :] = vec[56:64, :] + gain_in[...]
    for c in thirds:
        c.wait()
    low = at["core"] == 0
    q0, q1, q2, q3 = quarter[...], quarters[0], quarters[1], quarters[2]
    here = jnp.where(low, jnp.concatenate([q0[:, :64], q1[:, :64]], axis=1), jnp.concatenate([q1[:, :64], q0[:, :64]], axis=1))
    there = jnp.where(low, jnp.concatenate([q2[:, :64], q3[:, :64]], axis=1), jnp.concatenate([q3[:, :64], q2[:, :64]], axis=1))
    first = at["z"] < 2
    gstate[:, 0:128] = jnp.where(first, here, there)
    gstate[:, 128:256] = jnp.where(first, there, here)
    gstate[:, 256:384] = q0
    for chunk in range(n):
        for piece in range(3):
            for stage in range(3):
                for group in kinds(chunk, stage):
                    for i in group:
                        flight(chunk, piece, stage, i).wait_send()
    for s in (swap_br, swap_bc, swap_dn):
        s.wait_send()


def backward(tall, small, hidden, cot, gain):
    n = len(RCHUNKS)
    vm = pl.BlockSpec(memory_space=pltpu.VMEM)
    any_ = pl.BlockSpec(memory_space=pl.ANY)
    shapes = [(stage, piece, RCHUNKS[chunk][1]) for chunk in range(n) for piece in range(3) for stage in range(3)]
    regions = [pltpu.VMEM(region_shape(*s), BF16) for s in shapes]
    halves = [pltpu.VMEM(half_shape(*s), BF16) for s in shapes]
    dma = pltpu.SemaphoreType.DMA
    v = lambda shape, dtype=F32: pltpu.VMEM(shape, dtype)
    return pl.pallas_call(
        backward_kernel,
        in_specs=[any_] * len(tall) + [vm] * (len(small) + 3),
        out_specs=[vm] * 5,
        out_shape=[sds((48, 2304)), sds((48, 384)), sds((SUMS, 256)), sds((256, 1536), BF16), sds((256, 1536), BF16)],
        scratch_shapes=[v((2, 4, 4, 2, 3, 16, RCOLS), BF16)] + regions + regions + halves + halves + [
            v((1536, T), BF16)] + [v((1536, T), BF16)] * 4 + [v((1536, T)), v((2, 4, 4, 2, 3, 16, WIDE), BF16), v((2, 4, 4, 2, 3, 16, 256), BF16),
            v((1536, T)), v((2, SPAN, SPAN)), v((WIDE, T), BF16), v((128, T), BF16), v((WIDE, SPAN), BF16), v((WIDE, SPAN), BF16),
            v((WIDE, 128), BF16), v((WIDE, 128), BF16), v((2, 128, SPAN)), v((WIDE, 128)), v((6, 8, WIDE)), v((8, 256)),
            v((32, T)), v((32, T)), v((32, T)), v((2, 128, T), BF16), v((256, T), BF16), v((256, T), BF16),
            v((256, 1536), BF16), v((256, 1536), BF16), v((256, 1536), BF16), v((256, 1536), BF16), v((256, 1536), BF16),
            v((256, T), BF16), v((256, 128)), v((SUMS, 256)), v((3, 3, SUMS, 256)), v((256, 256), BF16), v((1, 1536)), v((8, 256)), v((48, 128)), v((3, 48, 128)),
            dma((n, 3, 3, 6)), dma((n, 3, 3, 6)), dma((9,)), dma((2,)), dma((3,)), dma((3,)), dma((3, 3)), dma((3, 3)), dma((4,)), dma((4,))],
        compiler_params=pltpu.CompilerParams(collective_id=1, has_side_effects=True, vmem_limit_bytes=63 << 20),
    )(*tall, *small, hidden, cot, gain)


def per_device(hidden, in_gain, proj_main, proj_step, proj_state, conv_inner, conv_inner_bias, conv_state, conv_state_bias,
               step_bias, decay_log, skip_gain, out_gain, proj_out, grad_out):
    z_hi = lax.axis_index("tensor") // 2
    space = jnp.zeros((116,), F32)
    vecs = jnp.concatenate([conv_inner_bias, out_gain, conv_state_bias, in_gain, step_bias, space, decay_log, space, skip_gain, space])[None]
    outs = forward(proj_main.reshape(48, 1536), proj_step, proj_state, proj_out, hidden, grad_out, vecs, conv_inner, conv_state)
    out, gstate, small, new_hidden, grad_hidden = backward(outs[:10], outs[10:], hidden, grad_out, in_gain[None])
    grad_main = jnp.stack([out[:, 768:1536], out[:, 1536:]], axis=1)
    own = lax.dynamic_slice(small, (z_hi * 24, 0), (24, 256)).reshape(3, 8, 256)
    inner = jnp.moveaxis(own, 1, 0).reshape(8, 768)
    heads = lax.dynamic_slice(small, (64, z_hi * 128), (8, 12))
    return (new_hidden, grad_hidden, small[56:62].reshape(1536), grad_main, gstate[:, 320:332], gstate[:, :256], inner[:4], inner[4],
            small[48:52], small[52], heads[0], heads[1], heads[2], inner[5], out[:, :768])


def solution(mesh):
    rows = P(("dp", "tensor"), None)
    per_head = P("tensor")
    in_specs = (rows, P(), P("dp", None, "tensor"), P("dp", "tensor"), P("dp", None), P(None, "tensor"), per_head, P(), P(),
                per_head, per_head, per_head, per_head, P("dp", "tensor"), rows)
    out_specs = (rows, rows, P(), P("dp", None, "tensor"), P("dp", "tensor"), P("dp", None), P(None, "tensor"), per_head, P(), P(),
                 per_head, per_head, per_head, per_head, P("dp", "tensor"))
    return jax.shard_map(per_device, mesh=mesh, in_specs=in_specs, out_specs=out_specs, check_vma=False)
```

```python
import functools

import jax
import jax.numpy as jnp
from jax import lax
from jax.experimental import pallas as pl
from jax.experimental.pallas import tpu as pltpu
from jax.sharding import PartitionSpec as P

MESH = pl.DeviceIdType.MESH
F32, BF16 = jnp.float32, jnp.bfloat16
EPS = 1e-5
T, SPAN, HEAD, GROUP = 512, 256, 64, 4
WIDE = GROUP * HEAD
INNER = 3072
COLS = 2560
STAGED = ((0, 256), (256, 768), (1024, 768), (1792, 768))
ORDERS = ("xyz", "yzx", "zxy")
RCHUNKS = ((0, 768), (768, 768), (1536, 512), (2048, 256), (2304, 128))
RCOLS = 2432
SUMS = 72


def sds(shape, dtype=F32):
    return jax.ShapeDtypeStruct(shape, dtype)


def place():
    dp, tp = lax.axis_index("dp"), lax.axis_index("tensor")
    return dict(x=dp // 8, y=(dp // 2) % 4, z=(tp // 2) * 2 + dp % 2, core=tp % 2)


def device_at(at):
    return ((at["x"] * 4 + at["y"]) * 2 + at["z"] % 2, (at["z"] // 2) * 2 + at["core"])


def moved(at, axis, by):
    return {**at, axis: (at[axis] + by) % 4}


def units(at, whole):
    return (slice(None) if "z" in whole else at["z"] // 2, slice(None) if "x" in whole else at["x"],
            slice(None) if "y" in whole else at["y"], slice(None) if "z" in whole else at["z"] % 2)


def greet(others):
    barrier = pltpu.get_barrier_semaphore()
    for other in others:
        pl.semaphore_signal(barrier, inc=1, device_id=device_at(other), device_id_type=MESH)
    return lambda: pl.semaphore_wait(barrier, len(others))


def half_of(ref, stage, piece, width, half):
    if stage == 0:
        return ref.at[pl.ds(2 * half, 2)] if piece == 0 else ref.at[:, pl.ds(2 * half, 2)]
    if stage == 1:
        return ref.at[pl.ds(2 * half, 2)] if piece < 2 else ref.at[half]
    return ref.at[:, pl.ds(half * (width // 2), width // 2)] if width > 128 else ref


def half_shape(stage, piece, width):
    if stage == 0:
        return (2, 4, 16, width) if piece == 0 else (2, 2, 2, 16, width)
    if stage == 1:
        return (2, 16, width)
    return (16, width // 2) if width > 128 else (16, width)


def region_shape(stage, piece, width):
    whole = ORDERS[piece][:2 - stage]
    dims = ([2] if "z" in whole else []) + ([4] if "x" in whole else []) + ([4] if "y" in whole else []) + ([2] if "z" in whole else [])
    return tuple(dims) + (16, width)


def dot(a, b, ca=1, cb=0):
    return lax.dot_general(a, b, (((ca,), (cb,)), ((), ())), preferred_element_type=F32)


def lanes(rows, width=T):
    return lax.broadcasted_iota(jnp.int32, (rows, width), 1)


def later(u, k):
    return jnp.where(lanes(u.shape[0]) >= k, pltpu.roll(u, k, 1), 0.0) if k else u


def sooner(u, k):
    return jnp.where(lanes(u.shape[0]) < T - k, pltpu.roll(u, T - k, 1), 0.0) if k else u


def sig(v):
    return 1.0 / (1.0 + jnp.exp(-v))


def split(v):
    a = v.astype(BF16)
    r = v - a.astype(F32)
    b = r.astype(BF16)
    return a, b, (r - b.astype(F32)).astype(BF16)


def exact_dot(v, ones):
    n = v.shape[0]
    s = dot(jnp.concatenate(split(v), axis=0), ones)
    return s[:n] + s[n:2 * n] + s[2 * n:]


def tri(n, keep):
    r = lax.broadcasted_iota(jnp.int32, (n, n), 0)
    c = lax.broadcasted_iota(jnp.int32, (n, n), 1)
    return jnp.where(keep(r, c), 1.0, 0.0).astype(BF16)


def conv(u, cols):
    shifted = [later(u, k) for k in range(4)]
    p = cols[:, 4:5] + cols[:, 0:1] * shifted[0]
    for k in range(1, 4):
        p = p + cols[:, k:k + 1] * shifted[k]
    return p, shifted


def conv_back(dp, cols):
    du = cols[:, 0:1] * dp
    for k in range(1, 4):
        du = du + cols[:, k:k + 1] * sooner(dp, k)
    return du


def decay(cum_row, cum_col, b):
    return jnp.exp(jnp.minimum(cum_row[:, b * SPAN:(b + 1) * SPAN] - cum_col, 0.0))


def group_at(n):
    zh, c = n % 2, n // 2
    return zh, c, pl.multiple_of((zh * 3 + c) * WIDE, WIDE), zh * 16 + c * GROUP


def group_cols(prm, zh, c):
    return prm[zh, :, pl.ds(pl.multiple_of(c * WIDE, WIDE), WIDE)].T


def group_skip(prm, zh, c):
    cols = prm[zh, :, 0:128].T
    return pltpu.roll(jnp.broadcast_to(cols[:, 8:9], (128, 128)), 128 - c * GROUP, 0)


def forward_kernel(main_h, step_h, state_h, out_h, hidden_h, cot_h, vecs_h, cinner_h, cstate_h,
                   xt_o, gt_o, zt_o, ut_o, dgt_o, vt_o, xst_o, dsil_o, yt_o, w_o, wst_o,
                   *rest):
    small_o, (step_w, hidden, vecs, cinner, cstate, w, x, g, xt, gt, zt, ut, dgt, vt, xst, dsil, yt, acc, acc_in,
              sums, dtt, cumt, cumc, stept, statet, bc, bct, cbt, prm, spar,
              send, recv, local, w_sem, out_sem, swap_send, swap_recv) = rest[:11], rest[11:]
    at = place()
    z_hi = at["z"] // 2
    mate = {**at, "core": 1 - at["core"]}
    far = moved(at, "z", 2)
    entered = greet([moved(at, axis, by) for axis in "xyz" for by in (1, 3)] + [mate, far])
    mine = pl.ds(pl.multiple_of(at["core"] * 256, 256), 256)
    own_unit = w.at[units(at, "")]
    moves = [(step_h, step_w), (hidden_h, hidden), (vecs_h, vecs), (cinner_h, cinner), (cstate_h, cstate), (cot_h, g.at[mine])]
    for piece in range(3):
        rows = pl.ds(piece * 16, 16)
        for source, begin, width in ((state_h.at[rows, pl.ds(pl.multiple_of(z_hi * 128, 128), 128)], 0, 128), (main_h.at[rows, pl.ds(768, 768)], 256, 768),
                                     (main_h.at[rows, pl.ds(0, 768)], 1024, 768), (out_h.at[rows], 1792, 768)):
            moves.append((source, own_unit.at[piece, :, pl.ds(begin, width)]))
    moves = [pltpu.make_async_copy(a, b, local.at[i]) for i, (a, b) in enumerate(moves)]
    for c in moves:
        c.start()
    moves[0].wait()
    for piece in range(3):
        w[units(at, "") + (piece, slice(None), pl.ds(128, 128))] = jnp.zeros((16, 128), BF16)
        w[units(at, "") + (piece, slice(None), pl.ds(128, 12))] = step_w[piece * 16:(piece + 1) * 16, :]
    for c in moves[6:]:
        c.wait()
    entered()

    def part(where, piece, stage, chunk):
        begin, width = STAGED[chunk] if stage == 2 else (0, COLS)
        return w.at[units(where, ORDERS[piece][:stage]) + (piece, slice(None), pl.ds(begin, width))]

    def flight(piece, stage, chunk, kind):
        axis, by = ORDERS[piece][stage], (1, 3)[kind % 2]
        width = STAGED[chunk][1] if stage == 2 else COLS
        if kind < 2:
            target = source = part(at, piece, stage, chunk)
        else:
            target = source = half_of(part(moved(at, axis, -by), piece, stage, chunk), 2 - stage, piece, width, kind - 2)
        sem = (stage + chunk if stage == 2 else stage, piece, kind)
        return pltpu.make_async_remote_copy(src_ref=source, dst_ref=target, send_sem=send.at[sem], recv_sem=recv.at[sem],
                                            device_id=device_at(moved(at, axis, by)), device_id_type=MESH)

    def fulls(stage, chunk=0):
        for piece in range(3):
            if stage > 0 and chunk == 0:
                for kind in (2, 3):
                    flight(piece, stage - 1, 0, kind).wait_recv()
            for kind in (0, 1):
                flight(piece, stage, chunk, kind).start()

    def halves(stage, chunk=0):
        for piece in range(3):
            for kind in (0, 1):
                flight(piece, stage, chunk, kind).wait_recv()
                flight(piece, stage, chunk, kind + 2).start()

    def arrived(chunk):
        for piece in range(3):
            for kind in (2, 3):
                flight(piece, 2, chunk, kind).wait_recv()

    fulls(0)
    for c in moves[1:6]:
        c.wait()

    prm[z_hi] = jnp.zeros((16, 768), F32)
    prm[z_hi, 0:4, :] = cinner[...]
    prm[z_hi, 4:5, :] = vecs[:, 0:768]
    prm[z_hi, 5:6, :] = vecs[:, 768:1536]
    for i in range(3):
        prm[z_hi, 6 + i:7 + i, 0:128] = vecs[:, 3328 + i * 128:3456 + i * 128]
    h = hidden[...].astype(F32)
    scale = lax.rsqrt(jnp.mean(h * h, axis=1, keepdims=True) + EPS)
    x[mine, :] = (h * scale * vecs[:, 1792:3328]).astype(BF16)
    swaps = [pltpu.make_async_remote_copy(src_ref=s, dst_ref=s, send_sem=swap_send.at[i], recv_sem=swap_recv.at[i],
                                          device_id=device_at(to), device_id_type=MESH)
             for i, (s, to) in enumerate([(x.at[mine], mate), (g.at[mine], mate), (prm.at[z_hi], far)])]
    for c in swaps:
        c.start()
    spar[...] = jnp.concatenate([cstate[...], vecs[:, 1536:1792], jnp.zeros((11, 256), F32)], axis=0).T

    halves(0)
    fulls(1)
    out_copies = []

    def put(i, source, target):
        c = pltpu.make_async_copy(source, target, out_sem.at[i])
        c.start()
        out_copies.append(c)

    for c in swaps[:2]:
        c.wait_recv()
    xt[...] = x[...].T
    gt[...] = g[...].T
    put(0, xt, xt_o)
    put(1, gt, gt_o)
    halves(1)
    swaps[2].wait_recv()
    acc[...] = jnp.zeros_like(acc)
    cumc[...] = jnp.zeros_like(cumc)
    fulls(2, 0)
    fulls(2, 1)
    halves(2, 0)
    halves(2, 1)
    fulls(2, 2)
    arrived(0)
    put(2, w.at[:, :, :, :, :, :, pl.ds(0, 256)], wst_o)

    def weight(zh, begin):
        return w[zh, :, :, :, :, :, pl.ds(begin, WIDE)].reshape(1536, WIDE)

    for zh in range(2):
        raw = dot(x[...], weight(zh, 0)).T.astype(BF16)
        statet[zh * 128:(zh + 1) * 128, :] = raw[:128]
        stept[zh * 16:(zh + 1) * 16, :] = raw[128:144]
    for q in range(4):
        r = slice(q * 64, (q + 1) * 64)
        p, _ = conv(statet[r, :].astype(F32), spar[r])
        bct[r, :] = (p * sig(p)).astype(BF16)
    bc[...] = bct[...].T
    upper = tri(SPAN, lambda r, c: r <= c)
    for b in range(2):
        rows = pl.ds(b * SPAN, SPAN)
        cbt[b] = dot(bc[rows, 0:128], bc[rows, 128:256], 1, 1) * upper.astype(F32)
    for zh in range(2):
        cols = prm[zh, :, 0:128].T
        v = stept[zh * 16:(zh + 1) * 16, :].astype(F32) + cols[:16, 6:7]
        dt = jnp.maximum(v, 0.0) + jnp.log1p(jnp.exp(-jnp.abs(v)))
        dtt[zh * 16:(zh + 1) * 16, :] = dt
        la = dt * -jnp.exp(cols[:16, 7:8])
        for b in range(2):
            cumt[zh * 16:(zh + 1) * 16, b * SPAN:(b + 1) * SPAN] = exact_dot(la[:, b * SPAN:(b + 1) * SPAN], upper)
    cumc[...] = jnp.concatenate([cumt[...], jnp.zeros((96, T), F32)], axis=0).T
    for i, ref in enumerate((dtt, cumt, cumc, stept, statet, bc, bct, cbt, prm, spar)):
        put(10 + i, ref, small_o[1 + i])

    def put_weights(kind, begin):
        for n in range(8):
            zh, q = n % 2, n // 2
            pltpu.make_async_copy(w.at[zh, q, :, :, :, :, pl.ds(begin, 768)], w_o.at[kind, q, zh], w_sem.at[kind]).start()

    arrived(1)
    put_weights(2, 256)

    @pl.loop(0, 6)
    def _(n):
        zh, c, off, base = group_at(n)
        cols = group_cols(prm, zh, c)
        skip = group_skip(prm, zh, c)
        cc = pltpu.roll(cumc[...], 128 - base, 1)
        ut[pl.ds(off, WIDE), :] = dot(x[...], weight(zh, pl.multiple_of(256 + c * WIDE, WIDE))).T.astype(BF16)
        for i in range(GROUP):
            r = slice(i * HEAD, (i + 1) * HEAD)
            rows = pl.ds(pl.multiple_of(off + i * HEAD, HEAD), HEAD)
            p, _ = conv(ut[rows, :].astype(F32), cols[r])
            sp = sig(p)
            xs = p * sp
            xsb = xs.astype(BF16)
            xst[rows, :] = xsb
            dsil[rows, :] = (sp + xs * (1.0 - sp)).astype(BF16)
            xs = xsb.astype(F32)
            cum = cumt[pl.ds(base + i, 1), :]
            xdt = xs * dtt[pl.ds(base + i, 1), :]
            xdtb = xdt.astype(BF16)
            ys = []
            for b in range(2):
                m = (decay(cum, cc[b * SPAN:(b + 1) * SPAN, i:i + 1], b) * cbt[b]).astype(BF16)
                ys.append(dot(xdtb[:, b * SPAN:(b + 1) * SPAN], m))
            tail = jnp.exp(cum[:, SPAN - 1:SPAN] - cum[:, :SPAN])
            state = dot((xdt[:, :SPAN] * tail).astype(BF16), bc[0:SPAN, 0:128]).astype(BF16)
            ys[1] = ys[1] + jnp.exp(cum[:, SPAN:]) * dot(state, bc[SPAN:, 128:256], 1, 1)
            yt[rows, :] = jnp.concatenate(ys, axis=1) + skip[i:i + 1, 0:1] * xs

        @pl.when(n == 2)
        def _():
            halves(2, 2)
            fulls(2, 3)

    put(3, xst, xst_o)
    put(4, yt, yt_o)
    put(5, ut, ut_o)
    put(9, dsil, dsil_o)
    arrived(2)
    put_weights(1, 1024)

    @pl.loop(0, 6)
    def _(n):
        zh, c, off, _ = group_at(n)
        zt[pl.ds(off, WIDE), :] = dot(x[...], weight(zh, pl.multiple_of(1024 + c * WIDE, WIDE))).T.astype(BF16)
        for i in range(GROUP):
            rows = pl.ds(pl.multiple_of(off + i * HEAD, HEAD), HEAD)
            z = zt[rows, :].astype(F32)
            vb = (yt[rows, :] * (z * sig(z))).astype(BF16)
            vt[rows, :] = vb
            v = vb.astype(F32)
            acc[0:1, :] += jnp.sum(v * v, axis=0, keepdims=True)

        @pl.when(n == 3)
        def _():
            halves(2, 3)

    put(6, zt, zt_o)
    put(7, vt, vt_o)
    arrived(3)
    put_weights(0, 1792)

    @pl.loop(0, 6)
    def _(n):
        zh, c, off, _ = group_at(n)
        cols = group_cols(prm, zh, c)
        dgt[pl.ds(off, WIDE), :] = dot(g[...], weight(zh, pl.multiple_of(1792 + c * WIDE, WIDE))).T.astype(BF16)
        for i in range(GROUP):
            rows = pl.ds(pl.multiple_of(off + i * HEAD, HEAD), HEAD)
            s = dgt[rows, :].astype(F32) * cols[i * HEAD:(i + 1) * HEAD, 5:6] * vt[rows, :].astype(F32)
            acc[1:2, :] += jnp.sum(s, axis=0, keepdims=True)

    c = pltpu.make_async_remote_copy(src_ref=acc, dst_ref=acc_in, send_sem=swap_send.at[3], recv_sem=swap_recv.at[3],
                                     device_id=device_at(mate), device_id_type=MESH)
    c.start()
    put(8, dgt, dgt_o)
    for piece in range(3):
        for kind in range(4):
            for stage in range(2):
                flight(piece, stage, 0, kind).wait_send()
            for chunk in range(4):
                flight(piece, 2, chunk, kind).wait_send()
    for s in swaps:
        s.wait_send()
    c.wait()
    sums[...] = acc[...] + acc_in[...]
    put(20, sums, small_o[0])
    for kind in range(3):
        pltpu.make_async_copy(w_o.at[kind], w_o.at[kind], w_sem.at[kind]).wait()
    for c in out_copies:
        c.wait()


def forward(main, step_w, state_w, out_w, hidden, cot, vecs, cinner, cstate):
    any_ = pl.BlockSpec(memory_space=pl.ANY)
    dma = pltpu.SemaphoreType.DMA
    tall = [sds((1536, T), BF16)] * 8 + [sds((1536, T))]
    big = tall + [sds((3, 4, 2, 4, 2, 3, 16, 768), BF16), sds((2, 4, 4, 2, 3, 16, 256), BF16)]
    small = [sds((8, T)), sds((32, T)), sds((32, T)), sds((T, 128)), sds((32, T), BF16), sds((256, T), BF16), sds((T, 256), BF16),
             sds((256, T), BF16), sds((2, SPAN, SPAN)), sds((2, 16, 768)), sds((256, 16))]
    return pl.pallas_call(
        forward_kernel, out_shape=big + small, in_specs=[any_] * 9, out_specs=[any_] * 22,
        scratch_shapes=[pltpu.VMEM((48, 12), BF16), pltpu.VMEM((256, 1536), BF16), pltpu.VMEM(vecs.shape, F32), pltpu.VMEM((4, 768), F32),
                        pltpu.VMEM((4, 256), F32), pltpu.VMEM((2, 4, 4, 2, 3, 16, COLS), BF16), pltpu.VMEM((T, 1536), BF16),
                        pltpu.VMEM((T, 1536), BF16)] + [pltpu.VMEM(s.shape, s.dtype) for s in tall] + [
            pltpu.VMEM((8, T), F32), pltpu.VMEM((8, T), F32)] + [pltpu.VMEM(s.shape, s.dtype) for s in small] + [
            dma((6, 3, 4)), dma((6, 3, 4)), dma((18,)), dma((3,)), dma((21,)), dma((4,)), dma((4,))],
        compiler_params=pltpu.CompilerParams(collective_id=0, has_side_effects=True, vmem_limit_bytes=60 << 20),
    )(main, step_w, state_w, out_w, hidden, cot, vecs, cinner, cstate)


SCAN_STEPS = {3: [(0, 2)], 7: [(1, 1)]}
CONV_STEPS = {0: [(0, 3)], 1: [(4, 0)], 2: [(1, 2), (0, 4)], 3: [(2, 0), (4, 1)], 4: [(0, 5), (1, 3)], 5: [(3, 0), (4, 2)]}
REST = [(0, 6), (1, 4), (2, 1), (4, 3), (3, 1), None, (1, 5), (2, 2), (4, 4), None, (3, 2), (4, 5), (1, 6), None, (2, 3), (4, 6), None,
        (3, 3), (2, 4), (3, 4), None, (2, 5), (3, 5), (2, 6), (3, 6)]


def add_into(target, *others):
    def add(t, o):
        v = t[...].astype(F32)
        for other in o:
            v = v + other[...].astype(F32)
        t[...] = v.astype(BF16)
    if len(target.shape) == 2:
        add(target, others)
    else:
        @pl.loop(0, target.shape[0])
        def _(i):
            add(target.at[i], [o.at[i] for o in others])


def backward_kernel(xt_h, gt_h, zt_h, ut_h, dgt_h, vt_h, xst_h, dsil_h, yt_h, w_h, wst_h,
                    *rest_refs):
    small_h, outs_h, scratch = rest_refs[:14], rest_refs[14:19], rest_refs[19:]
    n = len(RCHUNKS)
    part, regions, halves = scratch[0], scratch[1:1 + 9 * n], scratch[1 + 9 * n:1 + 18 * n]
    (xt, gt, zt, dgt, vt, gat, yt, wbuf, wst, total, dcbt, ld, dye_all, xe_all, st_all, ds_all, cross, prow, hrow,
     dcum, ddt1, gskip, dstep_t, dbct, dbct_in, dn_in, branch, br_in, dstate, dst, folds,
     sums, dtt, cumt, cumc, stept, statet, bc, bct, cbt, prm, spar, hidden, cot, gain, out, gstate, gsmall, new_hidden, grad_hidden, vec, vec_in, own_state, ggain, gain_in, quarter, quarters,
     send, recv, load_sem, w_sem, swap_send, swap_recv, vec_send, vec_recv, q_send, q_recv, out_sem) = scratch[1 + 18 * n:]
    xst, ut, dyt, dzt, dsil, dut = gt, vt, zt, dgt, gat, zt
    at = place()
    mate = {**at, "core": 1 - at["core"]}
    far = moved(at, "z", 2)
    far_mate = {**far, "core": 1 - at["core"]}
    entered = greet([moved(at, axis, by) for axis in "xyz" for by in (1, 2, 3)] + [mate, far_mate])
    mine = pl.ds(pl.multiple_of(at["core"] * 256, 256), 256)
    theirs = pl.ds(pl.multiple_of((1 - at["core"]) * 256, 256), 256)

    loads = [pltpu.make_async_copy(s, d, load_sem.at[i]) for i, (s, d) in enumerate(
        [(vt_h, vt), (gt_h, gt), (yt_h, yt), (zt_h, zt), (dgt_h, dgt), (xt_h, xt), (xst_h, xst), (ut_h, ut), (wst_h, wst), (dsil_h, dsil)]
        + list(zip(small_h, (sums, dtt, cumt, cumc, stept, statet, bc, bct, cbt, prm, spar, hidden, cot, gain))))]
    first = [loads[i] for i in (10, 19, 0, 1)]
    second = loads[2:6] + loads[8:9] + loads[11:19] + loads[20:]
    out_copies = []

    def put(i, source):
        c = pltpu.make_async_copy(source, outs_h[i], out_sem.at[i])
        c.start()
        out_copies.append(c)

    def weights(i):
        return pltpu.make_async_copy(w_h.at[i // 4, i % 4], wbuf.at[i % 2], w_sem.at[i % 2])

    def product(i, values):
        weights(i).wait()

        @pl.when(i + 1 < 12)
        def _():
            weights(i + 1).start()
        return (dot(wbuf[i % 2, 0].reshape(384, 768), values[0:768, :]) + dot(wbuf[i % 2, 1].reshape(384, 768), values[768:1536, :])).T

    for c in first:
        c.start()
    weights(0).start()
    for c in second:
        c.start()

    def remote(src, dst_ref, s, r, to):
        return pltpu.make_async_remote_copy(src_ref=src, dst_ref=dst_ref, send_sem=s, recv_sem=r, device_id=device_at(to), device_id_type=MESH)

    def block(where, chunk, piece, stage):
        begin, width = RCHUNKS[chunk]
        return part.at[units(where, ORDERS[piece][:2 - stage]) + (piece, slice(None), pl.ds(begin, width))]

    def whole(chunk, stage):
        return stage == 2 and RCHUNKS[chunk][1] <= 128

    def slot(chunk, piece, stage):
        return (chunk * 3 + piece) * 3 + stage

    def start(chunk, piece, stage, i):
        axis = ORDERS[piece][2 - stage]
        k = slot(chunk, piece, stage)
        right, left, opposite = moved(at, axis, 1), moved(at, axis, 3), moved(at, axis, 2)
        cut = lambda ref, h: half_of(ref, stage, piece, RCHUNKS[chunk][1], h)
        own = lambda where: block(where, chunk, piece, stage)
        src, dst_ref, to = (
            lambda: (cut(own(opposite), 0), halves[k].at[0], right),
            lambda: (cut(own(opposite), 1), halves[k].at[1], left),
            lambda: (cut(own(right), 1), cut(regions[k].at[0], 1), right),
            lambda: (cut(own(left), 0), cut(regions[k].at[1], 0), left),
            lambda: (cut(own(right), 0), cut(regions[k].at[0], 0), right),
            lambda: (cut(own(left), 1), cut(regions[k].at[1], 1), left))[i]()
        remote(src, dst_ref, send.at[chunk, piece, int(i > 1)], recv.at[chunk, piece, stage, int(i > 1)], to).start()

    def took(buffer, sem):
        pltpu.make_async_copy(buffer, buffer, sem).wait()

    def kinds(chunk, stage):
        return ((0,), (3,), (4,)) if whole(chunk, stage) else ((0, 1), (2, 3), (4, 5))

    def sent(chunk, piece, stage):
        k = slot(chunk, piece, stage)
        took(halves[k], send.at[chunk, piece, 0])
        took(regions[k], send.at[chunk, piece, 1])

    def step(chunk, k):
        for piece in range(3):
            stage = k // 2
            if k % 2:
                first, _, last = kinds(chunk, stage)
                took(halves[slot(chunk, piece, stage)], recv.at[chunk, piece, stage, 0])
                axis = ORDERS[piece][2 - stage]
                for j in last:
                    mid = half_of(block(moved(at, axis, 1 if j == 4 else 3), chunk, piece, stage), stage, piece, RCHUNKS[chunk][1], j - 4)
                    add_into(mid, halves[slot(chunk, piece, stage)].at[j - 4])
                    start(chunk, piece, stage, j)
            else:
                if k > 0:
                    s = slot(chunk, piece, stage - 1)
                    took(regions[s], recv.at[chunk, piece, stage - 1, 1])
                    add_into(block(at, chunk, piece, stage - 1), regions[s].at[0], regions[s].at[1])
                    sent(chunk, piece, stage - 1)
                if k < 6:
                    first, second, _ = kinds(chunk, stage)
                    for i in first + second:
                        start(chunk, piece, stage, i)

    def steps_after(table, index):
        for i, todo in table.items():
            @pl.when(index == i)
            def _(todo=todo):
                for chunk, k in todo:
                    step(chunk, k)

    def gradients(left, right, zh, col):
        for q in range(4):
            value = dot(left[q * 384:(q + 1) * 384, :], right, 1, 1).astype(BF16)
            part[zh, q, :, :, :, :, pl.ds(col, right.shape[0])] = value.reshape(4, 2, 3, 16, right.shape[0])

    def strip(q):
        return pl.ds(pl.multiple_of(q * 384, 128), 384)

    def fold(v):
        return v[:, 0:128] + v[:, 128:256] + v[:, 256:384] + v[:, 384:512]

    def row_sums(v):
        ones = jnp.ones((8, 128), BF16)
        a, b, _ = split(v)
        return (dot(ones, a, 1, 1) + dot(ones, b, 1, 1))[0:1]

    for ref in (dcbt, cross, dcum, ddt1, gskip, vec, ggain):
        ref[...] = jnp.zeros_like(ref)
    for c in first:
        c.wait()
    r_out = lax.rsqrt(sums[0:1, :] / INNER + EPS)
    k2 = r_out * r_out * r_out * sums[1:2, :] / INNER


    @pl.loop(0, 6)
    def _(m):
        zh, c, off, _ = group_at(m)
        cols = group_cols(prm, zh, c)
        group = pl.ds(off, WIDE)
        for i in range(GROUP):
            r = slice(i * HEAD, (i + 1) * HEAD)
            rows = pl.ds(pl.multiple_of(off + i * HEAD, HEAD), HEAD)
            gat[rows, :] = (vt[rows, :].astype(F32) * r_out * cols[r, 5:6]).astype(BF16)
        gradients(gt, gat[group, :], zh, pl.multiple_of(c * WIDE, WIDE))

    loads[6].start()
    entered()
    step(0, 0)
    for c in second:
        c.wait()

    @pl.loop(0, 6)
    def _(m):
        zh, c, off, _ = group_at(m)
        cols = group_cols(prm, zh, c)
        group = pl.ds(off, WIDE)
        for i in range(GROUP):
            r = slice(i * HEAD, (i + 1) * HEAD)
            rows = pl.ds(pl.multiple_of(off + i * HEAD, HEAD), HEAD)
            z = zt[rows, :].astype(F32)
            dg = dgt[rows, :].astype(F32)
            v = vt[rows, :].astype(F32)
            sz = sig(z)
            zs = z * sz
            dv = dg * cols[r, 5:6] * r_out - v * k2
            folds[0, r, :] = fold(dg * v * r_out)
            dyt[rows, :] = (dv * zs).astype(BF16)
            dzt[rows, :] = (dv * yt[rows, :] * (sz + zs * (1.0 - sz))).astype(BF16)
        prow[zh * 3 + c, 5:6, :] = row_sums(folds[0])
        gradients(xt, dzt[group, :], zh, pl.multiple_of(768 + c * WIDE, WIDE))

    loads[7].start()
    step(0, 1)
    step(1, 0)

    @pl.loop(0, 4)
    def _(q):
        branch[:, strip(q)] = product(q, gat).astype(BF16)

    loads[9].start()
    swap_br = remote(branch.at[theirs], br_in, swap_send.at[0], swap_recv.at[0], mate)
    swap_br.start()

    @pl.loop(0, 4)
    def _(q):
        total[:, strip(q)] = product(4 + q, dzt)

    loads[6].wait()

    @pl.loop(0, 6)
    def _(m):
        zh, c, off, base = group_at(m)
        cc = pltpu.roll(cumc[...], 128 - base, 1)
        skips = group_skip(prm, zh, c)
        for i in range(GROUP):
            r = slice(i * HEAD, (i + 1) * HEAD)
            rows = pl.ds(pl.multiple_of(off + i * HEAD, HEAD), HEAD)
            skip = skips[i:i + 1, 0:1]
            xs = xst[rows, :].astype(F32)
            dyb = dyt[rows, :]
            dy = dyb.astype(F32)
            yssm = yt[rows, :] - skip * xs
            gskip[pl.ds(base + i, 1), :] = jnp.sum(dy * xs, axis=0, keepdims=True)
            dt = dtt[pl.ds(base + i, 1), :]
            cum = cumt[pl.ds(base + i, 1), :]
            xdt = xs * dt
            xdtb = xdt.astype(BF16)
            dxs = []
            for b in range(2):
                s = slice(b * SPAN, (b + 1) * SPAN)
                w = decay(cum, cc[s, i:i + 1], b)
                dxs.append(dot(dyb[:, s], (w * cbt[b]).astype(BF16), 1, 1))
                dcbt[b] += dot(xdtb[:, s], dyb[:, s], 0, 0) * w
            tail = jnp.exp(cum[:, SPAN - 1:SPAN] - cum[:, :SPAN])
            xe = (xdt[:, :SPAN] * tail).astype(BF16)
            dye = (dy[:, SPAN:] * jnp.exp(cum[:, SPAN:])).astype(BF16)
            ds = dot(dye, bc[SPAN:, 128:256]).astype(BF16)
            xe_all[r, :] = xe
            dye_all[r, :] = dye
            st_all[r, :] = dot(xe, bc[0:SPAN, 0:128]).astype(BF16)
            ds_all[r, :] = ds
            dxs[0] = dxs[0] + tail * dot(ds, bc[0:SPAN, 0:128], 1, 1)
            dx = jnp.concatenate(dxs, axis=1)
            dcum[pl.ds(base + i, 1), :] = jnp.sum(dy * yssm - xdtb.astype(F32) * dx, axis=0, keepdims=True)
            ddt1[pl.ds(base + i, 1), :] = jnp.sum(xs * dx, axis=0, keepdims=True)
            dyt[rows, :] = (dt * dx + skip * dy).astype(BF16)
            if i % 2:
                steps_after(SCAN_STEPS, m * 2 + i // 2)
        cross[1] += dot(st_all[...], dye_all[...], 0, 0)
        cross[0] += dot(ds_all[...], xe_all[...], 0, 0)

    upper = tri(SPAN, lambda r, c: r <= c).astype(F32)
    for b in range(2):
        s = slice(b * SPAN, (b + 1) * SPAN)
        d = (dcbt[b] * upper).astype(BF16)
        db = dot(bct[128:256, s], d, 1, 1)
        dc = dot(bct[0:128, s], d)
        dbct[0:128, s] = (db + cross[0] if b == 0 else db).astype(BF16)
        dbct[128:256, s] = (dc + cross[1] if b == 1 else dc).astype(BF16)
    swap_bc = remote(dbct, dbct_in, swap_send.at[1], swap_recv.at[1], mate)
    swap_bc.start()

    dla = exact_dot(dcum[...], tri(T, lambda r, c: r >= c))
    for zh in range(2):
        rows = slice(zh * 16, (zh + 1) * 16)
        hc = prm[zh, :, 0:128].T
        rate = -jnp.exp(hc[:16, 7:8])
        d = dla[rows]
        dstep = (ddt1[rows, :] + rate * d) * sig(stept[rows, :].astype(F32) + hc[:16, 6:7])
        gd = jnp.sum(d * dtt[rows, :] * rate, axis=1, keepdims=True)
        hcol = jnp.concatenate([jnp.sum(dstep, axis=1, keepdims=True), gd, jnp.sum(gskip[rows, :], axis=1, keepdims=True),
                                jnp.zeros((16, 125), F32)], axis=1)
        hrow[:, zh * 128:(zh + 1) * 128] = jnp.concatenate([hcol, jnp.zeros((112, 128), F32)], axis=0).T[:8]
        keep = lax.broadcasted_iota(jnp.int32, (16, T), 0) < 12
        dstep_t[zh, 0:16, :] = jnp.where(keep, dstep, 0.0).astype(BF16)
        dstep_t[zh, 16:128, :] = jnp.zeros((112, T), BF16)

    loads[7].wait()
    loads[9].wait()

    def convolution(m):
        zh, c, off, _ = group_at(m)
        cols = group_cols(prm, zh, c)
        for i in range(GROUP):
            r = slice(i * HEAD, (i + 1) * HEAD)
            rows = pl.ds(pl.multiple_of(off + i * HEAD, HEAD), HEAD)
            u = ut[rows, :].astype(F32)
            dp = dyt[rows, :].astype(F32) * dsil[rows, :].astype(F32)
            du = cols[r, 0:1] * dp
            folds[0, r, :] = fold(u * dp)
            folds[4, r, :] = fold(dp)
            for k in range(1, 4):
                ahead = sooner(dp, k)
                du = du + cols[r, k:k + 1] * ahead
                folds[k, r, :] = fold(u * ahead)
            dut[rows, :] = du.astype(BF16)
        for k in range(5):
            prow[zh * 3 + c, k:k + 1, :] = row_sums(folds[k])
        gradients(xt, dut[pl.ds(off, WIDE), :], zh, pl.multiple_of(1536 + c * WIDE, WIDE))

    def state_back():
        swap_bc.wait_recv()
        for q in range(4):
            r = slice(q * 64, (q + 1) * 64)
            cols = spar[r]
            p, shifted = conv(statet[r, :].astype(F32), cols)
            sp = sig(p)
            dp = (dbct[r, :].astype(F32) + dbct_in[r, :].astype(F32)) * (sp + p * sp * (1.0 - sp))
            dstate[r, :] = conv_back(dp, cols).astype(BF16)
            dst[r, :] = jnp.concatenate([jnp.sum(dp * shifted[k], axis=1, keepdims=True) for k in range(4)]
                                        + [jnp.sum(dp, axis=1, keepdims=True), jnp.zeros((64, 123), F32)], axis=1)
        vec[48:56, :] = dst[...].T[:8]
        for zh in range(2):
            ld[0:64, :] = dstate[pl.ds(zh * 128 + pl.multiple_of(at["core"] * 64, 64), 64), :]
            ld[64:128, :] = dstep_t[zh, 0:64, :]
            gradients(xt, ld[...], zh, 2304)

    @pl.loop(0, 6)
    def _(m):
        convolution(m)

        @pl.when(m == 1)
        def _():
            state_back()
        steps_after(CONV_STEPS, m)

    swap_br.wait()

    @pl.loop(0, 4)
    def _(q):
        more = [dot(wst[zh, q, :, :, :, :, pl.ds(128, 128)].reshape(384, 128), dstep_t[zh]) for zh in range(2)]
        total[:, strip(q)] += product(8 + q, dut) + (more[0] + more[1]).T
        branch[theirs, strip(q)] = total[theirs, strip(q)].astype(BF16)

    swap_dn = remote(branch.at[theirs], dn_in, swap_send.at[2], swap_recv.at[2], mate)
    swap_dn.start()
    rest = list(REST)

    def go():
        while rest and rest[0] is not None:
            step(*rest.pop(0))
        rest[:1] = []

    go()
    own_state[...] = dstate[:, mine].T
    swap_dn.wait_recv()

    @pl.loop(0, 2)
    def _(q):
        r = pl.ds(pl.multiple_of(q * 128, 128), 128)
        full = total[pl.ds(pl.multiple_of(at["core"] * 256 + q * 128, 128), 128), :] + dn_in[r, :].astype(F32)
        for zh in range(2):
            full = full + dot(own_state[r, zh * 128:(zh + 1) * 128], wst[zh, :, :, :, :, :, pl.ds(0, 128)].reshape(1536, 128), 1, 1)
        h = hidden[r, :].astype(F32)
        r_in = lax.rsqrt(jnp.mean(h * h, axis=1, keepdims=True) + EPS)
        ggain[...] += jnp.sum(full * h * r_in, axis=0, keepdims=True)
        scaled = full * gain[...]
        back = scaled * r_in - h * (r_in * r_in * r_in * (jnp.sum(scaled * h, axis=1, keepdims=True) / 1536))
        grad_hidden[r, :] = (cot[r, :].astype(F32) + back).astype(BF16)

    for q in range(6):
        vec[q * 8:(q + 1) * 8, :] = prow[q]
        vec[56 + q:57 + q, :] = ggain[:, q * 256:(q + 1) * 256]
    vec[64:72, :] = hrow[...]

    def vec_flights(s):
        return [remote(vec, vec_in.at[s, by - 1], vec_send.at[s, by - 1], vec_recv.at[s, by - 1], moved(at, "xyz"[s], by)) for by in (1, 2, 3)]

    def vec_end(s):
        for c in vec_flights(s):
            c.wait()
        vec[...] = vec[...] + vec_in[s, 0] + vec_in[s, 1] + vec_in[s, 2]

    def vec_start(s):
        for c in vec_flights(s):
            c.start()

    vec_start(0)
    put(4, grad_hidden)

    @pl.loop(0, 2)
    def _(q):
        r = pl.ds(pl.multiple_of(q * 128, 128), 128)
        new_hidden[r, :] = (hidden[r, :].astype(F32) + branch[pl.ds(pl.multiple_of(at["core"] * 256 + q * 128, 128), 128), :].astype(F32) + br_in[r, :].astype(F32)).astype(BF16)

    put(3, new_hidden)
    go()
    vec_end(0)
    vec_start(1)
    go()
    vec_end(1)
    vec_start(2)
    go()
    own = units(at, "")
    last = RCHUNKS[n - 1][0]
    for piece in range(3):
        quarter[piece * 16:(piece + 1) * 16, :] = part[own + (piece, slice(None), pl.ds(last, 128))].astype(F32)
    thirds = [remote(quarter, quarters.at[i], q_send.at[i], q_recv.at[i], to) for i, to in enumerate((mate, far, far_mate))]
    for c in thirds:
        c.start()
    go()
    vec_end(2)
    final = remote(vec.at[pl.ds(56, 8)], gain_in, q_send.at[3], q_recv.at[3], mate)
    final.start()
    go()
    for piece in range(3):
        out[piece * 16:(piece + 1) * 16, :] = part[own + (piece, slice(None), pl.ds(0, 2304))].astype(F32)
    put(0, out)
    gsmall[...] = vec[...]
    final.wait()
    gsmall[56:64, :] = vec[56:64, :] + gain_in[...]
    put(2, gsmall)
    for c in thirds:
        c.wait()
    low = at["core"] == 0
    q0, q1, q2, q3 = quarter[...], quarters[0], quarters[1], quarters[2]
    here = jnp.where(low, jnp.concatenate([q0[:, :64], q1[:, :64]], axis=1), jnp.concatenate([q1[:, :64], q0[:, :64]], axis=1))
    there = jnp.where(low, jnp.concatenate([q2[:, :64], q3[:, :64]], axis=1), jnp.concatenate([q3[:, :64], q2[:, :64]], axis=1))
    first = at["z"] < 2
    gstate[:, 0:128] = jnp.where(first, here, there)
    gstate[:, 128:256] = jnp.where(first, there, here)
    gstate[:, 256:384] = q0
    put(1, gstate)
    for s in (swap_bc, swap_dn):
        s.wait_send()
    for c in out_copies:
        c.wait()


def backward(tall, small, hidden, cot, gain):
    n = len(RCHUNKS)
    results = [sds((48, 2304)), sds((48, 384)), sds((SUMS, 256)), sds((256, 1536), BF16), sds((256, 1536), BF16)]
    any_ = pl.BlockSpec(memory_space=pl.ANY)
    shapes = [(stage, piece, RCHUNKS[chunk][1]) for chunk in range(n) for piece in range(3) for stage in range(3)]
    regions = [pltpu.VMEM((2,) + region_shape(*s), BF16) for s in shapes]
    halves = [pltpu.VMEM((1 if s[0] == 2 and s[2] <= 128 else 2,) + half_shape(*s), BF16) for s in shapes]
    dma = pltpu.SemaphoreType.DMA
    v = lambda shape, dtype=F32: pltpu.VMEM(shape, dtype)
    return pl.pallas_call(
        backward_kernel,
        in_specs=[any_] * (len(tall) + len(small) + 3),
        out_specs=[any_] * 5,
        out_shape=results,
        scratch_shapes=[v((2, 4, 4, 2, 3, 16, RCOLS), BF16)] + regions + halves + [
            v((1536, T), BF16)] * 6 + [v((1536, T)), v((2, 2, 4, 2, 3, 16, 768), BF16), v((2, 4, 4, 2, 3, 16, 256), BF16),
            v((T, 1536)), v((2, SPAN, SPAN)), v((128, T), BF16), v((WIDE, SPAN), BF16), v((WIDE, SPAN), BF16),
            v((WIDE, 128), BF16), v((WIDE, 128), BF16), v((2, 128, SPAN)), v((6, 8, WIDE)), v((8, 256)),
            v((32, T)), v((32, T)), v((32, T)), v((2, 128, T), BF16), v((256, T), BF16), v((256, T), BF16),
            v((256, 1536), BF16), v((T, 1536), BF16), v((256, 1536), BF16),
            v((256, T), BF16), v((256, 128)), v((5, WIDE, 128))] + [v(a.shape, a.dtype) for a in (*small, hidden, cot, gain, *results)] + [ v((SUMS, 256)), v((3, 3, SUMS, 256)), v((256, 256), BF16), v((1, 1536)), v((8, 256)), v((48, 128)), v((3, 48, 128)),
            dma((n, 3, 2)), dma((n, 3, 3, 2)), dma((24,)), dma((2,)), dma((3,)), dma((3,)), dma((3, 3)), dma((3, 3)), dma((4,)), dma((4,)), dma((5,))],
        compiler_params=pltpu.CompilerParams(collective_id=1, has_side_effects=True, vmem_limit_bytes=65400 << 10),
    )(*tall, *small, hidden, cot, gain)


def per_device(hidden, in_gain, proj_main, proj_step, proj_state, conv_inner, conv_inner_bias, conv_state, conv_state_bias,
               step_bias, decay_log, skip_gain, out_gain, proj_out, grad_out):
    z_hi = lax.axis_index("tensor") // 2
    space = jnp.zeros((116,), F32)
    vecs = jnp.concatenate([conv_inner_bias, out_gain, conv_state_bias, in_gain, step_bias, space, decay_log, space, skip_gain, space])[None]
    outs = forward(proj_main.reshape(48, 1536), proj_step, proj_state, proj_out, hidden, grad_out, vecs, conv_inner, conv_state)
    out, gstate, small, new_hidden, grad_hidden = backward(outs[:11], outs[11:], hidden, grad_out, in_gain[None])
    grad_main = jnp.stack([out[:, 768:1536], out[:, 1536:]], axis=1)
    own = lax.dynamic_slice(small, (z_hi * 24, 0), (24, 256)).reshape(3, 8, 256)
    inner = jnp.moveaxis(own, 1, 0).reshape(8, 768)
    heads = lax.dynamic_slice(small, (64, z_hi * 128), (8, 12))
    return (new_hidden, grad_hidden, small[56:62].reshape(1536), grad_main, gstate[:, 320:332], gstate[:, :256], inner[:4], inner[4],
            small[48:52], small[52], heads[0], heads[1], heads[2], inner[5], out[:, :768])


def solution(mesh):
    rows = P(("dp", "tensor"), None)
    per_head = P("tensor")
    in_specs = (rows, P(), P("dp", None, "tensor"), P("dp", "tensor"), P("dp", None), P(None, "tensor"), per_head, P(), P(),
                per_head, per_head, per_head, per_head, P("dp", "tensor"), rows)
    out_specs = (rows, rows, P(), P("dp", None, "tensor"), P("dp", "tensor"), P("dp", None), P(None, "tensor"), per_head, P(), P(),
                 per_head, per_head, per_head, per_head, P("dp", "tensor"))
    return jax.shard_map(per_device, mesh=mesh, in_specs=in_specs, out_specs=out_specs, check_vma=False)
```

```python
import functools

import jax
import jax.numpy as jnp
from jax import lax
from jax.experimental import pallas as pl
from jax.experimental.pallas import tpu as pltpu
from jax.sharding import PartitionSpec as P

MESH = pl.DeviceIdType.MESH
F32, BF16 = jnp.float32, jnp.bfloat16
EPS = 1e-5
T, SPAN, HEAD, GROUP = 512, 256, 64, 4
WIDE = GROUP * HEAD
INNER = 3072
COLS = 2560
STAGED = ((0, 256), (256, 768), (1024, 768), (1792, 768))
ORDERS = ("xyz", "yzx", "zxy")
RCHUNKS = ((0, 768), (768, 768), (1536, 512), (2048, 256), (2304, 128))
RCOLS = 2432
SUMS = 72


def sds(shape, dtype=F32):
    return jax.ShapeDtypeStruct(shape, dtype)


def place():
    dp, tp = lax.axis_index("dp"), lax.axis_index("tensor")
    return dict(x=dp // 8, y=(dp // 2) % 4, z=(tp // 2) * 2 + dp % 2, core=tp % 2)


def device_at(at):
    return ((at["x"] * 4 + at["y"]) * 2 + at["z"] % 2, (at["z"] // 2) * 2 + at["core"])


def moved(at, axis, by):
    return {**at, axis: (at[axis] + by) % 4}


def units(at, whole):
    return (slice(None) if "z" in whole else at["z"] // 2, slice(None) if "x" in whole else at["x"],
            slice(None) if "y" in whole else at["y"], slice(None) if "z" in whole else at["z"] % 2)


def greet(others):
    barrier = pltpu.get_barrier_semaphore()
    for other in others:
        pl.semaphore_signal(barrier, inc=1, device_id=device_at(other), device_id_type=MESH)
    return lambda: pl.semaphore_wait(barrier, len(others))


def half_of(ref, stage, piece, width, half):
    if stage == 0:
        return ref.at[pl.ds(2 * half, 2)] if piece == 0 else ref.at[:, pl.ds(2 * half, 2)]
    if stage == 1:
        return ref.at[pl.ds(2 * half, 2)] if piece < 2 else ref.at[half]
    return ref.at[:, pl.ds(half * (width // 2), width // 2)] if width > 128 else ref


def half_shape(stage, piece, width):
    if stage == 0:
        return (2, 4, 16, width) if piece == 0 else (2, 2, 2, 16, width)
    if stage == 1:
        return (2, 16, width)
    return (16, width // 2) if width > 128 else (16, width)


def region_shape(stage, piece, width):
    whole = ORDERS[piece][:2 - stage]
    dims = ([2] if "z" in whole else []) + ([4] if "x" in whole else []) + ([4] if "y" in whole else []) + ([2] if "z" in whole else [])
    return tuple(dims) + (16, width)


def dot(a, b, ca=1, cb=0):
    return lax.dot_general(a, b, (((ca,), (cb,)), ((), ())), preferred_element_type=F32)


def lanes(rows, width=T):
    return lax.broadcasted_iota(jnp.int32, (rows, width), 1)


def later(u, k):
    return jnp.where(lanes(u.shape[0]) >= k, pltpu.roll(u, k, 1), 0.0) if k else u


def sooner(u, k):
    return jnp.where(lanes(u.shape[0]) < T - k, pltpu.roll(u, T - k, 1), 0.0) if k else u


def sig(v):
    return 1.0 / (1.0 + jnp.exp(-v))


def split(v):
    a = v.astype(BF16)
    r = v - a.astype(F32)
    b = r.astype(BF16)
    return a, b, (r - b.astype(F32)).astype(BF16)


def exact_dot(v, ones):
    n = v.shape[0]
    s = dot(jnp.concatenate(split(v), axis=0), ones)
    return s[:n] + s[n:2 * n] + s[2 * n:]


def tri(n, keep):
    r = lax.broadcasted_iota(jnp.int32, (n, n), 0)
    c = lax.broadcasted_iota(jnp.int32, (n, n), 1)
    return jnp.where(keep(r, c), 1.0, 0.0).astype(BF16)


def conv(u, cols):
    shifted = [later(u, k) for k in range(4)]
    p = cols[:, 4:5] + cols[:, 0:1] * shifted[0]
    for k in range(1, 4):
        p = p + cols[:, k:k + 1] * shifted[k]
    return p, shifted


def conv_back(dp, cols):
    du = cols[:, 0:1] * dp
    for k in range(1, 4):
        du = du + cols[:, k:k + 1] * sooner(dp, k)
    return du


def decay(cum_row, cum_col, b):
    return jnp.exp(jnp.minimum(cum_row[:, b * SPAN:(b + 1) * SPAN] - cum_col, 0.0))


def group_at(n):
    zh, c = n % 2, n // 2
    return zh, c, pl.multiple_of((zh * 3 + c) * WIDE, WIDE), zh * 16 + c * GROUP


def group_cols(prm, zh, c):
    return prm[zh, :, pl.ds(pl.multiple_of(c * WIDE, WIDE), WIDE)].T


def group_skip(prm, zh, c):
    cols = prm[zh, :, 0:128].T
    return pltpu.roll(jnp.broadcast_to(cols[:, 8:9], (128, 128)), 128 - c * GROUP, 0)


def forward_kernel(main_h, step_h, state_h, out_h, hidden_h, cot_h, cinner_h, cstate_h, offset_h, gain_h, state_offset_h, in_gain_h, bias_h, log_h, skip_h,
                   xt_o, gt_o, zt_o, ut_o, dgt_o, vt_o, xst_o, dsil_o, yt_o, w_o, wst_o,
                   *rest):
    small_o, (step_w, hidden, cinner, cstate, offset, gain, state_offset, in_gain, bias, log, skip_gain, w, x, g, xt, gt, zt, ut, dgt, vt, xst, dsil, yt, acc, acc_in,
              sums, dtt, cumt, cumc, stept, statet, bc, bct, cbt, prm, spar,
              send, recv, local, w_sem, out_sem, swap_send, swap_recv) = rest[:11], rest[11:]
    at = place()
    z_hi = at["z"] // 2
    mate = {**at, "core": 1 - at["core"]}
    far = moved(at, "z", 2)
    entered = greet([moved(at, axis, by) for axis in "xyz" for by in (1, 3)] + [mate, far])
    mine = pl.ds(pl.multiple_of(at["core"] * 256, 256), 256)
    own_unit = w.at[units(at, "")]
    moves = [(step_h, step_w), (hidden_h, hidden), (cot_h, g.at[mine]), (cinner_h, cinner), (cstate_h, cstate), (offset_h, offset), (gain_h, gain),
             (state_offset_h, state_offset), (in_gain_h, in_gain), (bias_h, bias), (log_h, log), (skip_h, skip_gain)]
    params = len(moves)
    for piece in range(3):
        rows = pl.ds(piece * 16, 16)
        for source, begin, width in ((state_h.at[rows, pl.ds(pl.multiple_of(z_hi * 128, 128), 128)], 0, 128), (main_h.at[rows, pl.ds(768, 768)], 256, 768),
                                     (main_h.at[rows, pl.ds(0, 768)], 1024, 768), (out_h.at[rows], 1792, 768)):
            moves.append((source, own_unit.at[piece, :, pl.ds(begin, width)]))
    moves = [pltpu.make_async_copy(a, b, local.at[i]) for i, (a, b) in enumerate(moves)]
    for c in moves:
        c.start()
    moves[0].wait()
    step_rows = jnp.concatenate([step_w[...].astype(F32), jnp.zeros((116, 48), F32)], axis=0).T.astype(BF16)
    for piece in range(3):
        w[units(at, "") + (piece, slice(None), pl.ds(128, 128))] = step_rows[piece * 16:(piece + 1) * 16]
    for c in moves[params:]:
        c.wait()
    entered()

    def part(where, piece, stage, chunk):
        begin, width = STAGED[chunk] if stage == 2 else (0, COLS)
        return w.at[units(where, ORDERS[piece][:stage]) + (piece, slice(None), pl.ds(begin, width))]

    def flight(piece, stage, chunk, kind):
        axis, by = ORDERS[piece][stage], (1, 3)[kind % 2]
        width = STAGED[chunk][1] if stage == 2 else COLS
        if kind < 2:
            target = source = part(at, piece, stage, chunk)
        else:
            target = source = half_of(part(moved(at, axis, -by), piece, stage, chunk), 2 - stage, piece, width, kind - 2)
        sem = (stage + chunk if stage == 2 else stage, piece, kind)
        return pltpu.make_async_remote_copy(src_ref=source, dst_ref=target, send_sem=send.at[sem], recv_sem=recv.at[sem],
                                            device_id=device_at(moved(at, axis, by)), device_id_type=MESH)

    def fulls(stage, chunk=0):
        for piece in range(3):
            if stage > 0 and chunk == 0:
                for kind in (2, 3):
                    flight(piece, stage - 1, 0, kind).wait_recv()
            for kind in (0, 1):
                flight(piece, stage, chunk, kind).start()

    def halves(stage, chunk=0):
        for piece in range(3):
            for kind in (0, 1):
                flight(piece, stage, chunk, kind).wait_recv()
                flight(piece, stage, chunk, kind + 2).start()

    def arrived(chunk):
        for piece in range(3):
            for kind in (2, 3):
                flight(piece, 2, chunk, kind).wait_recv()

    fulls(0)
    for c in moves[1:params]:
        c.wait()

    prm[z_hi] = jnp.zeros((16, 768), F32)
    prm[z_hi, 0:4, :] = cinner[...]
    prm[z_hi, 4:5, :] = offset[...].reshape(1, 768)
    prm[z_hi, 5:6, :] = gain[...].reshape(1, 768)
    for i, ref in enumerate((bias, log, skip_gain)):
        prm[z_hi, 6 + i:7 + i, 0:12] = ref[...].reshape(1, 12)
    h = hidden[...].astype(F32)
    scale = lax.rsqrt(jnp.mean(h * h, axis=1, keepdims=True) + EPS)
    x[mine, :] = (h * scale * in_gain[...].reshape(1, 1536)).astype(BF16)
    swaps = [pltpu.make_async_remote_copy(src_ref=s, dst_ref=s, send_sem=swap_send.at[i], recv_sem=swap_recv.at[i],
                                          device_id=device_at(to), device_id_type=MESH)
             for i, (s, to) in enumerate([(x.at[mine], mate), (g.at[mine], mate), (prm.at[z_hi], far)])]
    for c in swaps:
        c.start()
    spar[...] = jnp.concatenate([cstate[...], state_offset[...].reshape(1, 256), jnp.zeros((11, 256), F32)], axis=0).T

    halves(0)
    fulls(1)
    out_copies = []

    def put(i, source, target):
        c = pltpu.make_async_copy(source, target, out_sem.at[i])
        c.start()
        out_copies.append(c)

    for c in swaps[:2]:
        c.wait_recv()
    xt[...] = x[...].T
    gt[...] = g[...].T
    put(0, xt, xt_o)
    put(1, gt, gt_o)
    halves(1)
    swaps[2].wait_recv()
    acc[...] = jnp.zeros_like(acc)
    cumc[...] = jnp.zeros_like(cumc)
    fulls(2, 0)
    fulls(2, 1)
    halves(2, 0)
    halves(2, 1)
    fulls(2, 2)
    arrived(0)
    put(2, w.at[:, :, :, :, :, :, pl.ds(0, 256)], wst_o)

    def weight(zh, begin):
        return w[zh, :, :, :, :, :, pl.ds(begin, WIDE)].reshape(1536, WIDE)

    for zh in range(2):
        raw = dot(x[...], weight(zh, 0)).T.astype(BF16)
        statet[zh * 128:(zh + 1) * 128, :] = raw[:128]
        stept[zh * 16:(zh + 1) * 16, :] = raw[128:144]
    for q in range(4):
        r = slice(q * 64, (q + 1) * 64)
        p, _ = conv(statet[r, :].astype(F32), spar[r])
        bct[r, :] = (p * sig(p)).astype(BF16)
    bc[...] = bct[...].T
    upper = tri(SPAN, lambda r, c: r <= c)
    for b in range(2):
        rows = pl.ds(b * SPAN, SPAN)
        cbt[b] = dot(bc[rows, 0:128], bc[rows, 128:256], 1, 1) * upper.astype(F32)
    for zh in range(2):
        cols = prm[zh, :, 0:128].T
        v = stept[zh * 16:(zh + 1) * 16, :].astype(F32) + cols[:16, 6:7]
        dt = jnp.maximum(v, 0.0) + jnp.log1p(jnp.exp(-jnp.abs(v)))
        dtt[zh * 16:(zh + 1) * 16, :] = dt
        la = dt * -jnp.exp(cols[:16, 7:8])
        for b in range(2):
            cumt[zh * 16:(zh + 1) * 16, b * SPAN:(b + 1) * SPAN] = exact_dot(la[:, b * SPAN:(b + 1) * SPAN], upper)
    cumc[...] = jnp.concatenate([cumt[...], jnp.zeros((96, T), F32)], axis=0).T
    for i, ref in enumerate((dtt, cumt, cumc, stept, statet, bc, bct, cbt, prm, spar)):
        put(10 + i, ref, small_o[1 + i])

    def put_weights(kind, begin):
        for n in range(8):
            zh, q = n % 2, n // 2
            pltpu.make_async_copy(w.at[zh, q, :, :, :, :, pl.ds(begin, 768)], w_o.at[kind, q, zh], w_sem.at[kind]).start()

    arrived(1)
    put_weights(2, 256)

    @pl.loop(0, 6)
    def _(n):
        zh, c, off, base = group_at(n)
        cols = group_cols(prm, zh, c)
        skip = group_skip(prm, zh, c)
        cc = pltpu.roll(cumc[...], 128 - base, 1)
        ut[pl.ds(off, WIDE), :] = dot(x[...], weight(zh, pl.multiple_of(256 + c * WIDE, WIDE))).T.astype(BF16)
        for i in range(GROUP):
            r = slice(i * HEAD, (i + 1) * HEAD)
            rows = pl.ds(pl.multiple_of(off + i * HEAD, HEAD), HEAD)
            p, _ = conv(ut[rows, :].astype(F32), cols[r])
            sp = sig(p)
            xs = p * sp
            xsb = xs.astype(BF16)
            xst[rows, :] = xsb
            dsil[rows, :] = (sp + xs * (1.0 - sp)).astype(BF16)
            xs = xsb.astype(F32)
            cum = cumt[pl.ds(base + i, 1), :]
            xdt = xs * dtt[pl.ds(base + i, 1), :]
            xdtb = xdt.astype(BF16)
            ys = []
            for b in range(2):
                m = (decay(cum, cc[b * SPAN:(b + 1) * SPAN, i:i + 1], b) * cbt[b]).astype(BF16)
                ys.append(dot(xdtb[:, b * SPAN:(b + 1) * SPAN], m))
            tail = jnp.exp(cum[:, SPAN - 1:SPAN] - cum[:, :SPAN])
            state = dot((xdt[:, :SPAN] * tail).astype(BF16), bc[0:SPAN, 0:128]).astype(BF16)
            ys[1] = ys[1] + jnp.exp(cum[:, SPAN:]) * dot(state, bc[SPAN:, 128:256], 1, 1)
            yt[rows, :] = jnp.concatenate(ys, axis=1) + skip[i:i + 1, 0:1] * xs

        @pl.when(n == 2)
        def _():
            halves(2, 2)
            fulls(2, 3)

    put(3, xst, xst_o)
    put(4, yt, yt_o)
    put(5, ut, ut_o)
    put(9, dsil, dsil_o)
    arrived(2)
    put_weights(1, 1024)

    @pl.loop(0, 6)
    def _(n):
        zh, c, off, _ = group_at(n)
        zt[pl.ds(off, WIDE), :] = dot(x[...], weight(zh, pl.multiple_of(1024 + c * WIDE, WIDE))).T.astype(BF16)
        for i in range(GROUP):
            rows = pl.ds(pl.multiple_of(off + i * HEAD, HEAD), HEAD)
            z = zt[rows, :].astype(F32)
            vb = (yt[rows, :] * (z * sig(z))).astype(BF16)
            vt[rows, :] = vb
            v = vb.astype(F32)
            acc[0:1, :] += jnp.sum(v * v, axis=0, keepdims=True)

        @pl.when(n == 3)
        def _():
            halves(2, 3)

    put(6, zt, zt_o)
    put(7, vt, vt_o)
    arrived(3)
    put_weights(0, 1792)

    @pl.loop(0, 6)
    def _(n):
        zh, c, off, _ = group_at(n)
        cols = group_cols(prm, zh, c)
        dgt[pl.ds(off, WIDE), :] = dot(g[...], weight(zh, pl.multiple_of(1792 + c * WIDE, WIDE))).T.astype(BF16)
        for i in range(GROUP):
            rows = pl.ds(pl.multiple_of(off + i * HEAD, HEAD), HEAD)
            s = dgt[rows, :].astype(F32) * cols[i * HEAD:(i + 1) * HEAD, 5:6] * vt[rows, :].astype(F32)
            acc[1:2, :] += jnp.sum(s, axis=0, keepdims=True)

    c = pltpu.make_async_remote_copy(src_ref=acc, dst_ref=acc_in, send_sem=swap_send.at[3], recv_sem=swap_recv.at[3],
                                     device_id=device_at(mate), device_id_type=MESH)
    c.start()
    put(8, dgt, dgt_o)
    for piece in range(3):
        for kind in range(4):
            for stage in range(2):
                flight(piece, stage, 0, kind).wait_send()
            for chunk in range(4):
                flight(piece, 2, chunk, kind).wait_send()
    for s in swaps:
        s.wait_send()
    c.wait()
    sums[...] = acc[...] + acc_in[...]
    put(20, sums, small_o[0])
    for kind in range(3):
        pltpu.make_async_copy(w_o.at[kind], w_o.at[kind], w_sem.at[kind]).wait()
    for c in out_copies:
        c.wait()


def forward(main, step_w, *others):
    any_ = pl.BlockSpec(memory_space=pl.ANY)
    dma = pltpu.SemaphoreType.DMA
    tall = [sds((1536, T), BF16)] * 8 + [sds((1536, T))]
    big = tall + [sds((3, 4, 2, 4, 2, 3, 16, 768), BF16), sds((2, 4, 4, 2, 3, 16, 256), BF16)]
    small = [sds((8, T)), sds((32, T)), sds((32, T)), sds((T, 128)), sds((32, T), BF16), sds((256, T), BF16), sds((T, 256), BF16),
             sds((256, T), BF16), sds((2, SPAN, SPAN)), sds((2, 16, 768)), sds((256, 16))]
    return pl.pallas_call(
        forward_kernel, out_shape=big + small, in_specs=[any_] * (2 + len(others)), out_specs=[any_] * 22,
        scratch_shapes=[pltpu.VMEM(a.shape, a.dtype) for a in (step_w, others[2], *others[4:])] + [
                        pltpu.VMEM((2, 4, 4, 2, 3, 16, COLS), BF16), pltpu.VMEM((T, 1536), BF16),
                        pltpu.VMEM((T, 1536), BF16)] + [pltpu.VMEM(s.shape, s.dtype) for s in tall] + [
            pltpu.VMEM((8, T), F32), pltpu.VMEM((8, T), F32)] + [pltpu.VMEM(s.shape, s.dtype) for s in small] + [
            dma((6, 3, 4)), dma((6, 3, 4)), dma((25,)), dma((3,)), dma((21,)), dma((4,)), dma((4,))],
        compiler_params=pltpu.CompilerParams(collective_id=0, has_side_effects=True, vmem_limit_bytes=60 << 20),
    )(main, step_w, *others)


SCAN_STEPS = {6: [(0, 2)], 9: [(1, 1)]}
CONV_STEPS = {0: [(0, 3)], 1: [(4, 0)], 2: [(1, 2)], 3: [(2, 0), (0, 4)], 4: [(4, 1), (0, 5)], 5: [(3, 0), (1, 3)]}
TOKEN_STEPS = {0: [(2, 1), (4, 2)], 1: [(0, 6), (1, 4)], 2: [(3, 1), (4, 3)], 3: [(2, 2), (1, 5)]}
REST = [(4, 4), (3, 2), None, (2, 3), (4, 5), (1, 6), (3, 3), None, (4, 6), None, (2, 4), (3, 4), None, (2, 5), (3, 5), (2, 6), (3, 6)]


def add_into(target, *others):
    def add(t, o):
        v = t[...].astype(F32)
        for other in o:
            v = v + other[...].astype(F32)
        t[...] = v.astype(BF16)
    if len(target.shape) == 2:
        add(target, others)
    else:
        @pl.loop(0, target.shape[0])
        def _(i):
            add(target.at[i], [o.at[i] for o in others])


def backward_kernel(xt_h, gt_h, zt_h, ut_h, dgt_h, vt_h, xst_h, dsil_h, yt_h, w_h, wst_h,
                    *rest_refs):
    small_h, outs_h, scratch = rest_refs[:14], rest_refs[14:19], rest_refs[19:]
    n = len(RCHUNKS)
    part, regions, halves = scratch[0], scratch[1:1 + 9 * n], scratch[1 + 9 * n:1 + 18 * n]
    (xt, gt, zt, dgt, vt, gat, yt, wbuf, wst, total, dcbt, ld, dye_all, xe_all, st_all, ds_all, cross, prow, hrow,
     dcum, ddt1, gskip, dstep_t, dbct, dbct_in, dn_in, branch, br_in, dstate, dst, folds,
     sums, dtt, cumt, cumc, stept, statet, bc, bct, cbt, prm, spar, hidden, cot, gain, out, gstate, gsmall, new_hidden, grad_hidden, vec, vec_in, own_state, ggain, gain_in, quarter, quarters,
     send, recv, load_sem, w_sem, swap_send, swap_recv, vec_send, vec_recv, q_send, q_recv, out_sem) = scratch[1 + 18 * n:]
    xst, ut, dyt, dzt, dsil, dut = gt, vt, zt, dgt, gat, zt
    at = place()
    mate = {**at, "core": 1 - at["core"]}
    far = moved(at, "z", 2)
    far_mate = {**far, "core": 1 - at["core"]}
    entered = greet([moved(at, axis, by) for axis in "xyz" for by in (1, 2, 3)] + [mate, far_mate])
    mine = pl.ds(pl.multiple_of(at["core"] * 256, 256), 256)
    theirs = pl.ds(pl.multiple_of((1 - at["core"]) * 256, 256), 256)

    loads = [pltpu.make_async_copy(s, d, load_sem.at[i]) for i, (s, d) in enumerate(
        [(vt_h, vt), (gt_h, gt), (yt_h, yt), (zt_h, zt), (dgt_h, dgt), (xt_h, xt), (xst_h, xst), (ut_h, ut), (wst_h, wst), (dsil_h, dsil)]
        + list(zip(small_h, (sums, dtt, cumt, cumc, stept, statet, bc, bct, cbt, prm, spar, hidden, cot, gain))))]
    first = [loads[i] for i in (10, 19, 0, 1)]
    second = loads[2:6] + loads[8:9] + loads[11:19] + loads[20:]
    out_copies = []

    def put(i, source):
        c = pltpu.make_async_copy(source, outs_h[i], out_sem.at[i])
        c.start()
        out_copies.append(c)

    def weights(i):
        late = i >= 4
        return pltpu.make_async_copy(w_h.at[jnp.where(late, 1 + i % 2, 0), jnp.where(late, (i - 4) // 2, i)], wbuf.at[i % 2], w_sem.at[i % 2])

    def product(i, values):
        weights(i).wait()

        @pl.when(i + 1 < 12)
        def _():
            weights(i + 1).start()
        return (dot(wbuf[i % 2, 0].reshape(384, 768), values[0:768, :]) + dot(wbuf[i % 2, 1].reshape(384, 768), values[768:1536, :])).T

    for c in first:
        c.start()
    weights(0).start()
    for c in second:
        c.start()

    def remote(src, dst_ref, s, r, to):
        return pltpu.make_async_remote_copy(src_ref=src, dst_ref=dst_ref, send_sem=s, recv_sem=r, device_id=device_at(to), device_id_type=MESH)

    def block(where, chunk, piece, stage):
        begin, width = RCHUNKS[chunk]
        return part.at[units(where, ORDERS[piece][:2 - stage]) + (piece, slice(None), pl.ds(begin, width))]

    def whole(chunk, stage):
        return stage == 2 and RCHUNKS[chunk][1] <= 128

    def slot(chunk, piece, stage):
        return (chunk * 3 + piece) * 3 + stage

    def start(chunk, piece, stage, i):
        axis = ORDERS[piece][2 - stage]
        k = slot(chunk, piece, stage)
        right, left, opposite = moved(at, axis, 1), moved(at, axis, 3), moved(at, axis, 2)
        cut = lambda ref, h: half_of(ref, stage, piece, RCHUNKS[chunk][1], h)
        own = lambda where: block(where, chunk, piece, stage)
        src, dst_ref, to = (
            lambda: (cut(own(opposite), 0), halves[k].at[0], right),
            lambda: (cut(own(opposite), 1), halves[k].at[1], left),
            lambda: (cut(own(right), 1), cut(regions[k].at[0], 1), right),
            lambda: (cut(own(left), 0), cut(regions[k].at[1], 0), left),
            lambda: (cut(own(right), 0), cut(regions[k].at[0], 0), right),
            lambda: (cut(own(left), 1), cut(regions[k].at[1], 1), left))[i]()
        remote(src, dst_ref, send.at[chunk, piece, int(i > 1)], recv.at[chunk, piece, stage, int(i > 1)], to).start()

    def took(buffer, sem):
        pltpu.make_async_copy(buffer, buffer, sem).wait()

    def kinds(chunk, stage):
        return ((0,), (3,), (4,)) if whole(chunk, stage) else ((0, 1), (2, 3), (4, 5))

    def sent(chunk, piece, stage):
        k = slot(chunk, piece, stage)
        took(halves[k], send.at[chunk, piece, 0])
        took(regions[k], send.at[chunk, piece, 1])

    def step(chunk, k):
        for piece in range(3):
            stage = k // 2
            if k % 2:
                first, _, last = kinds(chunk, stage)
                took(halves[slot(chunk, piece, stage)], recv.at[chunk, piece, stage, 0])
                axis = ORDERS[piece][2 - stage]
                for j in last:
                    mid = half_of(block(moved(at, axis, 1 if j == 4 else 3), chunk, piece, stage), stage, piece, RCHUNKS[chunk][1], j - 4)
                    add_into(mid, halves[slot(chunk, piece, stage)].at[j - 4])
                    start(chunk, piece, stage, j)
            else:
                if k > 0:
                    s = slot(chunk, piece, stage - 1)
                    took(regions[s], recv.at[chunk, piece, stage - 1, 1])
                    add_into(block(at, chunk, piece, stage - 1), regions[s].at[0], regions[s].at[1])
                    sent(chunk, piece, stage - 1)
                if k < 6:
                    first, second, _ = kinds(chunk, stage)
                    for i in first + second:
                        start(chunk, piece, stage, i)

    def steps_after(table, index):
        for i, todo in table.items():
            @pl.when(index == i)
            def _(todo=todo):
                for chunk, k in todo:
                    step(chunk, k)

    def gradients(left, right, zh, col):
        for q in range(4):
            value = dot(left[q * 384:(q + 1) * 384, :], right, 1, 1).astype(BF16)
            part[zh, q, :, :, :, :, pl.ds(col, right.shape[0])] = value.reshape(4, 2, 3, 16, right.shape[0])

    def strip(q):
        return pl.ds(pl.multiple_of(q * 384, 128), 384)

    def fold(v):
        return v[:, 0:128] + v[:, 128:256] + v[:, 256:384] + v[:, 384:512]

    def row_sums(v):
        ones = jnp.ones((8, 128), BF16)
        a, b, _ = split(v)
        return (dot(ones, a, 1, 1) + dot(ones, b, 1, 1))[0:1]

    for ref in (dcbt, cross, dcum, ddt1, gskip, vec, ggain):
        ref[...] = jnp.zeros_like(ref)
    for c in first:
        c.wait()
    r_out = lax.rsqrt(sums[0:1, :] / INNER + EPS)
    k2 = r_out * r_out * r_out * sums[1:2, :] / INNER


    @pl.loop(0, 6)
    def _(m):
        zh, c, off, _ = group_at(m)
        cols = group_cols(prm, zh, c)
        group = pl.ds(off, WIDE)
        for i in range(GROUP):
            r = slice(i * HEAD, (i + 1) * HEAD)
            rows = pl.ds(pl.multiple_of(off + i * HEAD, HEAD), HEAD)
            gat[rows, :] = (vt[rows, :].astype(F32) * r_out * cols[r, 5:6]).astype(BF16)
        gradients(gt, gat[group, :], zh, pl.multiple_of(c * WIDE, WIDE))

    loads[6].start()
    entered()
    step(0, 0)
    for c in second:
        c.wait()

    @pl.loop(0, 6)
    def _(m):
        zh, c, off, _ = group_at(m)
        cols = group_cols(prm, zh, c)
        group = pl.ds(off, WIDE)
        for i in range(GROUP):
            r = slice(i * HEAD, (i + 1) * HEAD)
            rows = pl.ds(pl.multiple_of(off + i * HEAD, HEAD), HEAD)
            z = zt[rows, :].astype(F32)
            dg = dgt[rows, :].astype(F32)
            v = vt[rows, :].astype(F32)
            sz = sig(z)
            zs = z * sz
            dv = dg * cols[r, 5:6] * r_out - v * k2
            folds[0, r, :] = fold(dg * v * r_out)
            dyt[rows, :] = (dv * zs).astype(BF16)
            dzt[rows, :] = (dv * yt[rows, :] * (sz + zs * (1.0 - sz))).astype(BF16)
        prow[zh * 3 + c, 5:6, :] = row_sums(folds[0])
        gradients(xt, dzt[group, :], zh, pl.multiple_of(768 + c * WIDE, WIDE))

    loads[7].start()
    step(0, 1)
    step(1, 0)

    @pl.loop(0, 4)
    def _(q):
        branch[:, strip(q)] = product(q, gat).astype(BF16)

    swap_br = remote(branch.at[theirs], br_in, swap_send.at[0], swap_recv.at[0], mate)
    swap_br.start()

    loads[9].start()
    loads[6].wait()

    @pl.loop(0, 6)
    def _(m):
        zh, c, off, base = group_at(m)
        cc = pltpu.roll(cumc[...], 128 - base, 1)
        skips = group_skip(prm, zh, c)
        for i in range(GROUP):
            r = slice(i * HEAD, (i + 1) * HEAD)
            rows = pl.ds(pl.multiple_of(off + i * HEAD, HEAD), HEAD)
            skip = skips[i:i + 1, 0:1]
            xs = xst[rows, :].astype(F32)
            dyb = dyt[rows, :]
            dy = dyb.astype(F32)
            yssm = yt[rows, :] - skip * xs
            gskip[pl.ds(base + i, 1), :] = jnp.sum(dy * xs, axis=0, keepdims=True)
            dt = dtt[pl.ds(base + i, 1), :]
            cum = cumt[pl.ds(base + i, 1), :]
            xdt = xs * dt
            xdtb = xdt.astype(BF16)
            dxs = []
            for b in range(2):
                s = slice(b * SPAN, (b + 1) * SPAN)
                w = decay(cum, cc[s, i:i + 1], b)
                dxs.append(dot(dyb[:, s], (w * cbt[b]).astype(BF16), 1, 1))
                dcbt[b] += dot(xdtb[:, s], dyb[:, s], 0, 0) * w
            tail = jnp.exp(cum[:, SPAN - 1:SPAN] - cum[:, :SPAN])
            xe = (xdt[:, :SPAN] * tail).astype(BF16)
            dye = (dy[:, SPAN:] * jnp.exp(cum[:, SPAN:])).astype(BF16)
            ds = dot(dye, bc[SPAN:, 128:256]).astype(BF16)
            xe_all[r, :] = xe
            dye_all[r, :] = dye
            st_all[r, :] = dot(xe, bc[0:SPAN, 0:128]).astype(BF16)
            ds_all[r, :] = ds
            dxs[0] = dxs[0] + tail * dot(ds, bc[0:SPAN, 0:128], 1, 1)
            dx = jnp.concatenate(dxs, axis=1)
            dcum[pl.ds(base + i, 1), :] = jnp.sum(dy * yssm - xdtb.astype(F32) * dx, axis=0, keepdims=True)
            ddt1[pl.ds(base + i, 1), :] = jnp.sum(xs * dx, axis=0, keepdims=True)
            dyt[rows, :] = (dt * dx + skip * dy).astype(BF16)
            if i % 2:
                steps_after(SCAN_STEPS, m * 2 + i // 2)
        cross[1] += dot(st_all[...], dye_all[...], 0, 0)
        cross[0] += dot(ds_all[...], xe_all[...], 0, 0)

    upper = tri(SPAN, lambda r, c: r <= c).astype(F32)
    for b in range(2):
        s = slice(b * SPAN, (b + 1) * SPAN)
        d = (dcbt[b] * upper).astype(BF16)
        db = dot(bct[128:256, s], d, 1, 1)
        dc = dot(bct[0:128, s], d)
        dbct[0:128, s] = (db + cross[0] if b == 0 else db).astype(BF16)
        dbct[128:256, s] = (dc + cross[1] if b == 1 else dc).astype(BF16)
    swap_bc = remote(dbct, dbct_in, swap_send.at[1], swap_recv.at[1], mate)
    swap_bc.start()

    dla = exact_dot(dcum[...], tri(T, lambda r, c: r >= c))
    for zh in range(2):
        rows = slice(zh * 16, (zh + 1) * 16)
        hc = prm[zh, :, 0:128].T
        rate = -jnp.exp(hc[:16, 7:8])
        d = dla[rows]
        dstep = (ddt1[rows, :] + rate * d) * sig(stept[rows, :].astype(F32) + hc[:16, 6:7])
        gd = jnp.sum(d * dtt[rows, :] * rate, axis=1, keepdims=True)
        hcol = jnp.concatenate([jnp.sum(dstep, axis=1, keepdims=True), gd, jnp.sum(gskip[rows, :], axis=1, keepdims=True),
                                jnp.zeros((16, 125), F32)], axis=1)
        hrow[:, zh * 128:(zh + 1) * 128] = jnp.concatenate([hcol, jnp.zeros((112, 128), F32)], axis=0).T[:8]
        keep = lax.broadcasted_iota(jnp.int32, (16, T), 0) < 12
        dstep_t[zh, 0:16, :] = jnp.where(keep, dstep, 0.0).astype(BF16)
        dstep_t[zh, 16:128, :] = jnp.zeros((112, T), BF16)

    loads[7].wait()
    loads[9].wait()

    def convolution(m):
        zh, c, off, _ = group_at(m)
        cols = group_cols(prm, zh, c)
        for i in range(GROUP):
            r = slice(i * HEAD, (i + 1) * HEAD)
            rows = pl.ds(pl.multiple_of(off + i * HEAD, HEAD), HEAD)
            u = ut[rows, :].astype(F32)
            dp = dyt[rows, :].astype(F32) * dsil[rows, :].astype(F32)
            du = cols[r, 0:1] * dp
            folds[0, r, :] = fold(u * dp)
            folds[4, r, :] = fold(dp)
            for k in range(1, 4):
                ahead = sooner(dp, k)
                du = du + cols[r, k:k + 1] * ahead
                folds[k, r, :] = fold(u * ahead)
            dut[rows, :] = du.astype(BF16)
        for k in range(5):
            prow[zh * 3 + c, k:k + 1, :] = row_sums(folds[k])
        gradients(xt, dut[pl.ds(off, WIDE), :], zh, pl.multiple_of(1536 + c * WIDE, WIDE))

    def state_back():
        swap_bc.wait_recv()
        for q in range(4):
            r = slice(q * 64, (q + 1) * 64)
            cols = spar[r]
            p, shifted = conv(statet[r, :].astype(F32), cols)
            sp = sig(p)
            dp = (dbct[r, :].astype(F32) + dbct_in[r, :].astype(F32)) * (sp + p * sp * (1.0 - sp))
            dstate[r, :] = conv_back(dp, cols).astype(BF16)
            dst[r, :] = jnp.concatenate([jnp.sum(dp * shifted[k], axis=1, keepdims=True) for k in range(4)]
                                        + [jnp.sum(dp, axis=1, keepdims=True), jnp.zeros((64, 123), F32)], axis=1)
        vec[48:56, :] = dst[...].T[:8]
        for zh in range(2):
            ld[0:64, :] = dstate[pl.ds(zh * 128 + pl.multiple_of(at["core"] * 64, 64), 64), :]
            ld[64:128, :] = dstep_t[zh, 0:64, :]
            gradients(xt, ld[...], zh, 2304)

    @pl.loop(0, 6)
    def _(m):
        convolution(m)

        @pl.when(m == 1)
        def _():
            state_back()
        steps_after(CONV_STEPS, m)

    @pl.loop(0, 4)
    def _(q):
        more = [dot(wst[zh, q, :, :, :, :, pl.ds(128, 128)].reshape(384, 128), dstep_t[zh]) for zh in range(2)]
        total[:, strip(q)] = product(4 + 2 * q, dzt) + product(5 + 2 * q, dut) + (more[0] + more[1]).T
        steps_after(TOKEN_STEPS, q)

    swap_br.wait()
    for q in range(4):
        branch[theirs, strip(q)] = total[theirs, strip(q)].astype(BF16)
    swap_dn = remote(branch.at[theirs], dn_in, swap_send.at[2], swap_recv.at[2], mate)
    swap_dn.start()
    rest = list(REST)

    def go():
        while rest and rest[0] is not None:
            step(*rest.pop(0))
        rest[:1] = []

    go()
    own_state[...] = dstate[:, mine].T
    swap_dn.wait_recv()

    @pl.loop(0, 2)
    def _(q):
        r = pl.ds(pl.multiple_of(q * 128, 128), 128)
        full = total[pl.ds(pl.multiple_of(at["core"] * 256 + q * 128, 128), 128), :] + dn_in[r, :].astype(F32)
        for zh in range(2):
            full = full + dot(own_state[r, zh * 128:(zh + 1) * 128], wst[zh, :, :, :, :, :, pl.ds(0, 128)].reshape(1536, 128), 1, 1)
        h = hidden[r, :].astype(F32)
        r_in = lax.rsqrt(jnp.mean(h * h, axis=1, keepdims=True) + EPS)
        ggain[...] += jnp.sum(full * h * r_in, axis=0, keepdims=True)
        scaled = full * gain[...].reshape(1, 1536)
        back = scaled * r_in - h * (r_in * r_in * r_in * (jnp.sum(scaled * h, axis=1, keepdims=True) / 1536))
        grad_hidden[r, :] = (cot[r, :].astype(F32) + back).astype(BF16)

    for q in range(6):
        vec[q * 8:(q + 1) * 8, :] = prow[q]
        vec[56 + q:57 + q, :] = ggain[:, q * 256:(q + 1) * 256]
    vec[64:72, :] = hrow[...]

    def vec_flights(s):
        return [remote(vec, vec_in.at[s, by - 1], vec_send.at[s, by - 1], vec_recv.at[s, by - 1], moved(at, "xyz"[s], by)) for by in (1, 2, 3)]

    def vec_end(s):
        for c in vec_flights(s):
            c.wait()
        vec[...] = vec[...] + vec_in[s, 0] + vec_in[s, 1] + vec_in[s, 2]

    def vec_start(s):
        for c in vec_flights(s):
            c.start()

    vec_start(0)
    put(4, grad_hidden)

    @pl.loop(0, 2)
    def _(q):
        r = pl.ds(pl.multiple_of(q * 128, 128), 128)
        new_hidden[r, :] = (hidden[r, :].astype(F32) + branch[pl.ds(pl.multiple_of(at["core"] * 256 + q * 128, 128), 128), :].astype(F32) + br_in[r, :].astype(F32)).astype(BF16)

    put(3, new_hidden)
    go()
    vec_end(0)
    vec_start(1)
    go()
    vec_end(1)
    vec_start(2)
    go()
    own = units(at, "")
    last = RCHUNKS[n - 1][0]
    for piece in range(3):
        quarter[piece * 16:(piece + 1) * 16, :] = part[own + (piece, slice(None), pl.ds(last, 128))].astype(F32)
    thirds = [remote(quarter, quarters.at[i], q_send.at[i], q_recv.at[i], to) for i, to in enumerate((mate, far, far_mate))]
    for c in thirds:
        c.start()
    go()
    vec_end(2)
    final = remote(vec.at[pl.ds(56, 8)], gain_in, q_send.at[3], q_recv.at[3], mate)
    final.start()
    go()
    for piece in range(3):
        out[piece * 16:(piece + 1) * 16, :] = part[own + (piece, slice(None), pl.ds(0, 2304))].astype(F32)
    put(0, out)
    gsmall[...] = vec[...]
    final.wait()
    gsmall[56:64, :] = vec[56:64, :] + gain_in[...]
    put(2, gsmall)
    for c in thirds:
        c.wait()
    low = at["core"] == 0
    q0, q1, q2, q3 = quarter[...], quarters[0], quarters[1], quarters[2]
    here = jnp.where(low, jnp.concatenate([q0[:, :64], q1[:, :64]], axis=1), jnp.concatenate([q1[:, :64], q0[:, :64]], axis=1))
    there = jnp.where(low, jnp.concatenate([q2[:, :64], q3[:, :64]], axis=1), jnp.concatenate([q3[:, :64], q2[:, :64]], axis=1))
    first = at["z"] < 2
    gstate[:, 0:128] = jnp.where(first, here, there)
    gstate[:, 128:256] = jnp.where(first, there, here)
    gstate[:, 256:384] = q0
    put(1, gstate)
    for s in (swap_bc, swap_dn):
        s.wait_send()
    for c in out_copies:
        c.wait()


def backward(tall, small, hidden, cot, gain):
    n = len(RCHUNKS)
    results = [sds((48, 2304)), sds((48, 384)), sds((SUMS, 256)), sds((256, 1536), BF16), sds((256, 1536), BF16)]
    any_ = pl.BlockSpec(memory_space=pl.ANY)
    shapes = [(stage, piece, RCHUNKS[chunk][1]) for chunk in range(n) for piece in range(3) for stage in range(3)]
    regions = [pltpu.VMEM((2,) + region_shape(*s), BF16) for s in shapes]
    halves = [pltpu.VMEM((1 if s[0] == 2 and s[2] <= 128 else 2,) + half_shape(*s), BF16) for s in shapes]
    dma = pltpu.SemaphoreType.DMA
    v = lambda shape, dtype=F32: pltpu.VMEM(shape, dtype)
    return pl.pallas_call(
        backward_kernel,
        in_specs=[any_] * (len(tall) + len(small) + 3),
        out_specs=[any_] * 5,
        out_shape=results,
        scratch_shapes=[v((2, 4, 4, 2, 3, 16, RCOLS), BF16)] + regions + halves + [
            v((1536, T), BF16)] * 6 + [v((1536, T)), v((2, 2, 4, 2, 3, 16, 768), BF16), v((2, 4, 4, 2, 3, 16, 256), BF16),
            v((T, 1536)), v((2, SPAN, SPAN)), v((128, T), BF16), v((WIDE, SPAN), BF16), v((WIDE, SPAN), BF16),
            v((WIDE, 128), BF16), v((WIDE, 128), BF16), v((2, 128, SPAN)), v((6, 8, WIDE)), v((8, 256)),
            v((32, T)), v((32, T)), v((32, T)), v((2, 128, T), BF16), v((256, T), BF16), v((256, T), BF16),
            v((256, 1536), BF16), v((T, 1536), BF16), v((256, 1536), BF16),
            v((256, T), BF16), v((256, 128)), v((5, WIDE, 128))] + [v(a.shape, a.dtype) for a in (*small, hidden, cot, gain, *results)] + [ v((SUMS, 256)), v((3, 3, SUMS, 256)), v((256, 256), BF16), v((1, 1536)), v((8, 256)), v((48, 128)), v((3, 48, 128)),
            dma((n, 3, 2)), dma((n, 3, 3, 2)), dma((24,)), dma((2,)), dma((3,)), dma((3,)), dma((3, 3)), dma((3, 3)), dma((4,)), dma((4,)), dma((5,))],
        compiler_params=pltpu.CompilerParams(collective_id=1, has_side_effects=True, vmem_limit_bytes=65400 << 10),
    )(*tall, *small, hidden, cot, gain)


def finish_kernel(out, gstate, small, new_h, grad_h, new_hidden, grad_hidden, in_gain, main, step, state, inner, inner_bias, cstate, cstate_bias,
                  bias, log, skip, out_gain, proj_out, sems):
    moves = [pltpu.make_async_copy(a, b, sems.at[i]) for i, (a, b) in enumerate([(new_h, new_hidden), (grad_h, grad_hidden)])]
    for c in moves:
        c.start()
    z_hi = lax.axis_index("tensor") // 2
    proj_out[...] = out[:, 0:768]
    main[:, 0, :] = out[:, 768:1536]
    main[:, 1, :] = out[:, 1536:2304]
    step[...] = gstate[:, 256:384].T[64:76]
    state[...] = gstate[:, 0:256]
    for c in range(3):
        rows = small[pl.ds(pl.multiple_of(z_hi * 24 + c * 8, 8), 8), :]
        cols = slice(c * 256, (c + 1) * 256)
        inner[:, cols] = rows[0:4]
        inner_bias[cols] = rows[4:5].reshape(256)
        out_gain[cols] = rows[5:6].reshape(256)
    cstate[...] = small[48:52, :]
    cstate_bias[...] = small[52:53, :].reshape(256)
    for q in range(6):
        in_gain[q * 256:(q + 1) * 256] = small[56 + q:57 + q, :].reshape(256)
    heads = small[64:72, pl.ds(pl.multiple_of(z_hi * 128, 128), 128)]
    for i, ref in enumerate((bias, log, skip)):
        ref[...] = heads[i:i + 1, 0:12].reshape(12)
    for c in moves:
        c.wait()


def finish(out, gstate, small, new_hidden, grad_hidden):
    vm = pl.BlockSpec(memory_space=pltpu.VMEM)
    any_ = pl.BlockSpec(memory_space=pl.ANY)
    shapes = [sds(s) for s in ((1536,), (48, 2, 768), (12, 48), (48, 256), (4, 768), (768,), (4, 256), (256,), (12,), (12,), (12,), (768,), (48, 768))]
    return pl.pallas_call(
        finish_kernel, out_shape=[sds((256, 1536), BF16)] * 2 + shapes, in_specs=[vm] * 3 + [any_] * 2, out_specs=[any_] * 2 + [vm] * 13,
        scratch_shapes=[pltpu.SemaphoreType.DMA((2,))],
    )(out, gstate, small, new_hidden, grad_hidden)


def per_device(hidden, in_gain, proj_main, proj_step, proj_state, conv_inner, conv_inner_bias, conv_state, conv_state_bias,
               step_bias, decay_log, skip_gain, out_gain, proj_out, grad_out):
    outs = forward(proj_main.reshape(48, 1536), proj_step.T, proj_state, proj_out, hidden, grad_out, conv_inner, conv_state,
                   conv_inner_bias, out_gain, conv_state_bias, in_gain, step_bias, decay_log, skip_gain)
    results = backward(outs[:11], outs[11:], hidden, grad_out, in_gain)
    new_hidden, grad_hidden, ggain, main, step, *others = finish(*results)
    return (new_hidden, grad_hidden, ggain, main, step.T, *others)


def solution(mesh):
    rows = P(("dp", "tensor"), None)
    per_head = P("tensor")
    in_specs = (rows, P(), P("dp", None, "tensor"), P("dp", "tensor"), P("dp", None), P(None, "tensor"), per_head, P(), P(),
                per_head, per_head, per_head, per_head, P("dp", "tensor"), rows)
    out_specs = (rows, rows, P(), P("dp", None, "tensor"), P("dp", "tensor"), P("dp", None), P(None, "tensor"), per_head, P(), P(),
                 per_head, per_head, per_head, per_head, P("dp", "tensor"))
    return jax.shard_map(per_device, mesh=mesh, in_specs=in_specs, out_specs=out_specs, check_vma=False)
```

```python
import functools

import jax
import jax.numpy as jnp
from jax import lax
from jax.experimental import pallas as pl
from jax.experimental.pallas import tpu as pltpu
from jax.sharding import PartitionSpec as P

MESH = pl.DeviceIdType.MESH
F32, BF16 = jnp.float32, jnp.bfloat16
EPS = 1e-5
T, SPAN, HEAD, GROUP = 512, 256, 64, 4
WIDE = GROUP * HEAD
INNER = 3072
COLS = 2560
STAGED = ((0, 256), (256, 768), (1024, 768), (1792, 768))
ORDERS = ("xyz", "yzx", "zxy")
RCHUNKS = ((0, 768), (768, 768), (1536, 768), (2304, 128))
STATE_COL, INNER_COL = 2304, 1536
RCOLS = 2432
SUMS = 64


def sds(shape, dtype=F32):
    return jax.ShapeDtypeStruct(shape, dtype)


def place():
    dp, tp = lax.axis_index("dp"), lax.axis_index("tensor")
    return dict(x=dp // 8, y=(dp // 2) % 4, z=(tp // 2) * 2 + dp % 2, core=tp % 2)


def device_at(at):
    return ((at["x"] * 4 + at["y"]) * 2 + at["z"] % 2, (at["z"] // 2) * 2 + at["core"])


def moved(at, axis, by):
    return {**at, axis: (at[axis] + by) % 4}


def units(at, whole):
    return (slice(None) if "z" in whole else at["z"] // 2, slice(None) if "x" in whole else at["x"],
            slice(None) if "y" in whole else at["y"], slice(None) if "z" in whole else at["z"] % 2)


def greet(others):
    barrier = pltpu.get_barrier_semaphore()
    for other in others:
        pl.semaphore_signal(barrier, inc=1, device_id=device_at(other), device_id_type=MESH)
    return lambda: pl.semaphore_wait(barrier, len(others))


def half_of(ref, stage, piece, width, half):
    if stage == 0:
        return ref.at[pl.ds(2 * half, 2)] if piece == 0 else ref.at[:, pl.ds(2 * half, 2)]
    if stage == 1:
        return ref.at[pl.ds(2 * half, 2)] if piece < 2 else ref.at[half]
    return ref.at[:, pl.ds(half * (width // 2), width // 2)]


def half_shape(stage, piece, width):
    if stage == 0:
        return (2, 4, 16, width) if piece == 0 else (2, 2, 2, 16, width)
    if stage == 1:
        return (2, 16, width)
    return (16, width)


def region_shape(stage, piece, width):
    whole = ORDERS[piece][:2 - stage]
    dims = ([2] if "z" in whole else []) + ([4] if "x" in whole else []) + ([4] if "y" in whole else []) + ([2] if "z" in whole else [])
    return tuple(dims) + (16, width)


def dot(a, b, ca=1, cb=0):
    return lax.dot_general(a, b, (((ca,), (cb,)), ((), ())), preferred_element_type=F32)


def lanes(rows, width=T):
    return lax.broadcasted_iota(jnp.int32, (rows, width), 1)


def later(u, k):
    return jnp.where(lanes(u.shape[0]) >= k, pltpu.roll(u, k, 1), 0.0) if k else u


def sooner(u, k):
    return jnp.where(lanes(u.shape[0]) < T - k, pltpu.roll(u, T - k, 1), 0.0) if k else u


def sig(v):
    return 1.0 / (1.0 + jnp.exp(-v))


def split(v):
    a = v.astype(BF16)
    r = v - a.astype(F32)
    b = r.astype(BF16)
    return a, b, (r - b.astype(F32)).astype(BF16)


def exact_dot(v, ones):
    n = v.shape[0]
    s = dot(jnp.concatenate(split(v), axis=0), ones)
    return s[:n] + s[n:2 * n] + s[2 * n:]


def tri(n, keep):
    r = lax.broadcasted_iota(jnp.int32, (n, n), 0)
    c = lax.broadcasted_iota(jnp.int32, (n, n), 1)
    return jnp.where(keep(r, c), 1.0, 0.0).astype(BF16)


def conv(u, cols):
    shifted = [later(u, k) for k in range(4)]
    p = cols[:, 4:5] + cols[:, 0:1] * shifted[0]
    for k in range(1, 4):
        p = p + cols[:, k:k + 1] * shifted[k]
    return p, shifted


def conv_back(dp, cols):
    du = cols[:, 0:1] * dp
    for k in range(1, 4):
        du = du + cols[:, k:k + 1] * sooner(dp, k)
    return du


def decay(cum_row, cum_col, b):
    return jnp.exp(jnp.minimum(cum_row[:, b * SPAN:(b + 1) * SPAN] - cum_col, 0.0))


def group_at(n):
    zh, c = n % 2, n // 2
    return zh, c, pl.multiple_of((zh * 3 + c) * WIDE, WIDE), zh * 16 + c * GROUP


def group_cols(prm, zh, c):
    return prm[zh, :, pl.ds(pl.multiple_of(c * WIDE, WIDE), WIDE)].T


def group_skip(prm, zh, c):
    cols = prm[zh, :, 0:128].T
    return pltpu.roll(jnp.broadcast_to(cols[:, 8:9], (128, 128)), 128 - c * GROUP, 0)


def forward_kernel(main_h, step_h, state_h, out_h, hidden_h, cot_h, cinner_h, cstate_h, offset_h, gain_h, state_offset_h, in_gain_h, bias_h, log_h, skip_h,
                   xt_o, zt_o, ut_o, dgt_o, vt_o, xst_o, dsil_o, gat_o, yt_o, w_o, wst_o, pa_o,
                   *rest):
    small_o, (step_w, hidden, cinner, cstate, offset, gain, state_offset, in_gain, bias, log, skip_gain, w, x, g, xt, gt, zt, ut, dgt, vt, xst, dsil, gat, yt, pa, acc, acc_in,
              sums, dtt, cumt, cumc, stept, statet, bc, bct, cbt, prm, spar,
              send, recv, local, w_sem, out_sem, swap_send, swap_recv) = rest[:11], rest[11:]
    at = place()
    z_hi = at["z"] // 2
    mate = {**at, "core": 1 - at["core"]}
    far = moved(at, "z", 2)
    entered = greet([moved(at, axis, by) for axis in "xyz" for by in (1, 3)] + [mate, far])
    mine = pl.ds(pl.multiple_of(at["core"] * 256, 256), 256)
    own_unit = w.at[units(at, "")]
    moves = [(step_h, step_w), (hidden_h, hidden), (cot_h, g.at[mine]), (cinner_h, cinner), (cstate_h, cstate), (offset_h, offset), (gain_h, gain),
             (state_offset_h, state_offset), (in_gain_h, in_gain), (bias_h, bias), (log_h, log), (skip_h, skip_gain)]
    params = len(moves)
    for piece in range(3):
        rows = pl.ds(piece * 16, 16)
        for source, begin, width in ((state_h.at[rows, pl.ds(pl.multiple_of(z_hi * 128, 128), 128)], 0, 128), (main_h.at[rows, pl.ds(768, 768)], 256, 768),
                                     (main_h.at[rows, pl.ds(0, 768)], 1024, 768), (out_h.at[rows], 1792, 768)):
            moves.append((source, own_unit.at[piece, :, pl.ds(begin, width)]))
    moves = [pltpu.make_async_copy(a, b, local.at[i]) for i, (a, b) in enumerate(moves)]
    for c in moves:
        c.start()
    moves[0].wait()
    step_rows = jnp.concatenate([step_w[...].astype(F32), jnp.zeros((116, 48), F32)], axis=0).T.astype(BF16)
    for piece in range(3):
        w[units(at, "") + (piece, slice(None), pl.ds(128, 128))] = step_rows[piece * 16:(piece + 1) * 16]
    for c in moves[params:]:
        c.wait()
    entered()

    def part(where, piece, stage, chunk):
        begin, width = STAGED[chunk] if stage == 2 else (0, COLS)
        return w.at[units(where, ORDERS[piece][:stage]) + (piece, slice(None), pl.ds(begin, width))]

    def flight(piece, stage, chunk, kind):
        axis, by = ORDERS[piece][stage], (1, 3)[kind % 2]
        width = STAGED[chunk][1] if stage == 2 else COLS
        if kind < 2:
            target = source = part(at, piece, stage, chunk)
        else:
            target = source = half_of(part(moved(at, axis, -by), piece, stage, chunk), 2 - stage, piece, width, kind - 2)
        sem = (stage + chunk if stage == 2 else stage, piece, kind)
        return pltpu.make_async_remote_copy(src_ref=source, dst_ref=target, send_sem=send.at[sem], recv_sem=recv.at[sem],
                                            device_id=device_at(moved(at, axis, by)), device_id_type=MESH)

    def fulls(stage, chunk=0):
        for piece in range(3):
            if stage > 0 and chunk == 0:
                for kind in (2, 3):
                    flight(piece, stage - 1, 0, kind).wait_recv()
            for kind in (0, 1):
                flight(piece, stage, chunk, kind).start()

    def halves(stage, chunk=0):
        for piece in range(3):
            for kind in (0, 1):
                flight(piece, stage, chunk, kind).wait_recv()
                flight(piece, stage, chunk, kind + 2).start()

    def arrived(chunk):
        for piece in range(3):
            for kind in (2, 3):
                flight(piece, 2, chunk, kind).wait_recv()

    fulls(0)
    for c in moves[1:params]:
        c.wait()

    prm[z_hi] = jnp.zeros((16, 768), F32)
    prm[z_hi, 0:4, :] = cinner[...]
    prm[z_hi, 4:5, :] = offset[...].reshape(1, 768)
    prm[z_hi, 5:6, :] = gain[...].reshape(1, 768)
    for i, ref in enumerate((bias, log, skip_gain)):
        prm[z_hi, 6 + i:7 + i, 0:12] = ref[...].reshape(1, 12)
    h = hidden[...].astype(F32)
    scale = lax.rsqrt(jnp.mean(h * h, axis=1, keepdims=True) + EPS)
    x[mine, :] = (h * scale * in_gain[...].reshape(1, 1536)).astype(BF16)
    swaps = [pltpu.make_async_remote_copy(src_ref=s, dst_ref=s, send_sem=swap_send.at[i], recv_sem=swap_recv.at[i],
                                          device_id=device_at(to), device_id_type=MESH)
             for i, (s, to) in enumerate([(x.at[mine], mate), (g.at[mine], mate), (prm.at[z_hi], far)])]
    for c in swaps:
        c.start()
    spar[...] = jnp.concatenate([cstate[...], state_offset[...].reshape(1, 256), jnp.zeros((11, 256), F32)], axis=0).T

    halves(0)
    fulls(1)
    out_copies = []

    def put(i, source, target):
        c = pltpu.make_async_copy(source, target, out_sem.at[i])
        c.start()
        out_copies.append(c)

    for c in swaps[:2]:
        c.wait_recv()
    xt[...] = x[...].T
    gt[...] = g[...].T
    put(0, xt, xt_o)
    halves(1)
    swaps[2].wait_recv()
    acc[...] = jnp.zeros_like(acc)
    sums[...] = jnp.zeros_like(sums)
    cumc[...] = jnp.zeros_like(cumc)
    fulls(2, 0)
    fulls(2, 1)
    halves(2, 0)
    halves(2, 1)
    fulls(2, 2)
    arrived(0)
    put(2, w.at[:, :, :, :, :, :, pl.ds(0, 256)], wst_o)

    def weight(zh, begin):
        return w[zh, :, :, :, :, :, pl.ds(begin, WIDE)].reshape(1536, WIDE)

    for zh in range(2):
        raw = dot(x[...], weight(zh, 0)).T.astype(BF16)
        statet[zh * 128:(zh + 1) * 128, :] = raw[:128]
        stept[zh * 16:(zh + 1) * 16, :] = raw[128:144]
    for q in range(4):
        r = slice(q * 64, (q + 1) * 64)
        p, _ = conv(statet[r, :].astype(F32), spar[r])
        bct[r, :] = (p * sig(p)).astype(BF16)
    bc[...] = bct[...].T
    upper = tri(SPAN, lambda r, c: r <= c)
    for b in range(2):
        rows = pl.ds(b * SPAN, SPAN)
        cbt[b] = dot(bc[rows, 0:128], bc[rows, 128:256], 1, 1) * upper.astype(F32)
    for zh in range(2):
        cols = prm[zh, :, 0:128].T
        v = stept[zh * 16:(zh + 1) * 16, :].astype(F32) + cols[:16, 6:7]
        dt = jnp.maximum(v, 0.0) + jnp.log1p(jnp.exp(-jnp.abs(v)))
        dtt[zh * 16:(zh + 1) * 16, :] = dt
        la = dt * -jnp.exp(cols[:16, 7:8])
        for b in range(2):
            cumt[zh * 16:(zh + 1) * 16, b * SPAN:(b + 1) * SPAN] = exact_dot(la[:, b * SPAN:(b + 1) * SPAN], upper)
    cumc[...] = jnp.concatenate([cumt[...], jnp.zeros((96, T), F32)], axis=0).T
    for i, ref in enumerate((dtt, cumt, cumc, stept, statet, bc, bct, cbt, prm, spar)):
        put(10 + i, ref, small_o[1 + i])

    def put_weights(kind, begin):
        for n in range(8):
            zh, q = n % 2, n // 2
            pltpu.make_async_copy(w.at[zh, q, :, :, :, :, pl.ds(begin, 768)], w_o.at[kind, q, zh], w_sem.at[kind]).start()

    arrived(1)
    put_weights(2, 256)

    @pl.loop(0, 6)
    def _(n):
        zh, c, off, base = group_at(n)
        cols = group_cols(prm, zh, c)
        skip = group_skip(prm, zh, c)
        cc = pltpu.roll(cumc[...], 128 - base, 1)
        ut[pl.ds(off, WIDE), :] = dot(x[...], weight(zh, pl.multiple_of(256 + c * WIDE, WIDE))).T.astype(BF16)
        for i in range(GROUP):
            r = slice(i * HEAD, (i + 1) * HEAD)
            rows = pl.ds(pl.multiple_of(off + i * HEAD, HEAD), HEAD)
            p, _ = conv(ut[rows, :].astype(F32), cols[r])
            sp = sig(p)
            xs = p * sp
            xsb = xs.astype(BF16)
            xst[rows, :] = xsb
            dsil[rows, :] = (sp + xs * (1.0 - sp)).astype(BF16)
            xs = xsb.astype(F32)
            cum = cumt[pl.ds(base + i, 1), :]
            xdt = xs * dtt[pl.ds(base + i, 1), :]
            xdtb = xdt.astype(BF16)
            ys = []
            for b in range(2):
                m = (decay(cum, cc[b * SPAN:(b + 1) * SPAN, i:i + 1], b) * cbt[b]).astype(BF16)
                ys.append(dot(xdtb[:, b * SPAN:(b + 1) * SPAN], m))
            tail = jnp.exp(cum[:, SPAN - 1:SPAN] - cum[:, :SPAN])
            state = dot((xdt[:, :SPAN] * tail).astype(BF16), bc[0:SPAN, 0:128]).astype(BF16)
            ys[1] = ys[1] + jnp.exp(cum[:, SPAN:]) * dot(state, bc[SPAN:, 128:256], 1, 1)
            yt[rows, :] = jnp.concatenate(ys, axis=1) + skip[i:i + 1, 0:1] * xs

        @pl.when(n == 2)
        def _():
            halves(2, 2)
            fulls(2, 3)

    put(3, xst, xst_o)
    put(4, yt, yt_o)
    put(5, ut, ut_o)
    put(9, dsil, dsil_o)
    arrived(2)
    put_weights(1, 1024)

    @pl.loop(0, 6)
    def _(n):
        zh, c, off, _ = group_at(n)
        zt[pl.ds(off, WIDE), :] = dot(x[...], weight(zh, pl.multiple_of(1024 + c * WIDE, WIDE))).T.astype(BF16)
        for i in range(GROUP):
            rows = pl.ds(pl.multiple_of(off + i * HEAD, HEAD), HEAD)
            z = zt[rows, :].astype(F32)
            vb = (yt[rows, :] * (z * sig(z))).astype(BF16)
            vt[rows, :] = vb
            v = vb.astype(F32)
            acc[0, 0:1, :] += jnp.sum(v * v, axis=0, keepdims=True)

        @pl.when(n == 3)
        def _():
            halves(2, 3)

    put(6, zt, zt_o)
    put(7, vt, vt_o)

    def swap_sums(i):
        c = pltpu.make_async_remote_copy(src_ref=acc.at[i], dst_ref=acc_in.at[i], send_sem=swap_send.at[3 + i], recv_sem=swap_recv.at[3 + i],
                                         device_id=device_at(mate), device_id_type=MESH)
        c.start()
        c.wait()
        sums[i:i + 1, :] = acc[i, 0:1] + acc_in[i, 0:1]

    swap_sums(0)
    r_out = lax.rsqrt(sums[0:1, :] / INNER + EPS)

    @pl.loop(0, 6)
    def _(n):
        zh, c, off, _ = group_at(n)
        cols = group_cols(prm, zh, c)
        for i in range(GROUP):
            rows = pl.ds(pl.multiple_of(off + i * HEAD, HEAD), HEAD)
            gat[rows, :] = (vt[rows, :].astype(F32) * r_out * cols[i * HEAD:(i + 1) * HEAD, 5:6]).astype(BF16)
        value = dot(gt[...], gat[pl.ds(off, WIDE), :], 1, 1).astype(BF16)
        pa[zh, :, :, :, :, :, pl.ds(pl.multiple_of(c * WIDE, WIDE), WIDE)] = value.reshape(4, 4, 2, 3, 16, WIDE)

    put(21, gat, gat_o)
    put(22, pa, pa_o)
    arrived(3)
    put_weights(0, 1792)

    @pl.loop(0, 6)
    def _(n):
        zh, c, off, _ = group_at(n)
        cols = group_cols(prm, zh, c)
        dgt[pl.ds(off, WIDE), :] = dot(g[...], weight(zh, pl.multiple_of(1792 + c * WIDE, WIDE))).T.astype(BF16)
        for i in range(GROUP):
            rows = pl.ds(pl.multiple_of(off + i * HEAD, HEAD), HEAD)
            s = dgt[rows, :].astype(F32) * cols[i * HEAD:(i + 1) * HEAD, 5:6] * vt[rows, :].astype(F32)
            acc[1, 0:1, :] += jnp.sum(s, axis=0, keepdims=True)

    put(8, dgt, dgt_o)
    swap_sums(1)
    put(20, sums, small_o[0])
    for piece in range(3):
        for kind in range(4):
            for stage in range(2):
                flight(piece, stage, 0, kind).wait_send()
            for chunk in range(4):
                flight(piece, 2, chunk, kind).wait_send()
    for s in swaps:
        s.wait_send()
    for kind in range(3):
        pltpu.make_async_copy(w_o.at[kind], w_o.at[kind], w_sem.at[kind]).wait()
    for c in out_copies:
        c.wait()


def forward(main, step_w, *others):
    any_ = pl.BlockSpec(memory_space=pl.ANY)
    dma = pltpu.SemaphoreType.DMA
    tall = [sds((1536, T), BF16)] * 9 + [sds((1536, T))]
    big = tall[1:] + [sds((3, 4, 2, 4, 2, 3, 16, 768), BF16), sds((2, 4, 4, 2, 3, 16, 256), BF16), sds((2, 4, 4, 2, 3, 16, 768), BF16)]
    small = [sds((8, T)), sds((32, T)), sds((32, T)), sds((T, 128)), sds((32, T), BF16), sds((256, T), BF16), sds((T, 256), BF16),
             sds((256, T), BF16), sds((2, SPAN, SPAN)), sds((2, 16, 768)), sds((256, 16))]
    return pl.pallas_call(
        forward_kernel, out_shape=big + small, in_specs=[any_] * (2 + len(others)), out_specs=[any_] * 23,
        scratch_shapes=[pltpu.VMEM(a.shape, a.dtype) for a in (step_w, others[2], *others[4:])] + [
                        pltpu.VMEM((2, 4, 4, 2, 3, 16, COLS), BF16), pltpu.VMEM((T, 1536), BF16),
                        pltpu.VMEM((T, 1536), BF16)] + [pltpu.VMEM(s.shape, s.dtype) for s in (*tall, big[-1])] + [
            pltpu.VMEM((2, 8, T), F32), pltpu.VMEM((2, 8, T), F32)] + [pltpu.VMEM(s.shape, s.dtype) for s in small] + [
            dma((6, 3, 4)), dma((6, 3, 4)), dma((25,)), dma((3,)), dma((23,)), dma((5,)), dma((5,))],
        compiler_params=pltpu.CompilerParams(collective_id=0, has_side_effects=True, vmem_limit_bytes=60 << 20),
    )(main, step_w, *others)


SCAN_STEPS = {7: [(0, 2)], 11: [(1, 1)]}
CONV_STEPS = {1: [(0, 3)], 5: [(1, 2), (0, 4)]}
TOKEN_STEPS = {0: [(1, 3), (3, 1)], 3: [(2, 1)]}


def add_into(target, *others):
    def add(t, o):
        v = t[...].astype(F32)
        for other in o:
            v = v + other[...].astype(F32)
        t[...] = v.astype(BF16)
    if len(target.shape) == 2:
        add(target, others)
    else:
        @pl.loop(0, target.shape[0])
        def _(i):
            add(target.at[i], [o.at[i] for o in others])


def backward_kernel(xt_h, zt_h, ut_h, dgt_h, vt_h, xst_h, dsil_h, gat_h, yt_h, w_h, wst_h, pa_h,
                    *rest_refs):
    small_h, outs_h, scratch = rest_refs[:14], rest_refs[14:19], rest_refs[19:]
    n = len(RCHUNKS)
    part, regions, halves = scratch[0], scratch[1:1 + 9 * n], scratch[1 + 9 * n:1 + 18 * n]
    (xt, xst, zt, dgt, vt, gat, yt, wbuf, wst, total, both, dcbt, ld, dye_all, xe_all, st_all, ds_all, cross, prow, hrow,
     dcum, ddt1, gskip, dstep_t, dbct, dbct_in, dn_in, branch, br_in, dstate, dst, folds,
     sums, dtt, cumt, cumc, stept, statet, bc, bct, cbt, prm, spar, hidden, cot, gain, out, gstate, gsmall, grad_hidden, small, small_in, own_state, ggain, gain_in, quarter, quarters,
     send, recv, load_sem, w_sem, swap_send, swap_recv, small_send, small_recv, gain_send, gain_recv, q_send, q_recv, out_sem) = scratch[1 + 18 * n:]
    ut, dyt, dzt, dsil, dut = xst, zt, dgt, vt, zt
    at = place()
    mate = {**at, "core": 1 - at["core"]}
    far = moved(at, "z", 2)
    far_mate = {**far, "core": 1 - at["core"]}
    entered = greet([moved(at, axis, by) for axis in "xyz" for by in (1, 2, 3)] + [mate, far_mate]
                    + [moved(mate, "x", by) for by in (1, 2, 3)])
    mine = pl.ds(pl.multiple_of(at["core"] * 256, 256), 256)
    theirs = pl.ds(pl.multiple_of((1 - at["core"]) * 256, 256), 256)

    loads = [pltpu.make_async_copy(s, d, load_sem.at[i]) for i, (s, d) in enumerate(
        [(vt_h, vt), (yt_h, yt), (zt_h, zt), (dgt_h, dgt), (xt_h, xt), (xst_h, xst), (ut_h, ut), (wst_h, wst), (dsil_h, dsil), (gat_h, gat), (pa_h, part.at[..., pl.ds(0, 768)])]
        + list(zip(small_h, (sums, dtt, cumt, cumc, stept, statet, bc, bct, cbt, prm, spar, hidden, cot, gain))))]
    first = [loads[i] for i in (10, 11, 20, 0, 1, 2, 3, 4)]
    second = [loads[i] for i in (9, 5, 7, *range(12, 20), *range(21, 25))]
    out_copies = []

    def put(i, source):
        c = pltpu.make_async_copy(source, outs_h[i], out_sem.at[i])
        c.start()
        out_copies.append(c)

    def weights(i):
        late = i >= 4
        return pltpu.make_async_copy(w_h.at[jnp.where(late, 1 + i % 2, 0), jnp.where(late, (i - 4) // 2, i)], wbuf.at[i % 3], w_sem.at[i % 3])

    def product(i, values):
        weights(i).wait()

        @pl.when(i + 2 < 12)
        def _():
            weights(i + 2).start()
        return (dot(wbuf[i % 3, 0].reshape(384, 768), values[0:768, :]) + dot(wbuf[i % 3, 1].reshape(384, 768), values[768:1536, :])).T

    for c in first:
        c.start()
    weights(0).start()
    weights(1).start()
    for c in second:
        c.start()

    def remote(src, dst_ref, s, r, to):
        return pltpu.make_async_remote_copy(src_ref=src, dst_ref=dst_ref, send_sem=s, recv_sem=r, device_id=device_at(to), device_id_type=MESH)

    def block(where, chunk, piece, stage):
        begin, width = RCHUNKS[chunk]
        return part.at[units(where, ORDERS[piece][:2 - stage]) + (piece, slice(None), pl.ds(begin, width))]

    def whole(chunk, stage):
        return stage == 2

    def slot(chunk, piece, stage):
        return (chunk * 3 + piece) * 3 + stage

    def start(chunk, piece, stage, i):
        axis = ORDERS[piece][2 - stage]
        k = slot(chunk, piece, stage)
        right, left, opposite = moved(at, axis, 1), moved(at, axis, 3), moved(at, axis, 2)
        cut = lambda ref, h: ref if stage == 2 else half_of(ref, stage, piece, RCHUNKS[chunk][1], h)
        own = lambda where: block(where, chunk, piece, stage)
        src, dst_ref, to = (
            lambda: (cut(own(opposite), 0), halves[k].at[0], right),
            lambda: (cut(own(opposite), 1), halves[k].at[1], left),
            lambda: (cut(own(right), 1), cut(regions[k].at[0], 1), right),
            lambda: (cut(own(left), 0), cut(regions[k].at[1], 0), left),
            lambda: (cut(own(right), 0), cut(regions[k].at[0], 0), right),
            lambda: (cut(own(left), 1), cut(regions[k].at[1], 1), left))[i]()
        remote(src, dst_ref, send.at[chunk, piece, int(i > 1)], recv.at[chunk, piece, stage, int(i > 1)], to).start()

    def took(buffer, sem):
        pltpu.make_async_copy(buffer, buffer, sem).wait()

    def kinds(chunk, stage):
        return ((0,), (3,), (4,)) if whole(chunk, stage) else ((0, 1), (2, 3), (4, 5))

    def sent(chunk, piece, stage):
        k = slot(chunk, piece, stage)
        took(halves[k], send.at[chunk, piece, 0])
        took(regions[k], send.at[chunk, piece, 1])

    def step(chunk, k):
        for piece in range(3):
            stage = k // 2
            if k % 2:
                first, _, last = kinds(chunk, stage)
                took(halves[slot(chunk, piece, stage)], recv.at[chunk, piece, stage, 0])
                axis = ORDERS[piece][2 - stage]
                for j in last:
                    mid = block(moved(at, axis, 1 if j == 4 else 3), chunk, piece, stage)
                    if stage < 2:
                        mid = half_of(mid, stage, piece, RCHUNKS[chunk][1], j - 4)
                    add_into(mid, halves[slot(chunk, piece, stage)].at[j - 4])
                    start(chunk, piece, stage, j)
            else:
                if k > 0:
                    s = slot(chunk, piece, stage - 1)
                    took(regions[s], recv.at[chunk, piece, stage - 1, 1])
                    add_into(block(at, chunk, piece, stage - 1), regions[s].at[0], regions[s].at[1])
                    sent(chunk, piece, stage - 1)
                if k < 6:
                    first, second, _ = kinds(chunk, stage)
                    for i in first + second:
                        start(chunk, piece, stage, i)

    def steps_after(table, index):
        for i, todo in table.items():
            @pl.when(index == i)
            def _(todo=todo):
                for chunk, k in todo:
                    step(chunk, k)

    def gradients(left, right, zh, col):
        for q in range(4):
            value = dot(left[q * 384:(q + 1) * 384, :], right, 1, 1).astype(BF16)
            part[zh, q, :, :, :, :, pl.ds(col, right.shape[0])] = value.reshape(4, 2, 3, 16, right.shape[0])

    def strip(q):
        return pl.ds(pl.multiple_of(q * 384, 128), 384)

    def fold(v):
        return v[:, 0:128] + v[:, 128:256] + v[:, 256:384] + v[:, 384:512]

    def row_sums(v):
        ones = jnp.ones((8, 128), BF16)
        a, b, _ = split(v)
        return (dot(ones, a, 1, 1) + dot(ones, b, 1, 1))[0:1]

    for ref in (dcbt, cross, dcum, ddt1, gskip, ggain):
        ref[...] = jnp.zeros_like(ref)
    for c in first[:1]:
        c.wait()
    entered()
    step(0, 0)
    for c in first[1:]:
        c.wait()
    r_out = lax.rsqrt(sums[0:1, :] / INNER + EPS)
    k2 = r_out * r_out * r_out * sums[1:2, :] / INNER

    @pl.loop(0, 6)
    def _(m):
        zh, c, off, _ = group_at(m)
        cols = group_cols(prm, zh, c)
        for i in range(GROUP):
            r = slice(i * HEAD, (i + 1) * HEAD)
            rows = pl.ds(pl.multiple_of(off + i * HEAD, HEAD), HEAD)
            z = zt[rows, :].astype(F32)
            dg = dgt[rows, :].astype(F32)
            v = vt[rows, :].astype(F32)
            sz = sig(z)
            zs = z * sz
            dv = dg * cols[r, 5:6] * r_out - v * k2
            folds[0, r, :] = fold(dg * v * r_out)
            dyt[rows, :] = (dv * zs).astype(BF16)
            dzt[rows, :] = (dv * yt[rows, :] * (sz + zs * (1.0 - sz))).astype(BF16)
        prow[zh * 3 + c, 5:6, :] = row_sums(folds[0])
        gradients(xt, dzt[pl.ds(off, WIDE), :], zh, pl.multiple_of(768 + c * WIDE, WIDE))

    step(0, 1)
    step(1, 0)
    loads[8].start()
    for c in second:
        c.wait()

    @pl.loop(0, 6)
    def _(m):
        zh, c, off, base = group_at(m)
        cc = pltpu.roll(cumc[...], 128 - base, 1)
        skips = group_skip(prm, zh, c)
        for i in range(GROUP):
            r = slice(i * HEAD, (i + 1) * HEAD)
            rows = pl.ds(pl.multiple_of(off + i * HEAD, HEAD), HEAD)
            skip = skips[i:i + 1, 0:1]
            xs = xst[rows, :].astype(F32)
            dyb = dyt[rows, :]
            dy = dyb.astype(F32)
            yssm = yt[rows, :] - skip * xs
            gskip[pl.ds(base + i, 1), :] = jnp.sum(dy * xs, axis=0, keepdims=True)
            dt = dtt[pl.ds(base + i, 1), :]
            cum = cumt[pl.ds(base + i, 1), :]
            xdt = xs * dt
            xdtb = xdt.astype(BF16)
            dxs = []
            for b in range(2):
                s = slice(b * SPAN, (b + 1) * SPAN)
                w = decay(cum, cc[s, i:i + 1], b)
                dxs.append(dot(dyb[:, s], (w * cbt[b]).astype(BF16), 1, 1))
                dcbt[b] += dot(xdtb[:, s], dyb[:, s], 0, 0) * w
            tail = jnp.exp(cum[:, SPAN - 1:SPAN] - cum[:, :SPAN])
            xe = (xdt[:, :SPAN] * tail).astype(BF16)
            dye = (dy[:, SPAN:] * jnp.exp(cum[:, SPAN:])).astype(BF16)
            ds = dot(dye, bc[SPAN:, 128:256]).astype(BF16)
            xe_all[r, :] = xe
            dye_all[r, :] = dye
            st_all[r, :] = dot(xe, bc[0:SPAN, 0:128]).astype(BF16)
            ds_all[r, :] = ds
            dxs[0] = dxs[0] + tail * dot(ds, bc[0:SPAN, 0:128], 1, 1)
            dx = jnp.concatenate(dxs, axis=1)
            dcum[pl.ds(base + i, 1), :] = jnp.sum(dy * yssm - xdtb.astype(F32) * dx, axis=0, keepdims=True)
            ddt1[pl.ds(base + i, 1), :] = jnp.sum(xs * dx, axis=0, keepdims=True)
            dyt[rows, :] = (dt * dx + skip * dy).astype(BF16)
            if i % 2:
                steps_after(SCAN_STEPS, m * 2 + i // 2)
        cross[1] += dot(st_all[...], dye_all[...], 0, 0)
        cross[0] += dot(ds_all[...], xe_all[...], 0, 0)

    upper = tri(SPAN, lambda r, c: r <= c).astype(F32)
    for b in range(2):
        s = slice(b * SPAN, (b + 1) * SPAN)
        d = (dcbt[b] * upper).astype(BF16)
        db = dot(bct[128:256, s], d, 1, 1)
        dc = dot(bct[0:128, s], d)
        dbct[0:128, s] = (db + cross[0] if b == 0 else db).astype(BF16)
        dbct[128:256, s] = (dc + cross[1] if b == 1 else dc).astype(BF16)
    swap_bc = remote(dbct, dbct_in, swap_send.at[1], swap_recv.at[1], mate)
    swap_bc.start()
    loads[6].start()

    dla = exact_dot(dcum[...], tri(T, lambda r, c: r >= c))
    for zh in range(2):
        rows = slice(zh * 16, (zh + 1) * 16)
        hc = prm[zh, :, 0:128].T
        rate = -jnp.exp(hc[:16, 7:8])
        d = dla[rows]
        dstep = (ddt1[rows, :] + rate * d) * sig(stept[rows, :].astype(F32) + hc[:16, 6:7])
        gd = jnp.sum(d * dtt[rows, :] * rate, axis=1, keepdims=True)
        hcol = jnp.concatenate([jnp.sum(dstep, axis=1, keepdims=True), gd, jnp.sum(gskip[rows, :], axis=1, keepdims=True),
                                jnp.zeros((16, 125), F32)], axis=1)
        hrow[:, zh * 128:(zh + 1) * 128] = jnp.concatenate([hcol, jnp.zeros((112, 128), F32)], axis=0).T[:8]
        keep = lax.broadcasted_iota(jnp.int32, (16, T), 0) < 12
        dstep_t[zh, 0:16, :] = jnp.where(keep, dstep, 0.0).astype(BF16)
        dstep_t[zh, 16:128, :] = jnp.zeros((112, T), BF16)


    swap_bc.wait_recv()
    for q in range(4):
        r = slice(q * 64, (q + 1) * 64)
        cols = spar[r]
        p, shifted = conv(statet[r, :].astype(F32), cols)
        sp = sig(p)
        dp = (dbct[r, :].astype(F32) + dbct_in[r, :].astype(F32)) * (sp + p * sp * (1.0 - sp))
        dstate[r, :] = conv_back(dp, cols).astype(BF16)
        dst[r, :] = jnp.concatenate([jnp.sum(dp * shifted[k], axis=1, keepdims=True) for k in range(4)]
                                    + [jnp.sum(dp, axis=1, keepdims=True), jnp.zeros((64, 123), F32)], axis=1)
    small[48:56, :] = dst[...].T[:8].astype(BF16)
    for zh in range(2):
        ld[0:64, :] = dstate[pl.ds(zh * 128 + pl.multiple_of(at["core"] * 64, 64), 64), :]
        ld[64:128, :] = dstep_t[zh, 0:64, :]
        gradients(xt, ld[...], zh, STATE_COL)

    step(3, 0)
    loads[6].wait()
    loads[8].wait()

    @pl.loop(0, 6)
    def _(m):
        zh, c, off, _ = group_at(m)
        cols = group_cols(prm, zh, c)
        for i in range(GROUP):
            r = slice(i * HEAD, (i + 1) * HEAD)
            rows = pl.ds(pl.multiple_of(off + i * HEAD, HEAD), HEAD)
            u = ut[rows, :].astype(F32)
            dp = dyt[rows, :].astype(F32) * dsil[rows, :].astype(F32)
            du = cols[r, 0:1] * dp
            folds[0, r, :] = fold(u * dp)
            folds[4, r, :] = fold(dp)
            for k in range(1, 4):
                ahead = sooner(dp, k)
                du = du + cols[r, k:k + 1] * ahead
                folds[k, r, :] = fold(u * ahead)
            dut[rows, :] = du.astype(BF16)
        for k in range(5):
            prow[zh * 3 + c, k:k + 1, :] = row_sums(folds[k])
        gradients(xt, dut[pl.ds(off, WIDE), :], zh, pl.multiple_of(INNER_COL + c * WIDE, 128))
        steps_after(CONV_STEPS, m)

    for q in range(6):
        small[q * 8:(q + 1) * 8, :] = prow[q].astype(BF16)
    small[56:64, :] = hrow[...].astype(BF16)

    def small_flights(s):
        slot_here = small_in.at[s, at["xyz"[s]]]
        return [remote(slot_here, slot_here, small_send.at[s, by - 1], small_recv.at[s, by - 1], moved(at, "xyz"[s], by)) for by in (1, 2, 3)]

    def small_start(s):
        small_in[s, at["xyz"[s]]] = small[...]
        for c in small_flights(s):
            c.start()

    def small_end(s):
        for c in small_flights(s):
            c.wait()
        total4 = small_in[s, 0].astype(F32) + small_in[s, 1].astype(F32) + small_in[s, 2].astype(F32) + small_in[s, 3].astype(F32)
        small[...] = total4.astype(BF16)
        if s == 2:
            gsmall[0:64, :] = total4

    small_start(0)
    step(2, 0)

    @pl.loop(0, 4)
    def _(q):
        branch[:, strip(q)] = product(q, gat).astype(BF16)

    swap_br = remote(branch.at[theirs], br_in, swap_send.at[0], swap_recv.at[0], mate)
    swap_br.start()

    swap_br.wait()

    @pl.loop(0, 4)
    def _(q):
        more = [dot(wst[zh, q, :, :, :, :, pl.ds(128, 128)].reshape(384, 128), dstep_t[zh]) for zh in range(2)]
        both[...] = product(4 + 2 * q, dzt) + product(5 + 2 * q, dut) + (more[0] + more[1]).T
        total[:, strip(q)] = both[mine, :]
        branch[theirs, strip(q)] = both[theirs, :].astype(BF16)
        steps_after(TOKEN_STEPS, q)

        @pl.when(q == 2)
        def _():
            small_end(0)
            small_start(1)

    swap_dn = remote(branch.at[theirs], dn_in, swap_send.at[2], swap_recv.at[2], mate)
    swap_dn.start()
    own_state[...] = dstate[:, mine].T
    swap_dn.wait_recv()

    @pl.loop(0, 2)
    def _(q):
        r = pl.ds(pl.multiple_of(q * 128, 128), 128)
        full = total[r, :] + dn_in[r, :].astype(F32)
        for zh in range(2):
            full = full + dot(own_state[r, zh * 128:(zh + 1) * 128], wst[zh, :, :, :, :, :, pl.ds(0, 128)].reshape(1536, 128), 1, 1)
        h = hidden[r, :].astype(F32)
        r_in = lax.rsqrt(jnp.mean(h * h, axis=1, keepdims=True) + EPS)
        ggain[...] += jnp.sum(full * h * r_in, axis=0, keepdims=True)
        scaled = full * gain[...].reshape(1, 1536)
        back = scaled * r_in - h * (r_in * r_in * r_in * (jnp.sum(scaled * h, axis=1, keepdims=True) / 1536))
        grad_hidden[r, :] = (cot[r, :].astype(F32) + back).astype(BF16)

    def gain_peers(s):
        if s == 0:
            return [moved(at, "x", by) for by in (1, 2, 3)] + [mate] + [moved(mate, "x", by) for by in (1, 2, 3)]
        return [moved(at, "xyz"[s], by) for by in (1, 2, 3)]

    def gain_flights(s):
        here = gain_in.at[s, at["x"] * 2 + at["core"] if s == 0 else at["xyz"[s]]]
        return [remote(here, here, gain_send.at[s, i], gain_recv.at[s, i], to) for i, to in enumerate(gain_peers(s))]

    def gain_start(s, rows):
        gain_in[s, at["x"] * 2 + at["core"] if s == 0 else at["xyz"[s]]] = rows
        for c in gain_flights(s):
            c.start()

    def gain_end(s):
        for c in gain_flights(s):
            c.wait()
        rows = gain_in[s, 0]
        for i in range(1, 8 if s == 0 else 4):
            rows = rows + gain_in[s, i]
        return rows

    gain_start(0, jnp.concatenate([ggain[:, q * 256:(q + 1) * 256] for q in range(6)] + [jnp.zeros((2, 256), F32)], axis=0))
    put(4, grad_hidden)

    @pl.loop(0, 2)
    def _(q):
        r = pl.ds(pl.multiple_of(q * 128, 128), 128)
        own_rows = pl.ds(pl.multiple_of(at["core"] * 256 + q * 128, 128), 128)
        branch[own_rows, :] = (hidden[r, :].astype(F32) + branch[own_rows, :].astype(F32) + br_in[r, :].astype(F32)).astype(BF16)

    put(3, branch.at[mine])
    step(0, 5)
    step(1, 4)
    step(3, 2)
    small_end(1)
    small_start(2)
    step(2, 2)
    gain_start(1, gain_end(0))
    step(1, 5)
    step(0, 6)
    step(3, 3)
    step(2, 3)
    gain_start(2, gain_end(1))
    step(3, 4)
    step(1, 6)
    step(2, 4)
    small_end(2)
    step(3, 5)
    step(2, 5)
    gsmall[64:72, :] = gain_end(2)
    put(2, gsmall)
    step(3, 6)
    own = units(at, "")
    for piece in range(3):
        quarter[piece * 16:(piece + 1) * 16, :] = part[own + (piece, slice(None), pl.ds(STATE_COL, 128))].astype(F32)
    thirds = [remote(quarter, quarters.at[i], q_send.at[i], q_recv.at[i], to) for i, to in enumerate((mate, far, far_mate))]
    for c in thirds:
        c.start()
    step(2, 6)
    for piece in range(3):
        out[piece * 16:(piece + 1) * 16, :] = part[own + (piece, slice(None), pl.ds(0, 2304))]
    put(0, out)
    for c in thirds:
        c.wait()
    low = at["core"] == 0
    q0, q1, q2, q3 = quarter[...], quarters[0], quarters[1], quarters[2]
    here = jnp.where(low, jnp.concatenate([q0[:, :64], q1[:, :64]], axis=1), jnp.concatenate([q1[:, :64], q0[:, :64]], axis=1))
    there = jnp.where(low, jnp.concatenate([q2[:, :64], q3[:, :64]], axis=1), jnp.concatenate([q3[:, :64], q2[:, :64]], axis=1))
    first = at["z"] < 2
    gstate[:, 0:128] = jnp.where(first, here, there)
    gstate[:, 128:256] = jnp.where(first, there, here)
    gstate[:, 256:384] = q0
    put(1, gstate)
    for s in (swap_bc, swap_dn):
        s.wait_send()
    for c in out_copies:
        c.wait()


def backward(tall, small, hidden, cot, gain):
    n = len(RCHUNKS)
    results = [sds((48, 2304), BF16), sds((48, 384)), sds((SUMS + 8, 256)), sds((256, 1536), BF16), sds((256, 1536), BF16)]
    any_ = pl.BlockSpec(memory_space=pl.ANY)
    shapes = [(stage, piece, RCHUNKS[chunk][1]) for chunk in range(n) for piece in range(3) for stage in range(3)]
    regions = [pltpu.VMEM((2,) + region_shape(*s), BF16) for s in shapes]
    halves = [pltpu.VMEM((1 if s[0] == 2 else 2,) + half_shape(*s), BF16) for s in shapes]
    dma = pltpu.SemaphoreType.DMA
    v = lambda shape, dtype=F32: pltpu.VMEM(shape, dtype)
    return pl.pallas_call(
        backward_kernel,
        in_specs=[any_] * (len(tall) + len(small) + 3),
        out_specs=[any_] * 5,
        out_shape=results,
        scratch_shapes=[v((2, 4, 4, 2, 3, 16, RCOLS), BF16)] + regions + halves + [
            v((1536, T), BF16)] * 6 + [v((1536, T)), v((3, 2, 4, 2, 3, 16, 768), BF16), v((2, 4, 4, 2, 3, 16, 256), BF16),
            v((256, 1536)), v((T, 384)), v((2, SPAN, SPAN)), v((128, T), BF16), v((WIDE, SPAN), BF16), v((WIDE, SPAN), BF16),
            v((WIDE, 128), BF16), v((WIDE, 128), BF16), v((2, 128, SPAN)), v((6, 8, WIDE)), v((8, 256)),
            v((32, T)), v((32, T)), v((32, T)), v((2, 128, T), BF16), v((256, T), BF16), v((256, T), BF16),
            v((256, 1536), BF16), v((T, 1536), BF16), v((256, 1536), BF16),
            v((256, T), BF16), v((256, 128)), v((5, WIDE, 128))] + [v(a.shape, a.dtype) for a in (*small, hidden, cot, gain, *results[:3], results[4])] + [ v((SUMS, 256), BF16), v((3, 4, SUMS, 256), BF16), v((256, 256), BF16), v((1, 1536)), v((3, 8, 8, 256)), v((48, 128)), v((3, 48, 128)),
            dma((n, 3, 2)), dma((n, 3, 3, 2)), dma((25,)), dma((3,)), dma((3,)), dma((3,)), dma((3, 3)), dma((3, 3)), dma((3, 7)), dma((3, 7)), dma((3,)), dma((3,)), dma((5,))],
        compiler_params=pltpu.CompilerParams(collective_id=1, has_side_effects=True, vmem_limit_bytes=65400 << 10),
    )(*tall, *small, hidden, cot, gain)


def finish_kernel(out, gstate, small, new_h, grad_h, new_hidden, grad_hidden, in_gain, main, step, state, inner, inner_bias, cstate, cstate_bias,
                  bias, log, skip, out_gain, proj_out):
    new_hidden[...] = new_h[...]
    grad_hidden[...] = grad_h[...]
    z_hi = lax.axis_index("tensor") // 2
    proj_out[...] = out[:, 0:768].astype(F32)
    main[:, 0, :] = out[:, 768:1536].astype(F32)
    main[:, 1, :] = out[:, 1536:2304].astype(F32)
    step[...] = gstate[:, 256:384].T[64:76]
    state[...] = gstate[:, 0:256]
    for c in range(3):
        rows = small[pl.ds(pl.multiple_of(z_hi * 24 + c * 8, 8), 8), :]
        cols = slice(c * 256, (c + 1) * 256)
        inner[:, cols] = rows[0:4]
        inner_bias[cols] = rows[4:5].reshape(256)
        out_gain[cols] = rows[5:6].reshape(256)
    cstate[...] = small[48:52, :]
    cstate_bias[...] = small[52:53, :].reshape(256)
    for q in range(6):
        in_gain[q * 256:(q + 1) * 256] = small[64 + q:65 + q, :].reshape(256)
    heads = small[56:64, pl.ds(pl.multiple_of(z_hi * 128, 128), 128)]
    for i, ref in enumerate((bias, log, skip)):
        ref[...] = heads[i:i + 1, 0:12].reshape(12)


def finish(out, gstate, small, new_hidden, grad_hidden):
    vm = pl.BlockSpec(memory_space=pltpu.VMEM)
    shapes = [sds(s) for s in ((1536,), (48, 2, 768), (12, 48), (48, 256), (4, 768), (768,), (4, 256), (256,), (12,), (12,), (12,), (768,), (48, 768))]
    return pl.pallas_call(
        finish_kernel, out_shape=[sds((256, 1536), BF16)] * 2 + shapes, in_specs=[vm] * 5, out_specs=[vm] * 15,
    )(out, gstate, small, new_hidden, grad_hidden)


def per_device(hidden, in_gain, proj_main, proj_step, proj_state, conv_inner, conv_inner_bias, conv_state, conv_state_bias,
               step_bias, decay_log, skip_gain, out_gain, proj_out, grad_out):
    outs = forward(proj_main.reshape(48, 1536), proj_step.T, proj_state, proj_out, hidden, grad_out, conv_inner, conv_state,
                   conv_inner_bias, out_gain, conv_state_bias, in_gain, step_bias, decay_log, skip_gain)
    results = backward(outs[:12], outs[12:], hidden, grad_out, in_gain)
    new_hidden, grad_hidden, ggain, main, step, *others = finish(*results)
    return (new_hidden, grad_hidden, ggain, main, step.T, *others)


def solution(mesh):
    rows = P(("dp", "tensor"), None)
    per_head = P("tensor")
    in_specs = (rows, P(), P("dp", None, "tensor"), P("dp", "tensor"), P("dp", None), P(None, "tensor"), per_head, P(), P(),
                per_head, per_head, per_head, per_head, P("dp", "tensor"), rows)
    out_specs = (rows, rows, P(), P("dp", None, "tensor"), P("dp", "tensor"), P("dp", None), P(None, "tensor"), per_head, P(), P(),
                 per_head, per_head, per_head, per_head, P("dp", "tensor"))
    return jax.shard_map(per_device, mesh=mesh, in_specs=in_specs, out_specs=out_specs, check_vma=False)
```

```python
import functools

import jax
import jax.numpy as jnp
from jax import lax
from jax.experimental import pallas as pl
from jax.experimental.pallas import tpu as pltpu
from jax.sharding import PartitionSpec as P

MESH = pl.DeviceIdType.MESH
F32, BF16 = jnp.float32, jnp.bfloat16
EPS = 1e-5
T, SPAN, HEAD, GROUP = 512, 256, 64, 4
WIDE = GROUP * HEAD
INNER = 3072
COLS = 2560
STAGED = ((0, 256), (256, 768), (1024, 768), (1792, 768))
ORDERS = ("xyz", "yzx", "zxy")
RCHUNKS = ((0, 768), (768, 768), (1536, 512), (2048, 256), (2304, 128))
STATE_COL, INNER_COL = 2304, 1536
RCOLS = 2432
SUMS = 64


def sds(shape, dtype=F32):
    return jax.ShapeDtypeStruct(shape, dtype)


def place():
    dp, tp = lax.axis_index("dp"), lax.axis_index("tensor")
    return dict(x=dp // 8, y=(dp // 2) % 4, z=(tp // 2) * 2 + dp % 2, core=tp % 2)


def device_at(at):
    return ((at["x"] * 4 + at["y"]) * 2 + at["z"] % 2, (at["z"] // 2) * 2 + at["core"])


def moved(at, axis, by):
    return {**at, axis: (at[axis] + by) % 4}


def units(at, whole):
    return (slice(None) if "z" in whole else at["z"] // 2, slice(None) if "x" in whole else at["x"],
            slice(None) if "y" in whole else at["y"], slice(None) if "z" in whole else at["z"] % 2)


def greet(others):
    barrier = pltpu.get_barrier_semaphore()
    for other in others:
        pl.semaphore_signal(barrier, inc=1, device_id=device_at(other), device_id_type=MESH)
    return lambda: pl.semaphore_wait(barrier, len(others))


def half_of(ref, stage, piece, width, half):
    if stage == 0:
        return ref.at[pl.ds(2 * half, 2)] if piece == 0 else ref.at[:, pl.ds(2 * half, 2)]
    if stage == 1:
        return ref.at[pl.ds(2 * half, 2)] if piece < 2 else ref.at[half]
    return ref.at[:, pl.ds(half * (width // 2), width // 2)]


def half_shape(stage, piece, width):
    if stage == 0:
        return (2, 4, 16, width) if piece == 0 else (2, 2, 2, 16, width)
    return (2, 16, width)


def region_shape(stage, piece, width):
    whole = ORDERS[piece][:2 - stage]
    dims = ([2] if "z" in whole else []) + ([4] if "x" in whole else []) + ([4] if "y" in whole else []) + ([2] if "z" in whole else [])
    return tuple(dims) + (16, width)


def dot(a, b, ca=1, cb=0):
    return lax.dot_general(a, b, (((ca,), (cb,)), ((), ())), preferred_element_type=F32)


def lanes(rows, width=T):
    return lax.broadcasted_iota(jnp.int32, (rows, width), 1)


def later(u, k):
    return jnp.where(lanes(u.shape[0]) >= k, pltpu.roll(u, k, 1), 0.0) if k else u


def sooner(u, k):
    return jnp.where(lanes(u.shape[0]) < T - k, pltpu.roll(u, T - k, 1), 0.0) if k else u


def sig(v):
    return 1.0 / (1.0 + jnp.exp(-v))


def split(v):
    a = v.astype(BF16)
    r = v - a.astype(F32)
    b = r.astype(BF16)
    return a, b, (r - b.astype(F32)).astype(BF16)


def exact_dot(v, ones):
    n = v.shape[0]
    s = dot(jnp.concatenate(split(v), axis=0), ones)
    return s[:n] + s[n:2 * n] + s[2 * n:]


def tri(n, keep):
    r = lax.broadcasted_iota(jnp.int32, (n, n), 0)
    c = lax.broadcasted_iota(jnp.int32, (n, n), 1)
    return jnp.where(keep(r, c), 1.0, 0.0).astype(BF16)


def conv(u, cols):
    shifted = [later(u, k) for k in range(4)]
    p = cols[:, 4:5] + cols[:, 0:1] * shifted[0]
    for k in range(1, 4):
        p = p + cols[:, k:k + 1] * shifted[k]
    return p, shifted


def conv_back(dp, cols):
    du = cols[:, 0:1] * dp
    for k in range(1, 4):
        du = du + cols[:, k:k + 1] * sooner(dp, k)
    return du


def decay(cum_row, cum_col, b):
    return jnp.exp(jnp.minimum(cum_row[:, b * SPAN:(b + 1) * SPAN] - cum_col, 0.0))


def group_at(n):
    zh, c = n % 2, n // 2
    return zh, c, pl.multiple_of((zh * 3 + c) * WIDE, WIDE), zh * 16 + c * GROUP


def group_cols(prm, zh, c):
    return prm[zh, :, pl.ds(pl.multiple_of(c * WIDE, WIDE), WIDE)].T


def group_skip(prm, zh, c):
    cols = prm[zh, :, 0:128].T
    return pltpu.roll(jnp.broadcast_to(cols[:, 8:9], (128, 128)), 128 - c * GROUP, 0)


def forward_kernel(main_h, step_h, state_h, out_h, hidden_h, cot_h, cinner_h, cstate_h, offset_h, gain_h, state_offset_h, in_gain_h, bias_h, log_h, skip_h,
                   xt_o, zt_o, ut_o, dgt_o, vt_o, xst_o, dsil_o, gat_o, yt_o, w_o, wst_o, pa_o,
                   *rest):
    small_o, (step_w, hidden, cinner, cstate, offset, gain, state_offset, in_gain, bias, log, skip_gain, w, x, g, xt, gt, zt, ut, dgt, vt, xst, dsil, gat, yt, pa, acc, acc_in,
              sums, dtt, cumt, cumc, stept, statet, bc, bct, cbt, prm, spar,
              send, recv, local, w_sem, out_sem, swap_send, swap_recv) = rest[:11], rest[11:]
    at = place()
    z_hi = at["z"] // 2
    mate = {**at, "core": 1 - at["core"]}
    far = moved(at, "z", 2)
    entered = greet([moved(at, axis, by) for axis in "xyz" for by in (1, 3)] + [mate, far])
    mine = pl.ds(pl.multiple_of(at["core"] * 256, 256), 256)
    own_unit = w.at[units(at, "")]
    moves = [(step_h, step_w), (hidden_h, hidden), (cot_h, g.at[mine]), (cinner_h, cinner), (cstate_h, cstate), (offset_h, offset), (gain_h, gain),
             (state_offset_h, state_offset), (in_gain_h, in_gain), (bias_h, bias), (log_h, log), (skip_h, skip_gain)]
    params = len(moves)
    for piece in range(3):
        rows = pl.ds(piece * 16, 16)
        for source, begin, width in ((state_h.at[rows, pl.ds(pl.multiple_of(z_hi * 128, 128), 128)], 0, 128), (main_h.at[rows, pl.ds(768, 768)], 256, 768),
                                     (main_h.at[rows, pl.ds(0, 768)], 1024, 768), (out_h.at[rows], 1792, 768)):
            moves.append((source, own_unit.at[piece, :, pl.ds(begin, width)]))
    moves = [pltpu.make_async_copy(a, b, local.at[i]) for i, (a, b) in enumerate(moves)]
    for c in moves:
        c.start()
    moves[0].wait()
    step_rows = jnp.concatenate([step_w[...].astype(F32), jnp.zeros((116, 48), F32)], axis=0).T.astype(BF16)
    for piece in range(3):
        w[units(at, "") + (piece, slice(None), pl.ds(128, 128))] = step_rows[piece * 16:(piece + 1) * 16]
    for c in moves[params:]:
        c.wait()
    entered()

    def part(where, piece, stage, chunk):
        begin, width = STAGED[chunk] if stage == 2 else (0, COLS)
        return w.at[units(where, ORDERS[piece][:stage]) + (piece, slice(None), pl.ds(begin, width))]

    def flight(piece, stage, chunk, kind):
        axis, by = ORDERS[piece][stage], (1, 3)[kind % 2]
        width = STAGED[chunk][1] if stage == 2 else COLS
        if kind < 2:
            target = source = part(at, piece, stage, chunk)
        else:
            target = source = half_of(part(moved(at, axis, -by), piece, stage, chunk), 2 - stage, piece, width, kind - 2)
        sem = (stage + chunk if stage == 2 else stage, piece, kind)
        return pltpu.make_async_remote_copy(src_ref=source, dst_ref=target, send_sem=send.at[sem], recv_sem=recv.at[sem],
                                            device_id=device_at(moved(at, axis, by)), device_id_type=MESH)

    def fulls(stage, chunk=0):
        for piece in range(3):
            if stage > 0 and chunk == 0:
                for kind in (2, 3):
                    flight(piece, stage - 1, 0, kind).wait_recv()
            for kind in (0, 1):
                flight(piece, stage, chunk, kind).start()

    def halves(stage, chunk=0):
        for piece in range(3):
            for kind in (0, 1):
                flight(piece, stage, chunk, kind).wait_recv()
                flight(piece, stage, chunk, kind + 2).start()

    def arrived(chunk):
        for piece in range(3):
            for kind in (2, 3):
                flight(piece, 2, chunk, kind).wait_recv()

    fulls(0)
    for c in moves[1:params]:
        c.wait()

    prm[z_hi] = jnp.zeros((16, 768), F32)
    prm[z_hi, 0:4, :] = cinner[...]
    prm[z_hi, 4:5, :] = offset[...].reshape(1, 768)
    prm[z_hi, 5:6, :] = gain[...].reshape(1, 768)
    for i, ref in enumerate((bias, log, skip_gain)):
        prm[z_hi, 6 + i:7 + i, 0:12] = ref[...].reshape(1, 12)
    h = hidden[...].astype(F32)
    scale = lax.rsqrt(jnp.mean(h * h, axis=1, keepdims=True) + EPS)
    x[mine, :] = (h * scale * in_gain[...].reshape(1, 1536)).astype(BF16)
    swaps = [pltpu.make_async_remote_copy(src_ref=s, dst_ref=s, send_sem=swap_send.at[i], recv_sem=swap_recv.at[i],
                                          device_id=device_at(to), device_id_type=MESH)
             for i, (s, to) in enumerate([(x.at[mine], mate), (g.at[mine], mate), (prm.at[z_hi], far)])]
    for c in swaps:
        c.start()
    spar[...] = jnp.concatenate([cstate[...], state_offset[...].reshape(1, 256), jnp.zeros((11, 256), F32)], axis=0).T

    halves(0)
    fulls(1)
    out_copies = []

    def put(i, source, target):
        c = pltpu.make_async_copy(source, target, out_sem.at[i])
        c.start()
        out_copies.append(c)

    for c in swaps[:2]:
        c.wait_recv()
    xt[...] = x[...].T
    gt[...] = g[...].T
    put(0, xt, xt_o)
    halves(1)
    swaps[2].wait_recv()
    acc[...] = jnp.zeros_like(acc)
    sums[...] = jnp.zeros_like(sums)
    cumc[...] = jnp.zeros_like(cumc)
    fulls(2, 0)
    fulls(2, 1)
    halves(2, 0)
    halves(2, 1)
    fulls(2, 2)
    arrived(0)
    put(2, w.at[:, :, :, :, :, :, pl.ds(0, 256)], wst_o)

    def weight(zh, begin):
        return w[zh, :, :, :, :, :, pl.ds(begin, WIDE)].reshape(1536, WIDE)

    for zh in range(2):
        raw = dot(x[...], weight(zh, 0)).T.astype(BF16)
        statet[zh * 128:(zh + 1) * 128, :] = raw[:128]
        stept[zh * 16:(zh + 1) * 16, :] = raw[128:144]
    for q in range(4):
        r = slice(q * 64, (q + 1) * 64)
        p, _ = conv(statet[r, :].astype(F32), spar[r])
        bct[r, :] = (p * sig(p)).astype(BF16)
    bc[...] = bct[...].T
    upper = tri(SPAN, lambda r, c: r <= c)
    for b in range(2):
        rows = pl.ds(b * SPAN, SPAN)
        cbt[b] = dot(bc[rows, 0:128], bc[rows, 128:256], 1, 1) * upper.astype(F32)
    for zh in range(2):
        cols = prm[zh, :, 0:128].T
        v = stept[zh * 16:(zh + 1) * 16, :].astype(F32) + cols[:16, 6:7]
        dt = jnp.maximum(v, 0.0) + jnp.log1p(jnp.exp(-jnp.abs(v)))
        dtt[zh * 16:(zh + 1) * 16, :] = dt
        la = dt * -jnp.exp(cols[:16, 7:8])
        for b in range(2):
            cumt[zh * 16:(zh + 1) * 16, b * SPAN:(b + 1) * SPAN] = exact_dot(la[:, b * SPAN:(b + 1) * SPAN], upper)
    cumc[...] = jnp.concatenate([cumt[...], jnp.zeros((96, T), F32)], axis=0).T
    for i, ref in enumerate((dtt, cumt, cumc, stept, statet, bc, bct, cbt, prm, spar)):
        put(10 + i, ref, small_o[1 + i])

    def put_weights(kind, begin):
        for n in range(8):
            zh, q = n % 2, n // 2
            pltpu.make_async_copy(w.at[zh, q, :, :, :, :, pl.ds(begin, 768)], w_o.at[kind, q, zh], w_sem.at[kind]).start()

    arrived(1)
    put_weights(2, 256)

    @pl.loop(0, 6)
    def _(n):
        zh, c, off, base = group_at(n)
        cols = group_cols(prm, zh, c)
        skip = group_skip(prm, zh, c)
        cc = pltpu.roll(cumc[...], 128 - base, 1)
        ut[pl.ds(off, WIDE), :] = dot(x[...], weight(zh, pl.multiple_of(256 + c * WIDE, WIDE))).T.astype(BF16)
        for i in range(GROUP):
            r = slice(i * HEAD, (i + 1) * HEAD)
            rows = pl.ds(pl.multiple_of(off + i * HEAD, HEAD), HEAD)
            p, _ = conv(ut[rows, :].astype(F32), cols[r])
            sp = sig(p)
            xs = p * sp
            xsb = xs.astype(BF16)
            xst[rows, :] = xsb
            dsil[rows, :] = (sp + xs * (1.0 - sp)).astype(BF16)
            xs = xsb.astype(F32)
            cum = cumt[pl.ds(base + i, 1), :]
            xdt = xs * dtt[pl.ds(base + i, 1), :]
            xdtb = xdt.astype(BF16)
            ys = []
            for b in range(2):
                m = (decay(cum, cc[b * SPAN:(b + 1) * SPAN, i:i + 1], b) * cbt[b]).astype(BF16)
                ys.append(dot(xdtb[:, b * SPAN:(b + 1) * SPAN], m))
            tail = jnp.exp(cum[:, SPAN - 1:SPAN] - cum[:, :SPAN])
            state = dot((xdt[:, :SPAN] * tail).astype(BF16), bc[0:SPAN, 0:128]).astype(BF16)
            ys[1] = ys[1] + jnp.exp(cum[:, SPAN:]) * dot(state, bc[SPAN:, 128:256], 1, 1)
            yt[rows, :] = jnp.concatenate(ys, axis=1) + skip[i:i + 1, 0:1] * xs

        @pl.when(n == 2)
        def _():
            halves(2, 2)
            fulls(2, 3)

    put(3, xst, xst_o)
    put(4, yt, yt_o)
    put(5, ut, ut_o)
    put(9, dsil, dsil_o)
    arrived(2)
    put_weights(1, 1024)

    @pl.loop(0, 6)
    def _(n):
        zh, c, off, _ = group_at(n)
        zt[pl.ds(off, WIDE), :] = dot(x[...], weight(zh, pl.multiple_of(1024 + c * WIDE, WIDE))).T.astype(BF16)
        for i in range(GROUP):
            rows = pl.ds(pl.multiple_of(off + i * HEAD, HEAD), HEAD)
            z = zt[rows, :].astype(F32)
            vb = (yt[rows, :] * (z * sig(z))).astype(BF16)
            vt[rows, :] = vb
            v = vb.astype(F32)
            acc[0, 0:1, :] += jnp.sum(v * v, axis=0, keepdims=True)

        @pl.when(n == 3)
        def _():
            halves(2, 3)

    put(6, zt, zt_o)
    put(7, vt, vt_o)

    c = pltpu.make_async_remote_copy(src_ref=acc.at[0], dst_ref=acc_in.at[0], send_sem=swap_send.at[3], recv_sem=swap_recv.at[3],
                                     device_id=device_at(mate), device_id_type=MESH)
    c.start()
    c.wait()
    sums[0:1, :] = acc[0, 0:1] + acc_in[0, 0:1]

    r_out = lax.rsqrt(sums[0:1, :] / INNER + EPS)

    @pl.loop(0, 6)
    def _(n):
        zh, c, off, _ = group_at(n)
        cols = group_cols(prm, zh, c)
        for i in range(GROUP):
            rows = pl.ds(pl.multiple_of(off + i * HEAD, HEAD), HEAD)
            gat[rows, :] = (vt[rows, :].astype(F32) * r_out * cols[i * HEAD:(i + 1) * HEAD, 5:6]).astype(BF16)
        value = dot(gt[...], gat[pl.ds(off, WIDE), :], 1, 1).astype(BF16)
        pa[zh, :, :, :, :, :, pl.ds(pl.multiple_of(c * WIDE, WIDE), WIDE)] = value.reshape(4, 4, 2, 3, 16, WIDE)

    put(21, gat, gat_o)
    put(22, pa, pa_o)
    arrived(3)
    put_weights(0, 1792)

    @pl.loop(0, 6)
    def _(n):
        zh, c, off, _ = group_at(n)
        cols = group_cols(prm, zh, c)
        dgt[pl.ds(off, WIDE), :] = dot(g[...], weight(zh, pl.multiple_of(1792 + c * WIDE, WIDE))).T.astype(BF16)
        for i in range(GROUP):
            rows = pl.ds(pl.multiple_of(off + i * HEAD, HEAD), HEAD)
            s = dgt[rows, :].astype(F32) * cols[i * HEAD:(i + 1) * HEAD, 5:6] * vt[rows, :].astype(F32)
            acc[1, 0:1, :] += jnp.sum(s, axis=0, keepdims=True)

    put(8, dgt, dgt_o)
    sums[1:2, :] = acc[1, 0:1]
    put(20, sums, small_o[0])
    for piece in range(3):
        for kind in range(4):
            for stage in range(2):
                flight(piece, stage, 0, kind).wait_send()
            for chunk in range(4):
                flight(piece, 2, chunk, kind).wait_send()
    for s in swaps:
        s.wait_send()
    for kind in range(3):
        pltpu.make_async_copy(w_o.at[kind], w_o.at[kind], w_sem.at[kind]).wait()
    for c in out_copies:
        c.wait()


def forward(main, step_w, *others):
    any_ = pl.BlockSpec(memory_space=pl.ANY)
    dma = pltpu.SemaphoreType.DMA
    tall = [sds((1536, T), BF16)] * 9 + [sds((1536, T))]
    big = tall[1:] + [sds((3, 4, 2, 4, 2, 3, 16, 768), BF16), sds((2, 4, 4, 2, 3, 16, 256), BF16), sds((2, 4, 4, 2, 3, 16, 768), BF16)]
    small = [sds((8, T)), sds((32, T)), sds((32, T)), sds((T, 128)), sds((32, T), BF16), sds((256, T), BF16), sds((T, 256), BF16),
             sds((256, T), BF16), sds((2, SPAN, SPAN)), sds((2, 16, 768)), sds((256, 16))]
    return pl.pallas_call(
        forward_kernel, out_shape=big + small, in_specs=[any_] * (2 + len(others)), out_specs=[any_] * 23,
        scratch_shapes=[pltpu.VMEM(a.shape, a.dtype) for a in (step_w, others[2], *others[4:])] + [
                        pltpu.VMEM((2, 4, 4, 2, 3, 16, COLS), BF16), pltpu.VMEM((T, 1536), BF16),
                        pltpu.VMEM((T, 1536), BF16)] + [pltpu.VMEM(s.shape, s.dtype) for s in (*tall, big[-1])] + [
            pltpu.VMEM((2, 8, T), F32), pltpu.VMEM((2, 8, T), F32)] + [pltpu.VMEM(s.shape, s.dtype) for s in small] + [
            dma((6, 3, 4)), dma((6, 3, 4)), dma((25,)), dma((3,)), dma((23,)), dma((4,)), dma((4,))],
        compiler_params=pltpu.CompilerParams(collective_id=0, has_side_effects=True, vmem_limit_bytes=60 << 20),
    )(main, step_w, *others)


SCAN_STEPS = {7: [(0, 2)], 11: [(1, 1)]}
CONV_STEPS = {1: [(0, 3)], 3: [(2, 0)], 5: [(1, 2), (0, 4)]}
TOKEN_STEPS = {0: [(1, 3)], 1: [(2, 1)], 2: [(3, 1), (4, 1)]}


def add_into(target, *others):
    def add(t, o):
        v = t[...].astype(F32)
        for other in o:
            v = v + other[...].astype(F32)
        t[...] = v.astype(BF16)
    if len(target.shape) == 2:
        add(target, others)
    else:
        @pl.loop(0, target.shape[0])
        def _(i):
            add(target.at[i], [o.at[i] for o in others])


def backward_kernel(xt_h, zt_h, ut_h, dgt_h, vt_h, xst_h, dsil_h, gat_h, yt_h, w_h, wst_h, pa_h,
                    *rest_refs):
    small_h, outs_h, scratch = rest_refs[:14], rest_refs[14:19], rest_refs[19:]
    n = len(RCHUNKS)
    part, regions, halves = scratch[0], scratch[1:1 + 9 * n], scratch[1 + 9 * n:1 + 15 * n]
    (xt, xst, zt, dgt, vt, gat, yt, wbuf, wst, total, both, dcbt, ld, dye_all, xe_all, st_all, ds_all, cross, prow, hrow,
     dcum, ddt1, gskip, dstep_t, dbct, dbct_in, dn_in, branch, br_in, dstate, dst, folds,
     sums, dtt, cumt, cumc, stept, statet, bc, bct, cbt, prm, spar, hidden, cot, gain, out, gstate, gsmall, grad_hidden, small, small_in, own_state, ggain, gain_in, quarter, quarters, sums_in,
     send, recv, load_sem, w_sem, swap_send, swap_recv, small_send, small_recv, gain_send, gain_recv, q_send, q_recv, out_sem) = scratch[1 + 15 * n:]
    ut, dyt, dzt, dsil, dut = xst, zt, dgt, vt, zt
    at = place()
    mate = {**at, "core": 1 - at["core"]}
    far = moved(at, "z", 2)
    far_mate = {**far, "core": 1 - at["core"]}
    entered = greet([moved(at, axis, by) for axis in "xyz" for by in (1, 2, 3)] + [mate, far_mate]
                    + [moved(mate, "x", by) for by in (1, 2, 3)])
    mine = pl.ds(pl.multiple_of(at["core"] * 256, 256), 256)
    theirs = pl.ds(pl.multiple_of((1 - at["core"]) * 256, 256), 256)

    loads = [pltpu.make_async_copy(s, d, load_sem.at[i]) for i, (s, d) in enumerate(
        [(vt_h, vt), (yt_h, yt), (zt_h, zt), (dgt_h, dgt), (xt_h, xt), (xst_h, xst), (ut_h, ut), (wst_h, wst), (dsil_h, dsil), (gat_h, gat), (pa_h, part.at[..., pl.ds(0, 768)])]
        + list(zip(small_h, (sums, dtt, cumt, cumc, stept, statet, bc, bct, cbt, prm, spar, hidden, cot, gain))))]
    first = [loads[i] for i in (10, 11, 20, 0, 1, 2, 3, 4)]
    second = [loads[i] for i in (9, 5, 7, *range(12, 20), *range(21, 25))]
    out_copies = []

    def put(i, source):
        c = pltpu.make_async_copy(source, outs_h[i], out_sem.at[i])
        c.start()
        out_copies.append(c)

    def weights(i):
        late = i >= 8
        return pltpu.make_async_copy(w_h.at[jnp.where(late, 0, 1 + i % 2), jnp.where(late, i - 8, i // 2)], wbuf.at[i % 3], w_sem.at[i % 3])

    def product(i, values):
        weights(i).wait()

        @pl.when(i + 2 < 12)
        def _():
            weights(i + 2).start()
        return (dot(wbuf[i % 3, 0].reshape(384, 768), values[0:768, :]) + dot(wbuf[i % 3, 1].reshape(384, 768), values[768:1536, :])).T

    for c in first:
        c.start()
    weights(0).start()
    weights(1).start()
    for c in second:
        c.start()

    def remote(src, dst_ref, s, r, to):
        return pltpu.make_async_remote_copy(src_ref=src, dst_ref=dst_ref, send_sem=s, recv_sem=r, device_id=device_at(to), device_id_type=MESH)

    def block(where, chunk, piece, stage):
        begin, width = RCHUNKS[chunk]
        return part.at[units(where, ORDERS[piece][:2 - stage]) + (piece, slice(None), pl.ds(begin, width))]

    def slot(chunk, piece, stage):
        return (chunk * 3 + piece) * 3 + stage

    def start(chunk, piece, stage, i):
        axis = ORDERS[piece][2 - stage]
        region = regions[slot(chunk, piece, stage)]
        right, left, opposite = moved(at, axis, 1), moved(at, axis, 3), moved(at, axis, 2)
        if (chunk, stage) == (0, 0) and i < 4:
            own = lambda where: pa_h.at[units(where, ORDERS[piece][:2]) + (piece,)]
        else:
            own = lambda where: block(where, chunk, piece, stage)
        if stage == 2:
            to = (right, left, opposite)[i]
            remote(own(to), region.at[i], send.at[chunk, piece, 1], recv.at[chunk, piece, 2, 1], to).start()
            return
        half = halves[(chunk * 3 + piece) * 2 + stage]
        cut = lambda ref, h: half_of(ref, stage, piece, RCHUNKS[chunk][1], h)
        src, dst_ref, to = (
            lambda: (cut(own(opposite), 0), half.at[0], right),
            lambda: (cut(own(opposite), 1), half.at[1], left),
            lambda: (cut(own(right), 1), cut(region.at[0], 1), right),
            lambda: (cut(own(left), 0), cut(region.at[1], 0), left),
            lambda: (cut(own(right), 0), cut(region.at[0], 0), right),
            lambda: (cut(own(left), 1), cut(region.at[1], 1), left))[i]()
        remote(src, dst_ref, send.at[chunk, piece, int(i > 1)], recv.at[chunk, piece, stage, int(i > 1)], to).start()

    def took(buffer, sem):
        pltpu.make_async_copy(buffer, buffer, sem).wait()

    def step(chunk, k):
        stage = k // 2
        for piece in range(3):
            if k % 2:
                half = halves[(chunk * 3 + piece) * 2 + stage]
                took(half, recv.at[chunk, piece, stage, 0])
                axis = ORDERS[piece][2 - stage]
                for h, by in ((0, 1), (1, 3)):
                    mid = block(moved(at, axis, by), chunk, piece, stage)
                    add_into(half_of(mid, stage, piece, RCHUNKS[chunk][1], h), half.at[h])
                    start(chunk, piece, stage, 4 + h)
            else:
                if k > 0:
                    region = regions[slot(chunk, piece, stage - 1)]
                    took(region, recv.at[chunk, piece, stage - 1, 1])
                    add_into(block(at, chunk, piece, stage - 1), *[region.at[i] for i in range(region.shape[0])])
                    if stage < 3:
                        took(halves[(chunk * 3 + piece) * 2 + stage - 1], send.at[chunk, piece, 0])
                    took(region, send.at[chunk, piece, 1])
                if k < 6:
                    for i in range(3 if stage == 2 else 4):
                        start(chunk, piece, stage, i)

    def steps_after(table, index):
        for i, todo in table.items():
            @pl.when(index == i)
            def _(todo=todo):
                for chunk, k in todo:
                    step(chunk, k)

    def gradients(left, right, zh, col):
        for q in range(4):
            value = dot(left[q * 384:(q + 1) * 384, :], right, 1, 1).astype(BF16)
            part[zh, q, :, :, :, :, pl.ds(col, right.shape[0])] = value.reshape(4, 2, 3, 16, right.shape[0])

    def strip(q):
        return pl.ds(pl.multiple_of(q * 384, 128), 384)

    def fold(v):
        return v[:, 0:128] + v[:, 128:256] + v[:, 256:384] + v[:, 384:512]

    def row_sums(v):
        ones = jnp.ones((8, 128), BF16)
        a, b, _ = split(v)
        return (dot(ones, a, 1, 1) + dot(ones, b, 1, 1))[0:1]

    for ref in (dcbt, cross, dcum, ddt1, gskip, ggain):
        ref[...] = jnp.zeros_like(ref)
    first[1].wait()
    entered()
    step(0, 0)
    swap_sums = remote(sums, sums_in, swap_send.at[3], swap_recv.at[3], mate)
    swap_sums.start()
    for c in first[2:]:
        c.wait()
    swap_sums.wait()
    r_out = lax.rsqrt(sums[0:1, :] / INNER + EPS)
    k2 = r_out * r_out * r_out * (sums[1:2, :] + sums_in[1:2, :]) / INNER

    @pl.loop(0, 6)
    def _(m):
        zh, c, off, _ = group_at(m)
        cols = group_cols(prm, zh, c)
        for i in range(GROUP):
            r = slice(i * HEAD, (i + 1) * HEAD)
            rows = pl.ds(pl.multiple_of(off + i * HEAD, HEAD), HEAD)
            z = zt[rows, :].astype(F32)
            dg = dgt[rows, :].astype(F32)
            v = vt[rows, :].astype(F32)
            sz = sig(z)
            zs = z * sz
            dv = dg * cols[r, 5:6] * r_out - v * k2
            folds[0, r, :] = fold(dg * v * r_out)
            dyt[rows, :] = (dv * zs).astype(BF16)
            dzt[rows, :] = (dv * yt[rows, :] * (sz + zs * (1.0 - sz))).astype(BF16)
        prow[zh * 3 + c, 5:6, :] = row_sums(folds[0])
        gradients(xt, dzt[pl.ds(off, WIDE), :], zh, pl.multiple_of(768 + c * WIDE, WIDE))

    first[0].wait()
    step(0, 1)
    step(1, 0)
    loads[8].start()
    for c in second:
        c.wait()

    @pl.loop(0, 6)
    def _(m):
        zh, c, off, base = group_at(m)
        cc = pltpu.roll(cumc[...], 128 - base, 1)
        skips = group_skip(prm, zh, c)
        for i in range(GROUP):
            r = slice(i * HEAD, (i + 1) * HEAD)
            rows = pl.ds(pl.multiple_of(off + i * HEAD, HEAD), HEAD)
            skip = skips[i:i + 1, 0:1]
            xs = xst[rows, :].astype(F32)
            dyb = dyt[rows, :]
            dy = dyb.astype(F32)
            yssm = yt[rows, :] - skip * xs
            gskip[pl.ds(base + i, 1), :] = jnp.sum(dy * xs, axis=0, keepdims=True)
            dt = dtt[pl.ds(base + i, 1), :]
            cum = cumt[pl.ds(base + i, 1), :]
            xdt = xs * dt
            xdtb = xdt.astype(BF16)
            dxs = []
            for b in range(2):
                s = slice(b * SPAN, (b + 1) * SPAN)
                w = decay(cum, cc[s, i:i + 1], b)
                dxs.append(dot(dyb[:, s], (w * cbt[b]).astype(BF16), 1, 1))
                dcbt[b] += dot(xdtb[:, s], dyb[:, s], 0, 0) * w
            tail = jnp.exp(cum[:, SPAN - 1:SPAN] - cum[:, :SPAN])
            xe = (xdt[:, :SPAN] * tail).astype(BF16)
            dye = (dy[:, SPAN:] * jnp.exp(cum[:, SPAN:])).astype(BF16)
            ds = dot(dye, bc[SPAN:, 128:256]).astype(BF16)
            xe_all[r, :] = xe
            dye_all[r, :] = dye
            st_all[r, :] = dot(xe, bc[0:SPAN, 0:128]).astype(BF16)
            ds_all[r, :] = ds
            dxs[0] = dxs[0] + tail * dot(ds, bc[0:SPAN, 0:128], 1, 1)
            dx = jnp.concatenate(dxs, axis=1)
            dcum[pl.ds(base + i, 1), :] = jnp.sum(dy * yssm - xdtb.astype(F32) * dx, axis=0, keepdims=True)
            ddt1[pl.ds(base + i, 1), :] = jnp.sum(xs * dx, axis=0, keepdims=True)
            dyt[rows, :] = (dt * dx + skip * dy).astype(BF16)
            if i % 2:
                steps_after(SCAN_STEPS, m * 2 + i // 2)
        cross[1] += dot(st_all[...], dye_all[...], 0, 0)
        cross[0] += dot(ds_all[...], xe_all[...], 0, 0)

    upper = tri(SPAN, lambda r, c: r <= c).astype(F32)
    for b in range(2):
        s = slice(b * SPAN, (b + 1) * SPAN)
        d = (dcbt[b] * upper).astype(BF16)
        db = dot(bct[128:256, s], d, 1, 1)
        dc = dot(bct[0:128, s], d)
        dbct[0:128, s] = (db + cross[0] if b == 0 else db).astype(BF16)
        dbct[128:256, s] = (dc + cross[1] if b == 1 else dc).astype(BF16)
    swap_bc = remote(dbct, dbct_in, swap_send.at[1], swap_recv.at[1], mate)
    swap_bc.start()
    loads[6].start()

    dla = exact_dot(dcum[...], tri(T, lambda r, c: r >= c))
    for zh in range(2):
        rows = slice(zh * 16, (zh + 1) * 16)
        hc = prm[zh, :, 0:128].T
        rate = -jnp.exp(hc[:16, 7:8])
        d = dla[rows]
        dstep = (ddt1[rows, :] + rate * d) * sig(stept[rows, :].astype(F32) + hc[:16, 6:7])
        gd = jnp.sum(d * dtt[rows, :] * rate, axis=1, keepdims=True)
        hcol = jnp.concatenate([jnp.sum(dstep, axis=1, keepdims=True), gd, jnp.sum(gskip[rows, :], axis=1, keepdims=True),
                                jnp.zeros((16, 125), F32)], axis=1)
        hrow[:, zh * 128:(zh + 1) * 128] = jnp.concatenate([hcol, jnp.zeros((112, 128), F32)], axis=0).T[:8]
        keep = lax.broadcasted_iota(jnp.int32, (16, T), 0) < 12
        dstep_t[zh, 0:16, :] = jnp.where(keep, dstep, 0.0).astype(BF16)
        dstep_t[zh, 16:128, :] = jnp.zeros((112, T), BF16)


    swap_bc.wait_recv()
    for q in range(4):
        r = slice(q * 64, (q + 1) * 64)
        cols = spar[r]
        p, shifted = conv(statet[r, :].astype(F32), cols)
        sp = sig(p)
        dp = (dbct[r, :].astype(F32) + dbct_in[r, :].astype(F32)) * (sp + p * sp * (1.0 - sp))
        dstate[r, :] = conv_back(dp, cols).astype(BF16)
        dst[r, :] = jnp.concatenate([jnp.sum(dp * shifted[k], axis=1, keepdims=True) for k in range(4)]
                                    + [jnp.sum(dp, axis=1, keepdims=True), jnp.zeros((64, 123), F32)], axis=1)
    small[48:56, :] = dst[...].T[:8].astype(BF16)
    for zh in range(2):
        ld[0:64, :] = dstate[pl.ds(zh * 128 + pl.multiple_of(at["core"] * 64, 64), 64), :]
        ld[64:128, :] = dstep_t[zh, 0:64, :]
        gradients(xt, ld[...], zh, STATE_COL)

    step(4, 0)
    loads[6].wait()
    loads[8].wait()

    @pl.loop(0, 6)
    def _(m):
        zh, c, off, _ = group_at(m)
        cols = group_cols(prm, zh, c)
        for i in range(GROUP):
            r = slice(i * HEAD, (i + 1) * HEAD)
            rows = pl.ds(pl.multiple_of(off + i * HEAD, HEAD), HEAD)
            u = ut[rows, :].astype(F32)
            dp = dyt[rows, :].astype(F32) * dsil[rows, :].astype(F32)
            du = cols[r, 0:1] * dp
            folds[0, r, :] = fold(u * dp)
            folds[4, r, :] = fold(dp)
            for k in range(1, 4):
                ahead = sooner(dp, k)
                du = du + cols[r, k:k + 1] * ahead
                folds[k, r, :] = fold(u * ahead)
            dut[rows, :] = du.astype(BF16)
        for k in range(5):
            prow[zh * 3 + c, k:k + 1, :] = row_sums(folds[k])
        gradients(xt, dut[pl.ds(off, WIDE), :], zh, pl.multiple_of(INNER_COL + c * WIDE, 128))
        steps_after(CONV_STEPS, m)

    for q in range(6):
        small[q * 8:(q + 1) * 8, :] = prow[q].astype(BF16)
    small[56:64, :] = hrow[...].astype(BF16)

    def small_flights(s):
        slot_here = small_in.at[s, at["xyz"[s]]]
        return [remote(slot_here, slot_here, small_send.at[s, by - 1], small_recv.at[s, by - 1], moved(at, "xyz"[s], by)) for by in (1, 2, 3)]

    def small_start(s):
        small_in[s, at["xyz"[s]]] = small[...]
        for c in small_flights(s):
            c.start()

    def small_end(s):
        for c in small_flights(s):
            c.wait()
        total4 = small_in[s, 0].astype(F32) + small_in[s, 1].astype(F32) + small_in[s, 2].astype(F32) + small_in[s, 3].astype(F32)
        small[...] = total4.astype(BF16)
        if s == 2:
            gsmall[0:64, :] = total4

    small_start(0)
    step(3, 0)


    @pl.loop(0, 4)
    def _(q):
        more = [dot(wst[zh, q, :, :, :, :, pl.ds(128, 128)].reshape(384, 128), dstep_t[zh]) for zh in range(2)]
        both[...] = product(2 * q, dzt) + product(1 + 2 * q, dut) + (more[0] + more[1]).T
        total[:, strip(q)] = both[mine, :]
        branch[theirs, strip(q)] = both[theirs, :].astype(BF16)
        steps_after(TOKEN_STEPS, q)

    small_end(0)
    small_start(1)
    swap_dn = remote(branch.at[theirs], dn_in, swap_send.at[2], swap_recv.at[2], mate)
    swap_dn.start()
    own_state[...] = dstate[:, mine].T
    step(2, 2)
    swap_dn.wait()

    @pl.loop(0, 2)
    def _(q):
        r = pl.ds(pl.multiple_of(q * 128, 128), 128)
        full = total[r, :] + dn_in[r, :].astype(F32)
        for zh in range(2):
            full = full + dot(own_state[r, zh * 128:(zh + 1) * 128], wst[zh, :, :, :, :, :, pl.ds(0, 128)].reshape(1536, 128), 1, 1)
        h = hidden[r, :].astype(F32)
        r_in = lax.rsqrt(jnp.mean(h * h, axis=1, keepdims=True) + EPS)
        ggain[...] += jnp.sum(full * h * r_in, axis=0, keepdims=True)
        scaled = full * gain[...].reshape(1, 1536)
        back = scaled * r_in - h * (r_in * r_in * r_in * (jnp.sum(scaled * h, axis=1, keepdims=True) / 1536))
        grad_hidden[r, :] = (cot[r, :].astype(F32) + back).astype(BF16)

    def gain_peers(s):
        if s == 0:
            return [moved(at, "x", by) for by in (1, 2, 3)] + [mate] + [moved(mate, "x", by) for by in (1, 2, 3)]
        return [moved(at, "xyz"[s], by) for by in (1, 2, 3)]

    def gain_flights(s):
        here = gain_in.at[s, at["x"] * 2 + at["core"] if s == 0 else at["xyz"[s]]]
        return [remote(here, here, gain_send.at[s, i], gain_recv.at[s, i], to) for i, to in enumerate(gain_peers(s))]

    def gain_start(s, rows):
        gain_in[s, at["x"] * 2 + at["core"] if s == 0 else at["xyz"[s]]] = rows
        for c in gain_flights(s):
            c.start()

    def gain_end(s):
        for c in gain_flights(s):
            c.wait()
        rows = gain_in[s, 0]
        for i in range(1, 8 if s == 0 else 4):
            rows = rows + gain_in[s, i]
        return rows

    gain_start(0, jnp.concatenate([ggain[:, q * 256:(q + 1) * 256] for q in range(6)] + [jnp.zeros((2, 256), F32)], axis=0))
    put(4, grad_hidden)
    step(3, 2)
    step(4, 2)
    step(1, 4)

    def output(first_strip):
        @pl.loop(first_strip, first_strip + 2)
        def _(q):
            branch[:, strip(q)] = product(8 + q, gat).astype(BF16)

    output(0)
    step(2, 3)
    step(3, 3)
    step(4, 3)
    gain_start(1, gain_end(0))
    small_end(1)
    small_start(2)
    output(2)
    swap_br = remote(branch.at[theirs], br_in, swap_send.at[0], swap_recv.at[0], mate)
    swap_br.start()
    step(2, 4)
    step(3, 4)
    step(4, 4)
    gain_start(2, gain_end(1))
    step(1, 6)
    step(0, 6)
    step(4, 6)
    own = units(at, "")
    for piece in range(3):
        quarter[piece * 16:(piece + 1) * 16, :] = part[own + (piece, slice(None), pl.ds(STATE_COL, 128))].astype(F32)
    thirds = [remote(quarter, quarters.at[i], q_send.at[i], q_recv.at[i], to) for i, to in enumerate((mate, far, far_mate))]
    for c in thirds:
        c.start()
    step(2, 6)
    step(3, 6)
    for piece in range(3):
        out[piece * 16:(piece + 1) * 16, :] = part[own + (piece, slice(None), pl.ds(0, 2304))]
    put(0, out)
    swap_br.wait()

    @pl.loop(0, 2)
    def _(q):
        r = pl.ds(pl.multiple_of(q * 128, 128), 128)
        own_rows = pl.ds(pl.multiple_of(at["core"] * 256 + q * 128, 128), 128)
        branch[own_rows, :] = (hidden[r, :].astype(F32) + branch[own_rows, :].astype(F32) + br_in[r, :].astype(F32)).astype(BF16)

    put(3, branch.at[mine])
    small_end(2)
    gsmall[64:72, :] = gain_end(2)
    put(2, gsmall)
    for c in thirds:
        c.wait()
    low = at["core"] == 0
    q0, q1, q2, q3 = quarter[...], quarters[0], quarters[1], quarters[2]
    here = jnp.where(low, jnp.concatenate([q0[:, :64], q1[:, :64]], axis=1), jnp.concatenate([q1[:, :64], q0[:, :64]], axis=1))
    there = jnp.where(low, jnp.concatenate([q2[:, :64], q3[:, :64]], axis=1), jnp.concatenate([q3[:, :64], q2[:, :64]], axis=1))
    first = at["z"] < 2
    gstate[:, 0:128] = jnp.where(first, here, there)
    gstate[:, 128:256] = jnp.where(first, there, here)
    gstate[:, 256:384] = q0
    put(1, gstate)
    swap_bc.wait_send()
    for c in out_copies:
        c.wait()


def backward(tall, small, hidden, cot, gain):
    n = len(RCHUNKS)
    results = [sds((48, 2304), BF16), sds((48, 384)), sds((SUMS + 8, 256)), sds((256, 1536), BF16), sds((256, 1536), BF16)]
    any_ = pl.BlockSpec(memory_space=pl.ANY)
    shapes = [(stage, piece, RCHUNKS[chunk][1]) for chunk in range(n) for piece in range(3) for stage in range(3)]
    regions = [pltpu.VMEM((3 if s[0] == 2 else 2,) + region_shape(*s), BF16) for s in shapes]
    halves = [pltpu.VMEM((2,) + half_shape(*s), BF16) for s in shapes if s[0] < 2]
    dma = pltpu.SemaphoreType.DMA
    v = lambda shape, dtype=F32: pltpu.VMEM(shape, dtype)
    return pl.pallas_call(
        backward_kernel,
        in_specs=[any_] * (len(tall) + len(small) + 3),
        out_specs=[any_] * 5,
        out_shape=results,
        scratch_shapes=[v((2, 4, 4, 2, 3, 16, RCOLS), BF16)] + regions + halves + [
            v((1536, T), BF16)] * 6 + [v((1536, T)), v((3, 2, 4, 2, 3, 16, 768), BF16), v((2, 4, 4, 2, 3, 16, 256), BF16),
            v((256, 1536)), v((T, 384)), v((2, SPAN, SPAN)), v((128, T), BF16), v((WIDE, SPAN), BF16), v((WIDE, SPAN), BF16),
            v((WIDE, 128), BF16), v((WIDE, 128), BF16), v((2, 128, SPAN)), v((6, 8, WIDE)), v((8, 256)),
            v((32, T)), v((32, T)), v((32, T)), v((2, 128, T), BF16), v((256, T), BF16), v((256, T), BF16),
            v((256, 1536), BF16), v((T, 1536), BF16), v((256, 1536), BF16),
            v((256, T), BF16), v((256, 128)), v((5, WIDE, 128))] + [v(a.shape, a.dtype) for a in (*small, hidden, cot, gain, *results[:3], results[4])] + [ v((SUMS, 256), BF16), v((3, 4, SUMS, 256), BF16), v((256, 256), BF16), v((1, 1536)), v((3, 8, 8, 256)), v((48, 128)), v((3, 48, 128)), v((8, T)),
            dma((n, 3, 2)), dma((n, 3, 3, 2)), dma((25,)), dma((3,)), dma((4,)), dma((4,)), dma((3, 3)), dma((3, 3)), dma((3, 7)), dma((3, 7)), dma((3,)), dma((3,)), dma((5,))],
        compiler_params=pltpu.CompilerParams(collective_id=1, has_side_effects=True, vmem_limit_bytes=65400 << 10),
    )(*tall, *small, hidden, cot, gain)


def finish_kernel(out, gstate, small, new_h, grad_h, new_hidden, grad_hidden, in_gain, main, step, state, inner, inner_bias, cstate, cstate_bias,
                  bias, log, skip, out_gain, proj_out):
    new_hidden[...] = new_h[...]
    grad_hidden[...] = grad_h[...]
    z_hi = lax.axis_index("tensor") // 2
    proj_out[...] = out[:, 0:768].astype(F32)
    main[:, 0, :] = out[:, 768:1536].astype(F32)
    main[:, 1, :] = out[:, 1536:2304].astype(F32)
    step[...] = gstate[:, 256:384].T[64:76]
    state[...] = gstate[:, 0:256]
    for c in range(3):
        rows = small[pl.ds(pl.multiple_of(z_hi * 24 + c * 8, 8), 8), :]
        cols = slice(c * 256, (c + 1) * 256)
        inner[:, cols] = rows[0:4]
        inner_bias[cols] = rows[4:5].reshape(256)
        out_gain[cols] = rows[5:6].reshape(256)
    cstate[...] = small[48:52, :]
    cstate_bias[...] = small[52:53, :].reshape(256)
    for q in range(6):
        in_gain[q * 256:(q + 1) * 256] = small[64 + q:65 + q, :].reshape(256)
    heads = small[56:64, pl.ds(pl.multiple_of(z_hi * 128, 128), 128)]
    for i, ref in enumerate((bias, log, skip)):
        ref[...] = heads[i:i + 1, 0:12].reshape(12)


def finish(out, gstate, small, new_hidden, grad_hidden):
    vm = pl.BlockSpec(memory_space=pltpu.VMEM)
    shapes = [sds(s) for s in ((1536,), (48, 2, 768), (12, 48), (48, 256), (4, 768), (768,), (4, 256), (256,), (12,), (12,), (12,), (768,), (48, 768))]
    return pl.pallas_call(
        finish_kernel, out_shape=[sds((256, 1536), BF16)] * 2 + shapes, in_specs=[vm] * 5, out_specs=[vm] * 15,
    )(out, gstate, small, new_hidden, grad_hidden)


def per_device(hidden, in_gain, proj_main, proj_step, proj_state, conv_inner, conv_inner_bias, conv_state, conv_state_bias,
               step_bias, decay_log, skip_gain, out_gain, proj_out, grad_out):
    outs = forward(proj_main.reshape(48, 1536), proj_step.T, proj_state, proj_out, hidden, grad_out, conv_inner, conv_state,
                   conv_inner_bias, out_gain, conv_state_bias, in_gain, step_bias, decay_log, skip_gain)
    results = backward(outs[:12], outs[12:], hidden, grad_out, in_gain)
    new_hidden, grad_hidden, ggain, main, step, *others = finish(*results)
    return (new_hidden, grad_hidden, ggain, main, step.T, *others)


def solution(mesh):
    rows = P(("dp", "tensor"), None)
    per_head = P("tensor")
    in_specs = (rows, P(), P("dp", None, "tensor"), P("dp", "tensor"), P("dp", None), P(None, "tensor"), per_head, P(), P(),
                per_head, per_head, per_head, per_head, P("dp", "tensor"), rows)
    out_specs = (rows, rows, P(), P("dp", None, "tensor"), P("dp", "tensor"), P("dp", None), P(None, "tensor"), per_head, P(), P(),
                 per_head, per_head, per_head, per_head, P("dp", "tensor"))
    return jax.shard_map(per_device, mesh=mesh, in_specs=in_specs, out_specs=out_specs, check_vma=False)
```

```python
import functools

import jax
import jax.numpy as jnp
from jax import lax
from jax.experimental import pallas as pl
from jax.experimental.pallas import tpu as pltpu
from jax.sharding import PartitionSpec as P

MESH = pl.DeviceIdType.MESH
F32, BF16 = jnp.float32, jnp.bfloat16
EPS = 1e-5
T, SPAN, HEAD, GROUP = 512, 256, 64, 4
WIDE = GROUP * HEAD
INNER = 3072
COLS = 2560
STAGED = ((0, 256), (256, 768), (1024, 768), (1792, 768))
ORDERS = ("xyz", "yzx", "zxy")
RCHUNKS = ((0, 768), (768, 768), (1536, 512), (2048, 256), (2304, 128))
STATE_COL, INNER_COL = 2304, 1536
RCOLS = 2432
SUMS = 64


def sds(shape, dtype=F32):
    return jax.ShapeDtypeStruct(shape, dtype)


def place():
    dp, tp = lax.axis_index("dp"), lax.axis_index("tensor")
    return dict(x=dp // 8, y=(dp // 2) % 4, z=(tp // 2) * 2 + dp % 2, core=tp % 2)


def device_at(at):
    return ((at["x"] * 4 + at["y"]) * 2 + at["z"] % 2, (at["z"] // 2) * 2 + at["core"])


def moved(at, axis, by):
    return {**at, axis: (at[axis] + by) % 4}


def units(at, whole):
    return (slice(None) if "z" in whole else at["z"] // 2, slice(None) if "x" in whole else at["x"],
            slice(None) if "y" in whole else at["y"], slice(None) if "z" in whole else at["z"] % 2)


def greet(others):
    barrier = pltpu.get_barrier_semaphore()
    for other in others:
        pl.semaphore_signal(barrier, inc=1, device_id=device_at(other), device_id_type=MESH)
    return lambda: pl.semaphore_wait(barrier, len(others))


def half_of(ref, stage, piece, width, half):
    if stage == 0:
        return ref.at[pl.ds(2 * half, 2)] if piece == 0 else ref.at[:, pl.ds(2 * half, 2)]
    if stage == 1:
        return ref.at[pl.ds(2 * half, 2)] if piece < 2 else ref.at[half]
    return ref.at[:, pl.ds(half * (width // 2), width // 2)]


def half_shape(stage, piece, width):
    if stage == 0:
        return (2, 4, 16, width) if piece == 0 else (2, 2, 2, 16, width)
    return (2, 16, width)


def region_shape(stage, piece, width):
    whole = ORDERS[piece][:2 - stage]
    dims = ([2] if "z" in whole else []) + ([4] if "x" in whole else []) + ([4] if "y" in whole else []) + ([2] if "z" in whole else [])
    return tuple(dims) + (16, width)


def dot(a, b, ca=1, cb=0):
    return lax.dot_general(a, b, (((ca,), (cb,)), ((), ())), preferred_element_type=F32)


def lanes(rows, width=T):
    return lax.broadcasted_iota(jnp.int32, (rows, width), 1)


def later(u, k):
    return jnp.where(lanes(u.shape[0]) >= k, pltpu.roll(u, k, 1), 0.0) if k else u


def sooner(u, k):
    return jnp.where(lanes(u.shape[0]) < T - k, pltpu.roll(u, T - k, 1), 0.0) if k else u


def sig(v):
    return 1.0 / (1.0 + jnp.exp(-v))


def split(v):
    a = v.astype(BF16)
    r = v - a.astype(F32)
    b = r.astype(BF16)
    return a, b, (r - b.astype(F32)).astype(BF16)


def exact_dot(v, ones):
    n = v.shape[0]
    s = dot(jnp.concatenate(split(v), axis=0), ones)
    return s[:n] + s[n:2 * n] + s[2 * n:]


def tri(n, keep):
    r = lax.broadcasted_iota(jnp.int32, (n, n), 0)
    c = lax.broadcasted_iota(jnp.int32, (n, n), 1)
    return jnp.where(keep(r, c), 1.0, 0.0).astype(BF16)


def conv(u, cols):
    shifted = [later(u, k) for k in range(4)]
    p = cols[:, 4:5] + cols[:, 0:1] * shifted[0]
    for k in range(1, 4):
        p = p + cols[:, k:k + 1] * shifted[k]
    return p, shifted


def conv_back(dp, cols):
    du = cols[:, 0:1] * dp
    for k in range(1, 4):
        du = du + cols[:, k:k + 1] * sooner(dp, k)
    return du


def decay(cum_row, cum_col, b):
    return jnp.exp(jnp.minimum(cum_row[:, b * SPAN:(b + 1) * SPAN] - cum_col, 0.0))


def group_at(n):
    zh, c = n % 2, n // 2
    return zh, c, pl.multiple_of((zh * 3 + c) * WIDE, WIDE), zh * 16 + c * GROUP


def group_cols(prm, zh, c):
    return prm[zh, :, pl.ds(pl.multiple_of(c * WIDE, WIDE), WIDE)].T


def group_skip(prm, zh, c):
    cols = prm[zh, :, 0:128].T
    return pltpu.roll(jnp.broadcast_to(cols[:, 8:9], (128, 128)), 128 - c * GROUP, 0)


def forward_kernel(main_h, step_h, state_h, out_h, hidden_h, cot_h, cinner_h, cstate_h, offset_h, gain_h, state_offset_h, in_gain_h, bias_h, log_h, skip_h,
                   xt_o, zt_o, ut_o, dgt_o, vt_o, xst_o, dsil_o, gat_o, yt_o, w_o, wst_o, pa_o,
                   *rest):
    small_o, (step_w, hidden, cinner, cstate, offset, gain, state_offset, in_gain, bias, log, skip_gain, w, x, g, xt, gt, zt, ut, dgt, vt, xst, dsil, gat, yt, pa, acc, acc_in,
              sums, dtt, cumt, cumc, stept, statet, bc, bct, cbt, prm, spar,
              send, recv, local, w_sem, out_sem, swap_send, swap_recv) = rest[:11], rest[11:]
    at = place()
    z_hi = at["z"] // 2
    mate = {**at, "core": 1 - at["core"]}
    far = moved(at, "z", 2)
    entered = greet([moved(at, axis, by) for axis in "xyz" for by in (1, 3)] + [mate, far])
    mine = pl.ds(pl.multiple_of(at["core"] * 256, 256), 256)
    own_unit = w.at[units(at, "")]
    moves = [(step_h, step_w), (hidden_h, hidden), (cot_h, g.at[mine]), (cinner_h, cinner), (cstate_h, cstate), (offset_h, offset), (gain_h, gain),
             (state_offset_h, state_offset), (in_gain_h, in_gain), (bias_h, bias), (log_h, log), (skip_h, skip_gain)]
    params = len(moves)
    for piece in range(3):
        rows = pl.ds(piece * 16, 16)
        for source, begin, width in ((state_h.at[rows, pl.ds(pl.multiple_of(z_hi * 128, 128), 128)], 0, 128), (main_h.at[rows, pl.ds(768, 768)], 256, 768),
                                     (main_h.at[rows, pl.ds(0, 768)], 1024, 768), (out_h.at[rows], 1792, 768)):
            moves.append((source, own_unit.at[piece, :, pl.ds(begin, width)]))
    moves = [pltpu.make_async_copy(a, b, local.at[i]) for i, (a, b) in enumerate(moves)]
    for c in moves:
        c.start()
    moves[0].wait()
    step_rows = jnp.concatenate([step_w[...].astype(F32), jnp.zeros((116, 48), F32)], axis=0).T.astype(BF16)
    for piece in range(3):
        w[units(at, "") + (piece, slice(None), pl.ds(128, 128))] = step_rows[piece * 16:(piece + 1) * 16]
    for c in moves[params:]:
        c.wait()
    entered()

    def part(where, piece, stage, chunk):
        begin, width = STAGED[chunk] if stage == 2 else (0, COLS)
        return w.at[units(where, ORDERS[piece][:stage]) + (piece, slice(None), pl.ds(begin, width))]

    def flight(piece, stage, chunk, kind):
        axis, by = ORDERS[piece][stage], (1, 3)[kind % 2]
        width = STAGED[chunk][1] if stage == 2 else COLS
        if kind < 2:
            target = source = part(at, piece, stage, chunk)
        else:
            target = source = half_of(part(moved(at, axis, -by), piece, stage, chunk), 2 - stage, piece, width, kind - 2)
        sem = (stage + chunk if stage == 2 else stage, piece, kind)
        return pltpu.make_async_remote_copy(src_ref=source, dst_ref=target, send_sem=send.at[sem], recv_sem=recv.at[sem],
                                            device_id=device_at(moved(at, axis, by)), device_id_type=MESH)

    def fulls(stage, chunk=0):
        for piece in range(3):
            if stage > 0 and chunk == 0:
                for kind in (2, 3):
                    flight(piece, stage - 1, 0, kind).wait_recv()
            for kind in (0, 1):
                flight(piece, stage, chunk, kind).start()

    def halves(stage, chunk=0):
        for piece in range(3):
            for kind in (0, 1):
                flight(piece, stage, chunk, kind).wait_recv()
                flight(piece, stage, chunk, kind + 2).start()

    def arrived(chunk):
        for piece in range(3):
            for kind in (2, 3):
                flight(piece, 2, chunk, kind).wait_recv()

    fulls(0)
    for c in moves[1:params]:
        c.wait()

    prm[z_hi] = jnp.zeros((16, 768), F32)
    prm[z_hi, 0:4, :] = cinner[...]
    prm[z_hi, 4:5, :] = offset[...].reshape(1, 768)
    prm[z_hi, 5:6, :] = gain[...].reshape(1, 768)
    for i, ref in enumerate((bias, log, skip_gain)):
        prm[z_hi, 6 + i:7 + i, 0:12] = ref[...].reshape(1, 12)
    h = hidden[...].astype(F32)
    scale = lax.rsqrt(jnp.mean(h * h, axis=1, keepdims=True) + EPS)
    x[mine, :] = (h * scale * in_gain[...].reshape(1, 1536)).astype(BF16)
    swaps = [pltpu.make_async_remote_copy(src_ref=s, dst_ref=s, send_sem=swap_send.at[i], recv_sem=swap_recv.at[i],
                                          device_id=device_at(to), device_id_type=MESH)
             for i, (s, to) in enumerate([(x.at[mine], mate), (g.at[mine], mate), (prm.at[z_hi], far)])]
    for c in swaps:
        c.start()
    spar[...] = jnp.concatenate([cstate[...], state_offset[...].reshape(1, 256), jnp.zeros((11, 256), F32)], axis=0).T

    halves(0)
    fulls(1)
    out_copies = []

    def put(i, source, target):
        c = pltpu.make_async_copy(source, target, out_sem.at[i])
        c.start()
        out_copies.append(c)

    for c in swaps[:2]:
        c.wait_recv()
    xt[...] = x[...].T
    gt[...] = g[...].T
    put(0, xt, xt_o)
    halves(1)
    swaps[2].wait_recv()
    acc[...] = jnp.zeros_like(acc)
    sums[...] = jnp.zeros_like(sums)
    cumc[...] = jnp.zeros_like(cumc)
    fulls(2, 0)
    fulls(2, 1)
    halves(2, 0)
    halves(2, 1)
    fulls(2, 2)
    arrived(0)
    put(2, w.at[:, :, :, :, :, :, pl.ds(0, 256)], wst_o)

    def weight(zh, begin):
        return w[zh, :, :, :, :, :, pl.ds(begin, WIDE)].reshape(1536, WIDE)

    for zh in range(2):
        raw = dot(x[...], weight(zh, 0)).T.astype(BF16)
        statet[zh * 128:(zh + 1) * 128, :] = raw[:128]
        stept[zh * 16:(zh + 1) * 16, :] = raw[128:144]
    for q in range(4):
        r = slice(q * 64, (q + 1) * 64)
        p, _ = conv(statet[r, :].astype(F32), spar[r])
        bct[r, :] = (p * sig(p)).astype(BF16)
    bc[...] = bct[...].T
    upper = tri(SPAN, lambda r, c: r <= c)
    for b in range(2):
        rows = pl.ds(b * SPAN, SPAN)
        cbt[b] = dot(bc[rows, 0:128], bc[rows, 128:256], 1, 1) * upper.astype(F32)
    for zh in range(2):
        cols = prm[zh, :, 0:128].T
        v = stept[zh * 16:(zh + 1) * 16, :].astype(F32) + cols[:16, 6:7]
        dt = jnp.maximum(v, 0.0) + jnp.log1p(jnp.exp(-jnp.abs(v)))
        dtt[zh * 16:(zh + 1) * 16, :] = dt
        la = dt * -jnp.exp(cols[:16, 7:8])
        for b in range(2):
            cumt[zh * 16:(zh + 1) * 16, b * SPAN:(b + 1) * SPAN] = exact_dot(la[:, b * SPAN:(b + 1) * SPAN], upper)
    cumc[...] = jnp.concatenate([cumt[...], jnp.zeros((96, T), F32)], axis=0).T
    for i, ref in enumerate((dtt, cumt, cumc, stept, statet, bc, bct, cbt, prm, spar)):
        put(10 + i, ref, small_o[1 + i])

    def put_weights(kind, begin):
        for n in range(8):
            zh, q = n % 2, n // 2
            pltpu.make_async_copy(w.at[zh, q, :, :, :, :, pl.ds(begin, 768)], w_o.at[kind, q, zh], w_sem.at[kind]).start()

    arrived(1)
    put_weights(2, 256)

    @pl.loop(0, 6)
    def _(n):
        zh, c, off, base = group_at(n)
        cols = group_cols(prm, zh, c)
        skip = group_skip(prm, zh, c)
        cc = pltpu.roll(cumc[...], 128 - base, 1)
        ut[pl.ds(off, WIDE), :] = dot(x[...], weight(zh, pl.multiple_of(256 + c * WIDE, WIDE))).T.astype(BF16)
        for i in range(GROUP):
            r = slice(i * HEAD, (i + 1) * HEAD)
            rows = pl.ds(pl.multiple_of(off + i * HEAD, HEAD), HEAD)
            p, _ = conv(ut[rows, :].astype(F32), cols[r])
            sp = sig(p)
            xs = p * sp
            xsb = xs.astype(BF16)
            xst[rows, :] = xsb
            dsil[rows, :] = (sp + xs * (1.0 - sp)).astype(BF16)
            xs = xsb.astype(F32)
            cum = cumt[pl.ds(base + i, 1), :]
            xdt = xs * dtt[pl.ds(base + i, 1), :]
            xdtb = xdt.astype(BF16)
            ys = []
            for b in range(2):
                m = (decay(cum, cc[b * SPAN:(b + 1) * SPAN, i:i + 1], b) * cbt[b]).astype(BF16)
                ys.append(dot(xdtb[:, b * SPAN:(b + 1) * SPAN], m))
            tail = jnp.exp(cum[:, SPAN - 1:SPAN] - cum[:, :SPAN])
            state = dot((xdt[:, :SPAN] * tail).astype(BF16), bc[0:SPAN, 0:128]).astype(BF16)
            ys[1] = ys[1] + jnp.exp(cum[:, SPAN:]) * dot(state, bc[SPAN:, 128:256], 1, 1)
            yt[rows, :] = jnp.concatenate(ys, axis=1) + skip[i:i + 1, 0:1] * xs

        @pl.when(n == 2)
        def _():
            halves(2, 2)
            fulls(2, 3)

    put(3, xst, xst_o)
    put(4, yt, yt_o)
    put(5, ut, ut_o)
    put(9, dsil, dsil_o)
    arrived(2)
    put_weights(1, 1024)

    @pl.loop(0, 6)
    def _(n):
        zh, c, off, _ = group_at(n)
        zt[pl.ds(off, WIDE), :] = dot(x[...], weight(zh, pl.multiple_of(1024 + c * WIDE, WIDE))).T.astype(BF16)
        for i in range(GROUP):
            rows = pl.ds(pl.multiple_of(off + i * HEAD, HEAD), HEAD)
            z = zt[rows, :].astype(F32)
            vb = (yt[rows, :] * (z * sig(z))).astype(BF16)
            vt[rows, :] = vb
            v = vb.astype(F32)
            acc[0, 0:1, :] += jnp.sum(v * v, axis=0, keepdims=True)

        @pl.when(n == 3)
        def _():
            halves(2, 3)

    put(6, zt, zt_o)
    put(7, vt, vt_o)

    c = pltpu.make_async_remote_copy(src_ref=acc.at[0], dst_ref=acc_in.at[0], send_sem=swap_send.at[3], recv_sem=swap_recv.at[3],
                                     device_id=device_at(mate), device_id_type=MESH)
    c.start()
    c.wait()
    sums[0:1, :] = acc[0, 0:1] + acc_in[0, 0:1]

    r_out = lax.rsqrt(sums[0:1, :] / INNER + EPS)

    @pl.loop(0, 6)
    def _(n):
        zh, c, off, _ = group_at(n)
        cols = group_cols(prm, zh, c)
        for i in range(GROUP):
            rows = pl.ds(pl.multiple_of(off + i * HEAD, HEAD), HEAD)
            gat[rows, :] = (vt[rows, :].astype(F32) * r_out * cols[i * HEAD:(i + 1) * HEAD, 5:6]).astype(BF16)
        value = dot(gt[...], gat[pl.ds(off, WIDE), :], 1, 1).astype(BF16)
        pa[zh, :, :, :, :, :, pl.ds(pl.multiple_of(c * WIDE, WIDE), WIDE)] = value.reshape(4, 4, 2, 3, 16, WIDE)

    put(21, gat, gat_o)
    put(22, pa, pa_o)
    arrived(3)
    put_weights(0, 1792)

    @pl.loop(0, 6)
    def _(n):
        zh, c, off, _ = group_at(n)
        cols = group_cols(prm, zh, c)
        dgt[pl.ds(off, WIDE), :] = dot(g[...], weight(zh, pl.multiple_of(1792 + c * WIDE, WIDE))).T.astype(BF16)
        for i in range(GROUP):
            rows = pl.ds(pl.multiple_of(off + i * HEAD, HEAD), HEAD)
            s = dgt[rows, :].astype(F32) * cols[i * HEAD:(i + 1) * HEAD, 5:6] * vt[rows, :].astype(F32)
            acc[1, 0:1, :] += jnp.sum(s, axis=0, keepdims=True)

    put(8, dgt, dgt_o)
    sums[1:2, :] = acc[1, 0:1]
    put(20, sums, small_o[0])
    for piece in range(3):
        for kind in range(4):
            for stage in range(2):
                flight(piece, stage, 0, kind).wait_send()
            for chunk in range(4):
                flight(piece, 2, chunk, kind).wait_send()
    for s in swaps:
        s.wait_send()
    for kind in range(3):
        pltpu.make_async_copy(w_o.at[kind], w_o.at[kind], w_sem.at[kind]).wait()
    for c in out_copies:
        c.wait()


def forward(main, step_w, *others):
    any_ = pl.BlockSpec(memory_space=pl.ANY)
    dma = pltpu.SemaphoreType.DMA
    tall = [sds((1536, T), BF16)] * 9 + [sds((1536, T))]
    big = tall[1:] + [sds((3, 4, 2, 4, 2, 3, 16, 768), BF16), sds((2, 4, 4, 2, 3, 16, 256), BF16), sds((2, 4, 4, 2, 3, 16, 768), BF16)]
    small = [sds((8, T)), sds((32, T)), sds((32, T)), sds((T, 128)), sds((32, T), BF16), sds((256, T), BF16), sds((T, 256), BF16),
             sds((256, T), BF16), sds((2, SPAN, SPAN)), sds((2, 16, 768)), sds((256, 16))]
    return pl.pallas_call(
        forward_kernel, out_shape=big + small, in_specs=[any_] * (2 + len(others)), out_specs=[any_] * 23,
        scratch_shapes=[pltpu.VMEM(a.shape, a.dtype) for a in (step_w, others[2], *others[4:])] + [
                        pltpu.VMEM((2, 4, 4, 2, 3, 16, COLS), BF16), pltpu.VMEM((T, 1536), BF16),
                        pltpu.VMEM((T, 1536), BF16)] + [pltpu.VMEM(s.shape, s.dtype) for s in (*tall, big[-1])] + [
            pltpu.VMEM((2, 8, T), F32), pltpu.VMEM((2, 8, T), F32)] + [pltpu.VMEM(s.shape, s.dtype) for s in small] + [
            dma((6, 3, 4)), dma((6, 3, 4)), dma((25,)), dma((3,)), dma((23,)), dma((4,)), dma((4,))],
        compiler_params=pltpu.CompilerParams(collective_id=0, has_side_effects=True, vmem_limit_bytes=60 << 20),
    )(main, step_w, *others)


SCAN_STEPS = {7: [(0, 2)], 11: [(1, 1)]}
CONV_STEPS = {1: [(0, 3)], 3: [(2, 0)], 5: [(1, 2), (0, 4)]}
TOKEN_STEPS = {0: [(1, 3)], 1: [(2, 1)], 2: [(3, 1), (4, 1)]}


def add_into(target, *others):
    def add(t, o):
        v = t[...].astype(F32)
        for other in o:
            v = v + other[...].astype(F32)
        t[...] = v.astype(BF16)
    if len(target.shape) == 2:
        add(target, others)
    else:
        @pl.loop(0, target.shape[0])
        def _(i):
            add(target.at[i], [o.at[i] for o in others])


def backward_kernel(xt_h, zt_h, ut_h, dgt_h, vt_h, xst_h, dsil_h, gat_h, yt_h, w_h, wst_h, pa_h,
                    *rest_refs):
    small_h, outs_h, scratch = rest_refs[:14], rest_refs[14:19], rest_refs[19:]
    n = len(RCHUNKS)
    part, regions, halves = scratch[0], scratch[1:1 + 9 * n], scratch[1 + 9 * n:1 + 15 * n]
    (xt, xst, zt, dgt, vt, gat, yt, wbuf, wst, total, both, dcbt, ld, dye_all, xe_all, st_all, ds_all, cross, prow, hrow,
     dcum, ddt1, gskip, dstep_t, dbct, dbct_in, dn_in, branch, br_in, dstate, dst, folds,
     sums, dtt, cumt, cumc, stept, statet, bc, bct, cbt, prm, spar, hidden, cot, gain, out, gstate, gsmall, grad_hidden, small, small_in, own_state, ggain, gain_in, quarter, quarters, sums_in,
     send, recv, load_sem, w_sem, swap_send, swap_recv, small_send, small_recv, gain_send, gain_recv, q_send, q_recv, out_sem) = scratch[1 + 15 * n:]
    ut, dyt, dzt, dsil, dut = xst, zt, dgt, vt, zt
    at = place()
    mate = {**at, "core": 1 - at["core"]}
    far = moved(at, "z", 2)
    far_mate = {**far, "core": 1 - at["core"]}
    entered = greet([moved(at, axis, by) for axis in "xyz" for by in (1, 2, 3)] + [mate, far_mate]
                    + [moved(mate, "x", by) for by in (1, 2, 3)]
                    + [moved(moved(at, "y", a), "z", b) for a in (1, 2, 3) for b in (1, 2, 3)])
    mine = pl.ds(pl.multiple_of(at["core"] * 256, 256), 256)
    theirs = pl.ds(pl.multiple_of((1 - at["core"]) * 256, 256), 256)

    loads = [pltpu.make_async_copy(s, d, load_sem.at[i]) for i, (s, d) in enumerate(
        [(vt_h, vt), (yt_h, yt), (zt_h, zt), (dgt_h, dgt), (xt_h, xt), (xst_h, xst), (ut_h, ut), (wst_h, wst), (dsil_h, dsil), (gat_h, gat), (pa_h, part.at[..., pl.ds(0, 768)])]
        + list(zip(small_h, (sums, dtt, cumt, cumc, stept, statet, bc, bct, cbt, prm, spar, hidden, cot, gain))))]
    first = [loads[i] for i in (10, 11, 20, 0, 1, 2, 3, 4)]
    second = [loads[i] for i in (9, 5, 7, *range(12, 20), *range(21, 25))]
    out_copies = []

    def put(i, source):
        c = pltpu.make_async_copy(source, outs_h[i], out_sem.at[i])
        c.start()
        out_copies.append(c)

    def weights(i):
        late = i >= 8
        return pltpu.make_async_copy(w_h.at[jnp.where(late, 0, 1 + i % 2), jnp.where(late, i - 8, i // 2)], wbuf.at[i % 3], w_sem.at[i % 3])

    def product(i, values):
        weights(i).wait()

        @pl.when(i + 2 < 12)
        def _():
            weights(i + 2).start()
        return (dot(wbuf[i % 3, 0].reshape(384, 768), values[0:768, :]) + dot(wbuf[i % 3, 1].reshape(384, 768), values[768:1536, :])).T

    for c in first:
        c.start()
    weights(0).start()
    weights(1).start()
    for c in second:
        c.start()

    def remote(src, dst_ref, s, r, to):
        return pltpu.make_async_remote_copy(src_ref=src, dst_ref=dst_ref, send_sem=s, recv_sem=r, device_id=device_at(to), device_id_type=MESH)

    def block(where, chunk, piece, stage):
        begin, width = RCHUNKS[chunk]
        return part.at[units(where, ORDERS[piece][:2 - stage]) + (piece, slice(None), pl.ds(begin, width))]

    def slot(chunk, piece, stage):
        return (chunk * 3 + piece) * 3 + stage

    def start(chunk, piece, stage, i):
        axis = ORDERS[piece][2 - stage]
        region = regions[slot(chunk, piece, stage)]
        right, left, opposite = moved(at, axis, 1), moved(at, axis, 3), moved(at, axis, 2)
        if (chunk, stage) == (0, 0) and i < 4:
            own = lambda where: pa_h.at[units(where, ORDERS[piece][:2]) + (piece,)]
        else:
            own = lambda where: block(where, chunk, piece, stage)
        if stage == 2:
            to = (right, left, opposite)[i]
            remote(own(to), region.at[i], send.at[chunk, piece, 1], recv.at[chunk, piece, 2, 1], to).start()
            return
        half = halves[(chunk * 3 + piece) * 2 + stage]
        cut = lambda ref, h: half_of(ref, stage, piece, RCHUNKS[chunk][1], h)
        src, dst_ref, to = (
            lambda: (cut(own(opposite), 0), half.at[0], right),
            lambda: (cut(own(opposite), 1), half.at[1], left),
            lambda: (cut(own(right), 1), cut(region.at[0], 1), right),
            lambda: (cut(own(left), 0), cut(region.at[1], 0), left),
            lambda: (cut(own(right), 0), cut(region.at[0], 0), right),
            lambda: (cut(own(left), 1), cut(region.at[1], 1), left))[i]()
        remote(src, dst_ref, send.at[chunk, piece, int(i > 1)], recv.at[chunk, piece, stage, int(i > 1)], to).start()

    def took(buffer, sem):
        pltpu.make_async_copy(buffer, buffer, sem).wait()

    def step(chunk, k):
        stage = k // 2
        for piece in range(3):
            if k % 2:
                half = halves[(chunk * 3 + piece) * 2 + stage]
                took(half, recv.at[chunk, piece, stage, 0])
                axis = ORDERS[piece][2 - stage]
                for h, by in ((0, 1), (1, 3)):
                    mid = block(moved(at, axis, by), chunk, piece, stage)
                    add_into(half_of(mid, stage, piece, RCHUNKS[chunk][1], h), half.at[h])
                    start(chunk, piece, stage, 4 + h)
            else:
                if k > 0:
                    region = regions[slot(chunk, piece, stage - 1)]
                    took(region, recv.at[chunk, piece, stage - 1, 1])
                    add_into(block(at, chunk, piece, stage - 1), *[region.at[i] for i in range(region.shape[0])])
                    if stage < 3:
                        took(halves[(chunk * 3 + piece) * 2 + stage - 1], send.at[chunk, piece, 0])
                    took(region, send.at[chunk, piece, 1])
                if k < 6:
                    for i in range(3 if stage == 2 else 4):
                        start(chunk, piece, stage, i)

    def steps_after(table, index):
        for i, todo in table.items():
            @pl.when(index == i)
            def _(todo=todo):
                for chunk, k in todo:
                    step(chunk, k)

    def gradients(left, right, zh, col):
        for q in range(4):
            value = dot(left[q * 384:(q + 1) * 384, :], right, 1, 1).astype(BF16)
            part[zh, q, :, :, :, :, pl.ds(col, right.shape[0])] = value.reshape(4, 2, 3, 16, right.shape[0])

    def strip(q):
        return pl.ds(pl.multiple_of(q * 384, 128), 384)

    def fold(v):
        return v[:, 0:128] + v[:, 128:256] + v[:, 256:384] + v[:, 384:512]

    def row_sums(v):
        ones = jnp.ones((8, 128), BF16)
        a, b, _ = split(v)
        return (dot(ones, a, 1, 1) + dot(ones, b, 1, 1))[0:1]

    for ref in (dcbt, cross, dcum, ddt1, gskip, ggain):
        ref[...] = jnp.zeros_like(ref)
    first[1].wait()
    entered()
    step(0, 0)
    swap_sums = remote(sums, sums_in, swap_send.at[3], swap_recv.at[3], mate)
    swap_sums.start()
    for c in first[2:]:
        c.wait()
    swap_sums.wait()
    r_out = lax.rsqrt(sums[0:1, :] / INNER + EPS)
    k2 = r_out * r_out * r_out * (sums[1:2, :] + sums_in[1:2, :]) / INNER

    @pl.loop(0, 6)
    def _(m):
        zh, c, off, _ = group_at(m)
        cols = group_cols(prm, zh, c)
        for i in range(GROUP):
            r = slice(i * HEAD, (i + 1) * HEAD)
            rows = pl.ds(pl.multiple_of(off + i * HEAD, HEAD), HEAD)
            z = zt[rows, :].astype(F32)
            dg = dgt[rows, :].astype(F32)
            v = vt[rows, :].astype(F32)
            sz = sig(z)
            zs = z * sz
            dv = dg * cols[r, 5:6] * r_out - v * k2
            folds[0, r, :] = fold(dg * v * r_out)
            dyt[rows, :] = (dv * zs).astype(BF16)
            dzt[rows, :] = (dv * yt[rows, :] * (sz + zs * (1.0 - sz))).astype(BF16)
        prow[zh * 3 + c, 5:6, :] = row_sums(folds[0])
        gradients(xt, dzt[pl.ds(off, WIDE), :], zh, pl.multiple_of(768 + c * WIDE, WIDE))

    first[0].wait()
    step(0, 1)
    step(1, 0)
    loads[8].start()
    for c in second:
        c.wait()

    @pl.loop(0, 6)
    def _(m):
        zh, c, off, base = group_at(m)
        cc = pltpu.roll(cumc[...], 128 - base, 1)
        skips = group_skip(prm, zh, c)
        for i in range(GROUP):
            r = slice(i * HEAD, (i + 1) * HEAD)
            rows = pl.ds(pl.multiple_of(off + i * HEAD, HEAD), HEAD)
            skip = skips[i:i + 1, 0:1]
            xs = xst[rows, :].astype(F32)
            dyb = dyt[rows, :]
            dy = dyb.astype(F32)
            yssm = yt[rows, :] - skip * xs
            gskip[pl.ds(base + i, 1), :] = jnp.sum(dy * xs, axis=0, keepdims=True)
            dt = dtt[pl.ds(base + i, 1), :]
            cum = cumt[pl.ds(base + i, 1), :]
            xdt = xs * dt
            xdtb = xdt.astype(BF16)
            dxs = []
            for b in range(2):
                s = slice(b * SPAN, (b + 1) * SPAN)
                w = decay(cum, cc[s, i:i + 1], b)
                dxs.append(dot(dyb[:, s], (w * cbt[b]).astype(BF16), 1, 1))
                dcbt[b] += dot(xdtb[:, s], dyb[:, s], 0, 0) * w
            tail = jnp.exp(cum[:, SPAN - 1:SPAN] - cum[:, :SPAN])
            xe = (xdt[:, :SPAN] * tail).astype(BF16)
            dye = (dy[:, SPAN:] * jnp.exp(cum[:, SPAN:])).astype(BF16)
            ds = dot(dye, bc[SPAN:, 128:256]).astype(BF16)
            xe_all[r, :] = xe
            dye_all[r, :] = dye
            st_all[r, :] = dot(xe, bc[0:SPAN, 0:128]).astype(BF16)
            ds_all[r, :] = ds
            dxs[0] = dxs[0] + tail * dot(ds, bc[0:SPAN, 0:128], 1, 1)
            dx = jnp.concatenate(dxs, axis=1)
            dcum[pl.ds(base + i, 1), :] = jnp.sum(dy * yssm - xdtb.astype(F32) * dx, axis=0, keepdims=True)
            ddt1[pl.ds(base + i, 1), :] = jnp.sum(xs * dx, axis=0, keepdims=True)
            dyt[rows, :] = (dt * dx + skip * dy).astype(BF16)
            if i % 2:
                steps_after(SCAN_STEPS, m * 2 + i // 2)
        cross[1] += dot(st_all[...], dye_all[...], 0, 0)
        cross[0] += dot(ds_all[...], xe_all[...], 0, 0)

    upper = tri(SPAN, lambda r, c: r <= c).astype(F32)
    for b in range(2):
        s = slice(b * SPAN, (b + 1) * SPAN)
        d = (dcbt[b] * upper).astype(BF16)
        db = dot(bct[128:256, s], d, 1, 1)
        dc = dot(bct[0:128, s], d)
        dbct[0:128, s] = (db + cross[0] if b == 0 else db).astype(BF16)
        dbct[128:256, s] = (dc + cross[1] if b == 1 else dc).astype(BF16)
    swap_bc = remote(dbct, dbct_in, swap_send.at[1], swap_recv.at[1], mate)
    swap_bc.start()
    loads[6].start()

    dla = exact_dot(dcum[...], tri(T, lambda r, c: r >= c))
    for zh in range(2):
        rows = slice(zh * 16, (zh + 1) * 16)
        hc = prm[zh, :, 0:128].T
        rate = -jnp.exp(hc[:16, 7:8])
        d = dla[rows]
        dstep = (ddt1[rows, :] + rate * d) * sig(stept[rows, :].astype(F32) + hc[:16, 6:7])
        gd = jnp.sum(d * dtt[rows, :] * rate, axis=1, keepdims=True)
        hcol = jnp.concatenate([jnp.sum(dstep, axis=1, keepdims=True), gd, jnp.sum(gskip[rows, :], axis=1, keepdims=True),
                                jnp.zeros((16, 125), F32)], axis=1)
        hrow[:, zh * 128:(zh + 1) * 128] = jnp.concatenate([hcol, jnp.zeros((112, 128), F32)], axis=0).T[:8]
        keep = lax.broadcasted_iota(jnp.int32, (16, T), 0) < 12
        dstep_t[zh, 0:16, :] = jnp.where(keep, dstep, 0.0).astype(BF16)
        dstep_t[zh, 16:128, :] = jnp.zeros((112, T), BF16)


    swap_bc.wait_recv()
    for q in range(4):
        r = slice(q * 64, (q + 1) * 64)
        cols = spar[r]
        p, shifted = conv(statet[r, :].astype(F32), cols)
        sp = sig(p)
        dp = (dbct[r, :].astype(F32) + dbct_in[r, :].astype(F32)) * (sp + p * sp * (1.0 - sp))
        dstate[r, :] = conv_back(dp, cols).astype(BF16)
        dst[r, :] = jnp.concatenate([jnp.sum(dp * shifted[k], axis=1, keepdims=True) for k in range(4)]
                                    + [jnp.sum(dp, axis=1, keepdims=True), jnp.zeros((64, 123), F32)], axis=1)
    small[48:56, :] = dst[...].T[:8].astype(BF16)
    for zh in range(2):
        ld[0:64, :] = dstate[pl.ds(zh * 128 + pl.multiple_of(at["core"] * 64, 64), 64), :]
        ld[64:128, :] = dstep_t[zh, 0:64, :]
        gradients(xt, ld[...], zh, STATE_COL)

    step(4, 0)
    loads[6].wait()
    loads[8].wait()

    @pl.loop(0, 6)
    def _(m):
        zh, c, off, _ = group_at(m)
        cols = group_cols(prm, zh, c)
        for i in range(GROUP):
            r = slice(i * HEAD, (i + 1) * HEAD)
            rows = pl.ds(pl.multiple_of(off + i * HEAD, HEAD), HEAD)
            u = ut[rows, :].astype(F32)
            dp = dyt[rows, :].astype(F32) * dsil[rows, :].astype(F32)
            du = cols[r, 0:1] * dp
            folds[0, r, :] = fold(u * dp)
            folds[4, r, :] = fold(dp)
            for k in range(1, 4):
                ahead = sooner(dp, k)
                du = du + cols[r, k:k + 1] * ahead
                folds[k, r, :] = fold(u * ahead)
            dut[rows, :] = du.astype(BF16)
        for k in range(5):
            prow[zh * 3 + c, k:k + 1, :] = row_sums(folds[k])
        gradients(xt, dut[pl.ds(off, WIDE), :], zh, pl.multiple_of(INNER_COL + c * WIDE, 128))
        steps_after(CONV_STEPS, m)

    for q in range(6):
        small[q * 8:(q + 1) * 8, :] = prow[q].astype(BF16)
    small[56:64, :] = hrow[...].astype(BF16)

    def small_flights(s):
        slot_here = small_in.at[s, at["xyz"[s]]]
        return [remote(slot_here, slot_here, small_send.at[s, by - 1], small_recv.at[s, by - 1], moved(at, "xyz"[s], by)) for by in (1, 2, 3)]

    def small_start(s):
        small_in[s, at["xyz"[s]]] = small[...]
        for c in small_flights(s):
            c.start()

    def small_end(s):
        for c in small_flights(s):
            c.wait()
        total4 = small_in[s, 0].astype(F32) + small_in[s, 1].astype(F32) + small_in[s, 2].astype(F32) + small_in[s, 3].astype(F32)
        small[...] = total4.astype(BF16)
        if s == 2:
            gsmall[0:64, :] = total4

    small_start(0)
    step(3, 0)


    @pl.loop(0, 4)
    def _(q):
        more = [dot(wst[zh, q, :, :, :, :, pl.ds(128, 128)].reshape(384, 128), dstep_t[zh]) for zh in range(2)]
        both[...] = product(2 * q, dzt) + product(1 + 2 * q, dut) + (more[0] + more[1]).T
        total[:, strip(q)] = both[mine, :]
        branch[theirs, strip(q)] = both[theirs, :].astype(BF16)
        steps_after(TOKEN_STEPS, q)

    swap_dn = remote(branch.at[theirs], dn_in, swap_send.at[2], swap_recv.at[2], mate)
    swap_dn.start()
    own_state[...] = dstate[:, mine].T
    step(2, 2)
    small_end(0)
    small_start(1)
    swap_dn.wait()

    @pl.loop(0, 2)
    def _(q):
        r = pl.ds(pl.multiple_of(q * 128, 128), 128)
        full = total[r, :] + dn_in[r, :].astype(F32)
        for zh in range(2):
            full = full + dot(own_state[r, zh * 128:(zh + 1) * 128], wst[zh, :, :, :, :, :, pl.ds(0, 128)].reshape(1536, 128), 1, 1)
        h = hidden[r, :].astype(F32)
        r_in = lax.rsqrt(jnp.mean(h * h, axis=1, keepdims=True) + EPS)
        ggain[...] += jnp.sum(full * h * r_in, axis=0, keepdims=True)
        scaled = full * gain[...].reshape(1, 1536)
        back = scaled * r_in - h * (r_in * r_in * r_in * (jnp.sum(scaled * h, axis=1, keepdims=True) / 1536))
        grad_hidden[r, :] = (cot[r, :].astype(F32) + back).astype(BF16)

    def gain_peers(s):
        if s == 0:
            return [moved(at, "x", by) for by in (1, 2, 3)] + [mate] + [moved(mate, "x", by) for by in (1, 2, 3)]
        return [moved(moved(at, "y", a), "z", b) for a in range(4) for b in range(4) if a or b]

    def gain_slot(s):
        return at["x"] * 2 + at["core"] if s == 0 else at["y"] * 4 + at["z"]

    def gain_flights(s):
        here = gain_in.at[s, gain_slot(s)]
        return [remote(here, here, gain_send.at[s, i], gain_recv.at[s, i], to) for i, to in enumerate(gain_peers(s))]

    def gain_start(s, rows):
        gain_in[s, gain_slot(s)] = rows
        for c in gain_flights(s):
            c.start()

    def gain_end(s):
        for c in gain_flights(s):
            c.wait()
        rows = gain_in[s, 0]
        for i in range(1, 8 if s == 0 else 16):
            rows = rows + gain_in[s, i]
        return rows

    gain_start(0, jnp.concatenate([ggain[:, q * 256:(q + 1) * 256] for q in range(6)] + [jnp.zeros((2, 256), F32)], axis=0))
    put(4, grad_hidden)
    step(3, 2)
    step(4, 2)
    step(1, 4)

    def output(first_strip):
        @pl.loop(first_strip, first_strip + 2)
        def _(q):
            branch[:, strip(q)] = product(8 + q, gat).astype(BF16)

    output(0)
    step(2, 3)
    step(3, 3)
    step(4, 3)
    gain_start(1, gain_end(0))
    small_end(1)
    small_start(2)
    output(2)
    swap_br = remote(branch.at[theirs], br_in, swap_send.at[0], swap_recv.at[0], mate)
    swap_br.start()
    step(2, 4)
    step(3, 4)
    step(4, 4)
    step(1, 6)
    step(0, 6)
    step(4, 6)
    own = units(at, "")
    for piece in range(3):
        quarter[piece * 16:(piece + 1) * 16, :] = part[own + (piece, slice(None), pl.ds(STATE_COL, 128))].astype(F32)
    thirds = [remote(quarter, quarters.at[i], q_send.at[i], q_recv.at[i], to) for i, to in enumerate((mate, far, far_mate))]
    for c in thirds:
        c.start()
    step(2, 6)
    step(3, 6)
    for piece in range(3):
        out[piece * 16:(piece + 1) * 16, :] = part[own + (piece, slice(None), pl.ds(0, 2304))]
    put(0, out)
    swap_br.wait()

    @pl.loop(0, 2)
    def _(q):
        r = pl.ds(pl.multiple_of(q * 128, 128), 128)
        own_rows = pl.ds(pl.multiple_of(at["core"] * 256 + q * 128, 128), 128)
        branch[own_rows, :] = (hidden[r, :].astype(F32) + branch[own_rows, :].astype(F32) + br_in[r, :].astype(F32)).astype(BF16)

    put(3, branch.at[mine])
    small_end(2)
    gsmall[64:72, :] = gain_end(1)
    put(2, gsmall)
    for c in thirds:
        c.wait()
    low = at["core"] == 0
    q0, q1, q2, q3 = quarter[...], quarters[0], quarters[1], quarters[2]
    here = jnp.where(low, jnp.concatenate([q0[:, :64], q1[:, :64]], axis=1), jnp.concatenate([q1[:, :64], q0[:, :64]], axis=1))
    there = jnp.where(low, jnp.concatenate([q2[:, :64], q3[:, :64]], axis=1), jnp.concatenate([q3[:, :64], q2[:, :64]], axis=1))
    first = at["z"] < 2
    gstate[:, 0:128] = jnp.where(first, here, there)
    gstate[:, 128:256] = jnp.where(first, there, here)
    gstate[:, 256:384] = q0
    put(1, gstate)
    swap_bc.wait_send()
    for c in out_copies:
        c.wait()


def backward(tall, small, hidden, cot, gain):
    n = len(RCHUNKS)
    results = [sds((48, 2304), BF16), sds((48, 384)), sds((SUMS + 8, 256)), sds((256, 1536), BF16), sds((256, 1536), BF16)]
    any_ = pl.BlockSpec(memory_space=pl.ANY)
    shapes = [(stage, piece, RCHUNKS[chunk][1]) for chunk in range(n) for piece in range(3) for stage in range(3)]
    regions = [pltpu.VMEM((3 if s[0] == 2 else 2,) + region_shape(*s), BF16) for s in shapes]
    halves = [pltpu.VMEM((2,) + half_shape(*s), BF16) for s in shapes if s[0] < 2]
    dma = pltpu.SemaphoreType.DMA
    v = lambda shape, dtype=F32: pltpu.VMEM(shape, dtype)
    return pl.pallas_call(
        backward_kernel,
        in_specs=[any_] * (len(tall) + len(small) + 3),
        out_specs=[any_] * 5,
        out_shape=results,
        scratch_shapes=[v((2, 4, 4, 2, 3, 16, RCOLS), BF16)] + regions + halves + [
            v((1536, T), BF16)] * 6 + [v((1536, T)), v((3, 2, 4, 2, 3, 16, 768), BF16), v((2, 4, 4, 2, 3, 16, 256), BF16),
            v((256, 1536)), v((T, 384)), v((2, SPAN, SPAN)), v((128, T), BF16), v((WIDE, SPAN), BF16), v((WIDE, SPAN), BF16),
            v((WIDE, 128), BF16), v((WIDE, 128), BF16), v((2, 128, SPAN)), v((6, 8, WIDE)), v((8, 256)),
            v((32, T)), v((32, T)), v((32, T)), v((2, 128, T), BF16), v((256, T), BF16), v((256, T), BF16),
            v((256, 1536), BF16), v((T, 1536), BF16), v((256, 1536), BF16),
            v((256, T), BF16), v((256, 128)), v((5, WIDE, 128))] + [v(a.shape, a.dtype) for a in (*small, hidden, cot, gain, *results[:3], results[4])] + [ v((SUMS, 256), BF16), v((3, 4, SUMS, 256), BF16), v((256, 256), BF16), v((1, 1536)), v((2, 16, 8, 256)), v((48, 128)), v((3, 48, 128)), v((8, T)),
            dma((n, 3, 2)), dma((n, 3, 3, 2)), dma((25,)), dma((3,)), dma((4,)), dma((4,)), dma((3, 3)), dma((3, 3)), dma((2, 15)), dma((2, 15)), dma((3,)), dma((3,)), dma((5,))],
        compiler_params=pltpu.CompilerParams(collective_id=1, has_side_effects=True, vmem_limit_bytes=65400 << 10),
    )(*tall, *small, hidden, cot, gain)


def finish_kernel(out, gstate, small, new_h, grad_h, new_hidden, grad_hidden, in_gain, main, step, state, inner, inner_bias, cstate, cstate_bias,
                  bias, log, skip, out_gain, proj_out):
    new_hidden[...] = new_h[...]
    grad_hidden[...] = grad_h[...]
    z_hi = lax.axis_index("tensor") // 2
    proj_out[...] = out[:, 0:768].astype(F32)
    main[:, 0, :] = out[:, 768:1536].astype(F32)
    main[:, 1, :] = out[:, 1536:2304].astype(F32)
    step[...] = gstate[:, 256:384].T[64:76]
    state[...] = gstate[:, 0:256]
    for c in range(3):
        rows = small[pl.ds(pl.multiple_of(z_hi * 24 + c * 8, 8), 8), :]
        cols = slice(c * 256, (c + 1) * 256)
        inner[:, cols] = rows[0:4]
        inner_bias[cols] = rows[4:5].reshape(256)
        out_gain[cols] = rows[5:6].reshape(256)
    cstate[...] = small[48:52, :]
    cstate_bias[...] = small[52:53, :].reshape(256)
    for q in range(6):
        in_gain[q * 256:(q + 1) * 256] = small[64 + q:65 + q, :].reshape(256)
    heads = small[56:64, pl.ds(pl.multiple_of(z_hi * 128, 128), 128)]
    for i, ref in enumerate((bias, log, skip)):
        ref[...] = heads[i:i + 1, 0:12].reshape(12)


def finish(out, gstate, small, new_hidden, grad_hidden):
    vm = pl.BlockSpec(memory_space=pltpu.VMEM)
    shapes = [sds(s) for s in ((1536,), (48, 2, 768), (12, 48), (48, 256), (4, 768), (768,), (4, 256), (256,), (12,), (12,), (12,), (768,), (48, 768))]
    return pl.pallas_call(
        finish_kernel, out_shape=[sds((256, 1536), BF16)] * 2 + shapes, in_specs=[vm] * 5, out_specs=[vm] * 15,
    )(out, gstate, small, new_hidden, grad_hidden)


def per_device(hidden, in_gain, proj_main, proj_step, proj_state, conv_inner, conv_inner_bias, conv_state, conv_state_bias,
               step_bias, decay_log, skip_gain, out_gain, proj_out, grad_out):
    outs = forward(proj_main.reshape(48, 1536), proj_step.T, proj_state, proj_out, hidden, grad_out, conv_inner, conv_state,
                   conv_inner_bias, out_gain, conv_state_bias, in_gain, step_bias, decay_log, skip_gain)
    results = backward(outs[:12], outs[12:], hidden, grad_out, in_gain)
    new_hidden, grad_hidden, ggain, main, step, *others = finish(*results)
    return (new_hidden, grad_hidden, ggain, main, step.T, *others)


def solution(mesh):
    rows = P(("dp", "tensor"), None)
    per_head = P("tensor")
    in_specs = (rows, P(), P("dp", None, "tensor"), P("dp", "tensor"), P("dp", None), P(None, "tensor"), per_head, P(), P(),
                per_head, per_head, per_head, per_head, P("dp", "tensor"), rows)
    out_specs = (rows, rows, P(), P("dp", None, "tensor"), P("dp", "tensor"), P("dp", None), P(None, "tensor"), per_head, P(), P(),
                 per_head, per_head, per_head, per_head, P("dp", "tensor"))
    return jax.shard_map(per_device, mesh=mesh, in_specs=in_specs, out_specs=out_specs, check_vma=False)
```
